32 devices in a mesh: dp: 8 (over z, y), tensor: 4 (over x, core).
Axes of the slice: x: 2, y: 2, z: 4, core: 2. Of those that a mesh axis runs over, the one named last changes fastest.
Arguments:
- tokens: bfloat16 [8192, 1536], P(('dp', 'tensor')), may hold values from -6 to 6
- gain_attn: float32 [1536], replicated, may hold values from 0.25 to 1.75
- query_weight: bfloat16 [1536, 1536], P(None, 'tensor'), may hold values from -0.21875 to 0.21875
- key_weight: bfloat16 [1536, 512], P(None, 'tensor'), may hold values from -0.15625 to 0.15625
- value_weight: bfloat16 [1536, 512], P(None, 'tensor'), may hold values from -0.15625 to 0.15625
- w_output: bfloat16 [1536, 1536], P('tensor'), may hold values from -0.875 to 0.875
- gain_ffn: float32 [1536], replicated, may hold values from 0.25 to 1.75
- w_router: bfloat16 [1536, 16], replicated, may hold values from -0.078125 to 0.078125
- w_gate: bfloat16 [16, 1536, 512], P('dp'), may hold values from -0.15625 to 0.15625
- w_up: bfloat16 [16, 1536, 512], P('dp'), may hold values from -0.15625 to 0.15625
- w_down: bfloat16 [16, 512, 1536], P('dp'), may hold values from -0.75 to 0.75
- segments: int32 [8, 1024], P('dp'), may hold values from 0 to 3, never falling along the last dimension, each value on 1 to 512 neighbouring positions
- routes: int32 [8192, 8], P(('dp', 'tensor')), may hold values from 0 to 15, all different within a row; in each aligned block of 256 rows (0 to 255, 256 to 511, ...) at most 160 rows name the same one
- cotangent: bfloat16 [8192, 1536], P(('dp', 'tensor')), may hold values from -6 to 6
Outputs:
- mixed: bfloat16 [8192, 1536], P(('dp', 'tensor'))
- grad_tokens: bfloat16 [8192, 1536], P(('dp', 'tensor'))
- grad_gain_attn: float32 [1536], replicated
- grad_query: float32 [1536, 1536], P(None, 'tensor')
- grad_key: float32 [1536, 512], P(None, 'tensor')
- grad_value: float32 [1536, 512], P(None, 'tensor')
- grad_output: float32 [1536, 1536], P('tensor')
- grad_gain_ffn: float32 [1536], replicated
- grad_router: float32 [1536, 16], replicated
- grad_gate: float32 [16, 1536, 512], P('dp')
- grad_up: float32 [16, 1536, 512], P('dp')
- grad_down: float32 [16, 512, 1536], P('dp')
The draws below stay inside these ranges and needn't reach their ends.
Inputs may be any that keep to these rules, and one draw needn't show every extreme that they name: `routes`: each token names 8 different experts; of the tokens of one device no more than 160 name one expert, and in every draw some device's tokens name some expert exactly 160 times. `segments`: never falling along a sequence; each document covers 1 to 512 positions of its sequence, and some covers exactly 512.
All inputs are finite; a program needn't handle non-finite values.
Results may differ from the reference program's by a relative error of at most 0.024.
Values may be sent and summed in bfloat16 or wider, within the bound.
No kernel may reach another device: no remote copies, remote signals or barrier semaphores. Data moves between devices by JAX's collectives and lax.ppermute only.
A program may use at most 256 MiB of HBM per device.

```python
import math
import jax
import jax.numpy as jnp
import numpy as np
from jax import lax

MODEL_WIDTH = 1536
QUERY_HEADS = 24
KEY_VALUE_HEADS = 8
HEAD_WIDTH = 64
FF = 512
TOPK = 8
SEQUENCE_LENGTH = 1024
EXPERTS = 16
ROWS_DEV = 256
SEQUENCE_COUNT = 8
TOKENS = 8192
CAP = 160


def steps_of(own_key, extent, cuts, low, largest):
    level = 1.0
    for dim, shards_of in cuts:
        draws = jax.random.uniform(jax.random.fold_in(jax.random.fold_in(own_key, 6), dim), (shards_of,), jnp.float32, low / len(cuts), largest / len(cuts))
        level = level * jnp.repeat(jnp.exp(draws), extent[dim] // shards_of).reshape((-1,) + (1,) * (len(extent) - 1 - dim))
    return level


def split_up(amount, total, reach, slope):
    portions = [(1 << 20) // math.isqrt(grade ** slope) + 1 for grade in range(2, amount + 1)]
    rest, holding = total - reach - (amount - 1), [1] * (amount - 1)
    while rest > 0:
        movable = [i for i in range(amount - 1) if holding[i] < reach]
        mass, remaining = sum([portions[i] for i in movable]), rest
        for i in movable:
            extra = min(reach - holding[i], max(1, remaining * portions[i] // mass), rest)
            holding[i] = holding[i] + extra
            rest = rest - extra
    return np.array([reach] + holding)


def ragged(rng, count, total, most, lean):
    if count == 2:
        one = jax.random.randint(rng, (), max(1, total - most), min(most, total - 1) + 1)
        return jnp.stack([one, total - one])
    tallies = jnp.asarray(split_up(count, total, most, lean), jnp.int32)
    pairs = (count - 1) // 2
    donor, sink = tallies[1:1 + 2 * pairs:2], tallies[2:2 + 2 * pairs:2]
    margin = jnp.minimum(donor - 1, most - sink)
    moved = jax.random.randint(jax.random.fold_in(rng, 1), (pairs,), 0, 1 << 20) % (margin + 1)
    tallies = tallies.at[1:1 + 2 * pairs:2].set(donor - moved).at[2:2 + 2 * pairs:2].set(sink + moved)
    return tallies[jax.random.permutation(jax.random.fold_in(rng, 2), count)]


def routed_block(own_key, own, number, rows, amount, top, reach, lean):
    order = jax.random.permutation(own_key, amount)
    packed, common = shares(amount, rows * top, reach, lean, True), shares(amount, rows * top, reach, lean, False)
    places = jnp.arange(amount)

    def named(tallies, offset_by):
        used = int((tallies > 0).sum())
        fixed = max(1, used // 4)
        shifted = fixed + (places - fixed + offset_by * (used - fixed)) % max(1, amount - fixed)
        return jnp.zeros((amount,), jnp.int32).at[order[jnp.where(places < fixed, places, shifted)]].set(jnp.asarray(tallies, jnp.int32))

    tallies = jnp.where(number % 4 == 0, named(packed, number // 4), named(common, number - number // 4 - 1))
    mixed = jax.random.permutation(jax.random.fold_in(own, 3), amount)
    giver, sink = mixed[0:amount // 2 * 2:2], mixed[1:amount // 2 * 2:2]
    margin = jnp.minimum(tallies[giver] - 1, reach - tallies[sink]) // 2
    margin = jnp.where((giver == order[0]) | (sink == order[0]) | (tallies[sink] == 0), 0, jnp.maximum(margin, 0))
    shifted = jax.random.randint(jax.random.fold_in(own, 4), (amount // 2,), 0, 1 << 20) % (margin + 1)
    tallies = tallies.at[giver].add(-shifted).at[sink].add(shifted)
    items = jnp.searchsorted(jnp.cumsum(tallies), jnp.arange(rows * top), side="right").astype(jnp.int32)
    listing = items.reshape(top, rows).T
    listing = listing[jax.random.permutation(jax.random.fold_in(own, 1), rows)]
    offset_by = jax.random.randint(jax.random.fold_in(own, 2), (rows, 1), 0, top)
    return jnp.take_along_axis(listing, (jnp.arange(top)[None, :] + offset_by) % top, axis=1)


def shares(count, total, bound, skew, full):
    loads = [(1 << 20) // math.isqrt(standing ** skew) + 1 for standing in range(1, count + 1)]
    largest = bound if full else min(bound, max(-(-total // count), total * loads[0] // sum(loads)))
    least = 1 if total - largest >= count - 1 else 0
    given, spare = [largest] + [least] * (count - 1), total - largest - least * (count - 1)
    while spare > 0:
        movable = [i for i in range(1, count) if given[i] < largest] or [i for i in range(1, count) if given[i] < bound]
        pool, budget = sum([loads[i] for i in movable]), spare
        for i in movable:
            addition = min(bound - given[i], max(1, budget * loads[i] // pool), spare)
            given[i] = given[i] + addition
            spare = spare - addition
    return np.array(given)


def bell_draw(own_key, shape, scale, reach, shards=(), kind=jnp.bfloat16):
    entries = scale * jax.random.normal(own_key, shape, jnp.float32)
    if shards:
        entries = entries * steps_of(own_key, shape, shards, -0.22, 0.18)
    return jnp.clip(entries, -reach, reach).astype(kind)


def setup_inputs(seed: int = 0) -> dict:
    splits = jax.random.split(jax.random.key(seed), 15)
    tokens = bell_draw(splits[0], (TOKENS, MODEL_WIDTH), 1.0, 6.0, ((0, 32),))
    gain_attn = jnp.clip(1.0 + 0.15 * jax.random.normal(splits[1], (MODEL_WIDTH,), jnp.float32), 0.25, 1.75)
    query_weight = bell_draw(splits[2], (MODEL_WIDTH, QUERY_HEADS * HEAD_WIDTH), (MODEL_WIDTH // 2) ** -0.5, 0.21875, ((1, 4),))
    key_weight = bell_draw(splits[3], (MODEL_WIDTH, KEY_VALUE_HEADS * HEAD_WIDTH), MODEL_WIDTH ** -0.5, 0.15625, ((1, 4),))
    value_weight = bell_draw(splits[4], (MODEL_WIDTH, KEY_VALUE_HEADS * HEAD_WIDTH), MODEL_WIDTH ** -0.5, 0.15625, ((1, 4),))
    w_output = bell_draw(splits[5], (QUERY_HEADS * HEAD_WIDTH, MODEL_WIDTH), (QUERY_HEADS * HEAD_WIDTH // 32) ** -0.5, 0.875, ((0, 4),))
    gain_ffn = jnp.clip(1.0 + 0.15 * jax.random.normal(splits[6], (MODEL_WIDTH,), jnp.float32), 0.25, 1.75)
    w_router = bell_draw(splits[7], (MODEL_WIDTH, EXPERTS), (4 * MODEL_WIDTH) ** -0.5, 0.078125)
    w_gate = bell_draw(splits[8], (EXPERTS, MODEL_WIDTH, FF), MODEL_WIDTH ** -0.5, 0.15625, ((0, 8),))
    w_up = bell_draw(splits[9], (EXPERTS, MODEL_WIDTH, FF), MODEL_WIDTH ** -0.5, 0.15625, ((0, 8),))
    w_down = bell_draw(splits[10], (EXPERTS, FF, MODEL_WIDTH), (FF // 8) ** -0.5, 0.75, ((0, 8),))
    segments = jax.vmap(lambda own: jnp.searchsorted(jnp.cumsum(ragged(own, 4, SEQUENCE_LENGTH, SEQUENCE_LENGTH // 2, 1)), jnp.arange(SEQUENCE_LENGTH), side="right"))(jax.random.split(splits[11], SEQUENCE_COUNT)).reshape((SEQUENCE_COUNT, SEQUENCE_LENGTH)).astype(jnp.int32)
    routes_keys = jax.random.split(jax.random.fold_in(splits[12], 1), TOKENS // ROWS_DEV)
    routes_turns = jax.random.permutation(jax.random.fold_in(splits[12], 3), TOKENS // ROWS_DEV)
    routes = jax.vmap(lambda own, number: routed_block(jax.random.fold_in(splits[12], 2), own, number, ROWS_DEV, EXPERTS, TOPK, CAP, 1))(routes_keys, routes_turns).reshape((TOKENS, TOPK))
    cotangent = bell_draw(splits[13], (TOKENS, MODEL_WIDTH), 1.0, 6.0, ((0, 32),))
    return dict(tokens=tokens, gain_attn=gain_attn, query_weight=query_weight, key_weight=key_weight, value_weight=value_weight, w_output=w_output, gain_ffn=gain_ffn, w_router=w_router, w_gate=w_gate, w_up=w_up, w_down=w_down, segments=segments, routes=routes, cotangent=cotangent)


EPS = 1e-06
ROPE_BASE = 10000.0
NEG = -1e+30

@jax.custom_vjp
def lowered_values(v):
    return lax.optimization_barrier(v.astype(jnp.bfloat16)).astype(jnp.float32)

@jax.custom_vjp
def lowered_gradient(v):
    return v

def low_keep(v):
    return (lowered_values(v), None)

def low_pass(kept, grad):
    return (grad,)

def back_keep(v):
    return (v, None)

def back_low(kept, grad):
    return (lowered_values(grad),)
lowered_values.defvjp(low_keep, low_pass)
lowered_gradient.defvjp(back_keep, back_low)

def matrix_product(left, right):
    return jnp.dot(left, right, precision=lax.Precision.HIGHEST)

def rms_norm(value_rows, gain_vec):
    return value_rows * lax.rsqrt(lax.optimization_barrier(jnp.mean(value_rows * value_rows, axis=-1, keepdims=True)) + EPS) * gain_vec

def rope_tables(length, head_size):
    half = head_size // 2
    freq = jnp.exp(-(jnp.arange(half, dtype=jnp.float32) * (2.0 / head_size)) * math.log(ROPE_BASE))
    angle = jnp.arange(length, dtype=jnp.float32)[:, None] * freq[None, :]
    return (jnp.cos(angle), jnp.sin(angle))

def rotate(value_rows, cos_tab, sin_tab):
    half = value_rows.shape[-1] // 2
    first = value_rows[..., :half]
    second = value_rows[..., half:]
    return jnp.concatenate([first * cos_tab - second * sin_tab, second * cos_tab + first * sin_tab], axis=-1)

def forward(inputs, gain_attn, query_weight, key_weight, value_weight, w_output, gain_ffn, w_router, w_gate, w_up, w_down, segments, position, chosen):
    highest = lax.Precision.HIGHEST
    query_group_width = QUERY_HEADS // KEY_VALUE_HEADS
    first_normed_input = lowered_values(rms_norm(inputs, gain_attn))
    query_projected = lowered_gradient(matrix_product(first_normed_input, query_weight)).reshape(SEQUENCE_COUNT, SEQUENCE_LENGTH, KEY_VALUE_HEADS, query_group_width, HEAD_WIDTH)
    key_projected = lowered_gradient(matrix_product(first_normed_input, key_weight)).reshape(SEQUENCE_COUNT, SEQUENCE_LENGTH, KEY_VALUE_HEADS, HEAD_WIDTH)
    value_rows = lowered_values(lowered_gradient(matrix_product(first_normed_input, value_weight))).reshape(SEQUENCE_COUNT, SEQUENCE_LENGTH, KEY_VALUE_HEADS, HEAD_WIDTH)
    cos_tab, sin_tab = rope_tables(SEQUENCE_LENGTH, HEAD_WIDTH)
    places = jnp.arange(SEQUENCE_LENGTH, dtype=jnp.int32)
    score_scale = HEAD_WIDTH ** (-0.5)

    def attend(pieces):
        query_seq, key_seq, value_seq, seg_seq = pieces
        queries = lowered_values(rotate(query_seq, cos_tab[:, None, None, :], sin_tab[:, None, None, :]))
        keys = lowered_values(rotate(key_seq, cos_tab[:, None, :], sin_tab[:, None, :]))
        scores = lowered_gradient(jnp.einsum('qkgd,tkd->kgqt', queries, keys, precision=highest) * score_scale)
        allowed = (seg_seq[:, None] == seg_seq[None, :]) & (places[:, None] >= places[None, :])
        scores = jnp.where(allowed, scores, NEG)
        probs = lowered_values(jax.nn.softmax(scores, axis=-1))
        attended = jnp.einsum('kgqt,tkd->qkgd', probs, value_seq, precision=highest)
        return lowered_values(lowered_gradient(attended)).reshape(SEQUENCE_LENGTH, QUERY_HEADS * HEAD_WIDTH)
    attended = lax.map(jax.checkpoint(attend), (query_projected, key_projected, value_rows, segments)).reshape(TOKENS, QUERY_HEADS * HEAD_WIDTH)
    branch = lowered_gradient(matrix_product(attended, w_output))
    residual = inputs + branch
    normed_two = lowered_values(rms_norm(residual, gain_ffn))
    logits = lowered_gradient(matrix_product(normed_two, w_router))
    picked = lax.optimization_barrier(jnp.sum(chosen * logits[:, None, :], axis=2))
    gates = jax.nn.softmax(picked, axis=1)
    copies = lowered_gradient(jnp.broadcast_to(normed_two[:, None, :], (TOKENS, TOPK, MODEL_WIDTH))).reshape(TOKENS * TOPK, MODEL_WIDTH)
    block_count = TOKENS // ROWS_DEV
    buffer = jnp.zeros((EXPERTS * block_count * CAP, MODEL_WIDTH), jnp.float32).at[position].set(copies)
    buffer = buffer.reshape(EXPERTS, block_count * CAP, MODEL_WIDTH)

    def expert(pieces):
        rows_in, gate_w, up_w, down_w = pieces
        gate_pre = lowered_gradient(matrix_product(rows_in, gate_w))
        up_pre = lowered_gradient(matrix_product(rows_in, up_w))
        hidden = lowered_values(jax.nn.silu(gate_pre) * up_pre)
        return lowered_values(lowered_gradient(matrix_product(hidden, down_w)))
    outputs = lax.map(jax.checkpoint(expert), (buffer, w_gate, w_up, w_down)).reshape(EXPERTS * block_count * CAP, MODEL_WIDTH)
    returned = outputs[position].reshape(TOKENS, TOPK, MODEL_WIDTH)
    return residual + lax.optimization_barrier(jnp.sum(gates[:, :, None] * returned, axis=1))

def reference(tokens, gain_attn, query_weight, key_weight, value_weight, w_output, gain_ffn, w_router, w_gate, w_up, w_down, segments, routes, cotangent):
    chosen_int = (routes[:, :, None] == jnp.arange(EXPERTS, dtype=jnp.int32)[None, None, :]).astype(jnp.int32)
    per_row = lax.optimization_barrier(jnp.sum(chosen_int, axis=1))
    block_count = TOKENS // ROWS_DEV
    grouped = per_row.reshape(block_count, ROWS_DEV, EXPERTS)
    earlier = (jnp.cumsum(grouped, axis=1) - grouped).reshape(TOKENS, EXPERTS)
    slots = lax.optimization_barrier(jnp.sum(chosen_int * earlier[:, None, :], axis=2))
    block_of = (jnp.arange(TOKENS, dtype=jnp.int32) // ROWS_DEV)[:, None]
    position = ((routes * block_count + block_of) * CAP + slots).reshape(-1).astype(jnp.int32)
    chosen = chosen_int.astype(jnp.float32)

    def run(inputs, gain_one, query_w, key_w, value_w, output_w, gain_two, router_w, gate_w, up_w, down_w):
        return forward(inputs, gain_one, query_w, key_w, value_w, output_w, gain_two, router_w, gate_w, up_w, down_w, segments, position, chosen)
    mixed, pullback = jax.vjp(run, tokens.astype(jnp.float32), gain_attn.astype(jnp.float32), query_weight.astype(jnp.float32), key_weight.astype(jnp.float32), value_weight.astype(jnp.float32), w_output.astype(jnp.float32), gain_ffn.astype(jnp.float32), w_router.astype(jnp.float32), w_gate.astype(jnp.float32), w_up.astype(jnp.float32), w_down.astype(jnp.float32))
    grads = pullback(cotangent.astype(jnp.float32))
    return (mixed.astype(jnp.bfloat16), grads[0].astype(jnp.bfloat16), grads[1], grads[2], grads[3], grads[4], grads[5], grads[6], grads[7], grads[8], grads[9], grads[10])
```

```python
import functools
import math

import jax
import jax.numpy as jnp
import numpy as np
from jax import lax
from jax.experimental import pallas as pl
from jax.experimental.pallas import tpu as pltpu
from jax.sharding import PartitionSpec as P

HEAD_WIDTH = 64
EPS = 1e-06
ROPE_BASE = 10000.0
NEG = -1e30
LANES = 128
BLOCK = 256
REACH = 512
VMEM_BYTES = 52 * 1024 * 1024
low = jnp.bfloat16
wide = jnp.float32
NN = (((1,), (0,)), ((), ()))
NT = (((1,), (1,)), ((), ()))
TN = (((0,), (0,)), ((), ()))
dot = functools.partial(lax.dot_general, preferred_element_type=jnp.float32)
Shape = jax.ShapeDtypeStruct
ANY = pl.BlockSpec(memory_space=pl.ANY)
VMEM = pl.BlockSpec(memory_space=pltpu.VMEM)
SMEM = pl.BlockSpec(memory_space=pltpu.SMEM)


def rope_tables(length):
    half = HEAD_WIDTH // 2
    freq = np.exp(-(np.arange(half, dtype=np.float32) * (2.0 / HEAD_WIDTH)) * math.log(ROPE_BASE))
    angle = np.arange(length, dtype=np.float32)[:, None] * freq.astype(np.float32)[None, :]
    cos, sin = np.cos(angle), np.sin(angle)
    cos = np.concatenate([cos] * 4, axis=1).astype(np.float32)
    sin = np.concatenate([-sin, sin, -sin, sin], axis=1).astype(np.float32)
    return jnp.asarray(cos), jnp.asarray(sin)


def ring_order(count):
    return list(range(0, count, 2)) + list(range(count - 1, 0, -2))


def ring_send(array, step):
    count = lax.axis_size("dp")
    order = ring_order(count)
    return lax.ppermute(
        array, "dp", [(order[i], order[(i + step) % count]) for i in range(count)]
    )


def ring_places():
    count = lax.axis_size("dp")
    order = ring_order(count)
    place = jnp.asarray([order.index(i) for i in range(count)], jnp.int32)
    return (place[lax.axis_index("dp")] + jnp.arange(count, dtype=jnp.int32)) % count


def ring_gather(array, opposite=None):
    count = lax.axis_size("dp")
    half = array.shape[0] // 2
    below, above = [], []
    up, down = array, array
    for _ in range(count // 2 - 1):
        up = ring_send(up, 1)
        down = ring_send(down, -1)
        below.append(up)
        above.append(down)
    top = ring_send(up[:half], 1)
    bottom = ring_send(down[half:], -1)
    return below, above, (top, bottom)


def add_low(first, second):
    return (first.astype(wide) + second.astype(wide)).astype(low)


def ring_scatter(below, above, opposite):
    up_half, down_half = opposite
    half = up_half.shape[0]
    up = ring_send(up_half, 1)
    down = ring_send(down_half, -1)
    for k in range(len(above), 0, -1):
        part_up, part_down = above[k - 1], below[k - 1]
        if k == len(above):
            up = jnp.concatenate([add_low(up, part_up[:half]), part_up[half:]], axis=0)
            down = jnp.concatenate([part_down[:half], add_low(down, part_down[half:])], axis=0)
        else:
            up = add_low(up, part_up)
            down = add_low(down, part_down)
        up = ring_send(up, 1)
        down = ring_send(down, -1)
    return up, down


def swap(array, axis, mask):
    return lax.ppermute(array, axis, [(i, i ^ mask) for i in range(lax.axis_size(axis))])


def cube_sum(array, axes):
    for axis in axes:
        mask = 1
        while mask < lax.axis_size(axis):
            array = array + swap(array, axis, mask)
            mask *= 2
    return array


def tensor_blocks(array):
    far = swap(array, "tensor", 2)
    return array, swap(array, "tensor", 1), far, swap(far, "tensor", 1)


def call(body, operands, in_specs, out_specs, out_shape, scratch=(), grid=None, after=(), name=None, cost=None, alias=None):
    count = len(after)
    position = len(operands)

    def kernel(*refs):
        body(*refs[:position], *refs[position + count :])

    extra = {} if grid is None else {"grid": grid}
    if cost is not None:
        extra["cost_estimate"] = pl.CostEstimate(
            flops=int(cost[0]), bytes_accessed=int(cost[1]), transcendentals=0
        )
    if alias is not None:
        extra["input_output_aliases"] = alias
    return pl.pallas_call(
        kernel,
        in_specs=list(in_specs) + [ANY] * count,
        out_specs=out_specs,
        out_shape=out_shape,
        scratch_shapes=list(scratch),
        compiler_params=pltpu.CompilerParams(vmem_limit_bytes=VMEM_BYTES),
        name=name,
        **extra,
    )(*operands, *after)


def half_turn(array):
    width = array.shape[-1]
    half = HEAD_WIDTH // 2
    lane = lax.broadcasted_iota(jnp.int32, array.shape, 1)
    return jnp.where(
        lane % HEAD_WIDTH < half, pltpu.roll(array, width - half, 1), pltpu.roll(array, half, 1)
    )


def spread_heads(array):
    lane = lax.broadcasted_iota(jnp.int32, array.shape, 1)
    first = lane < HEAD_WIDTH
    other = pltpu.roll(array, HEAD_WIDTH, 1)
    zero = jnp.zeros_like(array)
    return [
        [jnp.where(first, array, zero), jnp.where(first, zero, other)],
        [jnp.where(first, other, zero), jnp.where(first, zero, array)],
    ]


def load_blocks(place, blocks, target, sems):
    rows = blocks[0].shape[0]
    copies = []
    for mask, block in enumerate(blocks):
        start = pl.multiple_of((place ^ mask) * rows, rows)
        copies.append(pltpu.make_async_copy(block, target.at[pl.ds(start, rows), :], sems.at[mask]))
    for copy in copies:
        copy.start()
    return copies


def wait_all(copies):
    for copy in copies:
        copy.wait()


def column_of(row_ref, start, size):
    row = jnp.broadcast_to(row_ref[:, start : start + size].astype(wide), (LANES, size))
    return jnp.transpose(row)[:, :1].astype(jnp.int32)


def attend_body(
    place_ref, own, near, far, both, wq_ref, wk_ref, wv_ref, cos_ref, sin_ref, row_ref,
    att_ref, q_ref, k_ref, v_ref, lse_ref, rows_s, kz_s, vz_s, sems,
):
    place = place_ref[0]
    wait_all(load_blocks(place, (own, near, far, both), rows_s, sems))
    length = rows_s.shape[0]
    pairs = wq_ref.shape[1] // LANES
    scale = HEAD_WIDTH**-0.5
    for start in range(0, length, BLOCK):
        at = pl.ds(start, BLOCK)
        rows = rows_s[at, :]
        cos, sin = cos_ref[at, :], sin_ref[at, :]
        query = dot(rows, wq_ref[...], NN)
        for j in range(pairs):
            part = query[:, j * LANES : (j + 1) * LANES]
            turned = (part * cos + half_turn(part) * sin).astype(low)
            q_ref[at, j * LANES : (j + 1) * LANES] = (turned.astype(wide) * scale).astype(low)
        key = dot(rows, wk_ref[...], NN)
        key = (key * cos + half_turn(key) * sin).astype(low)
        k_ref[at, :] = key
        value = dot(rows, wv_ref[...], NN).astype(low)
        v_ref[at, :] = value
        keys, values = spread_heads(key.astype(wide)), spread_heads(value.astype(wide))
        for g in range(2):
            for off in range(2):
                kz_s[2 * g + off, at, :] = keys[g][off].astype(low)
                vz_s[2 * g + off, at, :] = values[g][off].astype(low)
    lane = lax.broadcasted_iota(jnp.int32, (BLOCK, LANES), 1)
    for start in range(0, length, BLOCK):
        at = pl.ds(start, BLOCK)
        first = max(0, start - REACH)
        span = start + BLOCK - first
        keys_at = pl.ds(first, span)
        row_id = lax.broadcasted_iota(jnp.int32, (BLOCK, span), 0) + start
        col_id = lax.broadcasted_iota(jnp.int32, (BLOCK, span), 1) + first
        allowed = (column_of(row_ref, start, BLOCK) == row_ref[:, keys_at]) & (row_id >= col_id)
        bias = jnp.where(allowed, 0.0, NEG)
        stats = jnp.zeros((BLOCK, LANES), wide)
        for j in range(pairs):
            query = q_ref[at, j * LANES : (j + 1) * LANES]
            total = None
            for off in range(2):
                h = 2 * j + off
                slot = 2 * (h // pairs) + off
                scores = dot(query, kz_s[slot, keys_at, :], NT) + bias
                largest = jnp.max(scores, axis=1, keepdims=True)
                shifted = jnp.exp(scores - largest)
                summed = jnp.sum(shifted, axis=1, keepdims=True)
                probs = (shifted * (1.0 / summed)).astype(low)
                part = dot(probs, vz_s[slot, keys_at, :], NN)
                total = part if total is None else total + part
                stats = jnp.where(lane == h, largest + jnp.log(summed), stats)
            att_ref[at, j * LANES : (j + 1) * LANES] = total.astype(low)
        lse_ref[at, :] = stats


def attend(place, blocks, wq, wk, wv, cos, sin, segs, after):
    rows, width = blocks[0].shape
    length = 4 * rows
    return call(
        attend_body,
        (place, *blocks, wq, wk, wv, cos, sin, segs.reshape(1, length)),
        [SMEM] + [ANY] * 4 + [VMEM] * 6,
        [VMEM] * 5,
        [
            Shape((length, wq.shape[1]), low),
            Shape((length, wq.shape[1]), low),
            Shape((length, wk.shape[1]), low),
            Shape((length, wk.shape[1]), low),
            Shape((length, LANES), wide),
        ],
        [
            pltpu.VMEM((length, width), low),
            pltpu.VMEM((4, length, LANES), low),
            pltpu.VMEM((4, length, LANES), low),
            pltpu.SemaphoreType.DMA((4,)),
        ],
        after=after,
        name="attend",
        cost=(15e-6 * 1.1e15, 12e6),
    )


def branch_body(flip, place_ref, att_ref, wo_ref, out_ref):
    rows = out_ref.shape[1]
    core = place_ref[0] % 2
    core = 1 - core if flip else core
    for x in range(2):
        at = pl.ds(pl.multiple_of((2 * x + core) * rows, rows), rows)
        out_ref[x] = dot(att_ref[at, :], wo_ref[...], NN).astype(low)


def branch_half(place, att, wo, flip, after=()):
    rows, width = att.shape[0] // 4, wo.shape[1]
    return call(
        functools.partial(branch_body, flip),
        (place, att, wo),
        [SMEM] + [VMEM] * 2,
        VMEM,
        Shape((2, rows, width), low),
        after=after,
        name="branch",
        cost=(2e9, 4e6),
    )


def attend_back_body(
    place_ref, own, near, far, both, wo_ref, att_ref, q_ref, k_ref, v_ref, lse_ref, cos_ref, sin_ref, row_ref,
    d_lin_ref, rows_s, kz_s, kt_s, vz_s, d_att_s, d_key_s, d_value_s, d_query_s, sems,
):
    place = place_ref[0]
    wait_all(load_blocks(place, (own, near, far, both), rows_s, sems))
    length, q_width = att_ref.shape
    heads = q_width // HEAD_WIDTH
    pairs = heads // 2
    scale = HEAD_WIDTH**-0.5
    lane = lax.broadcasted_iota(jnp.int32, (BLOCK, LANES), 1)
    stats_t = []
    for start in range(0, length, BLOCK):
        at = pl.ds(start, BLOCK)
        d_att = dot(rows_s[at, :], wo_ref[...], NT).astype(low)
        d_att_s[at, :] = d_att
        product = d_att.astype(wide) * att_ref[at, :].astype(wide)
        stats = lse_ref[at, :]
        for h in range(heads):
            part = product[:, (h // 2) * LANES : (h // 2 + 1) * LANES]
            mine = lane // HEAD_WIDTH == h % 2
            inner = jnp.sum(jnp.where(mine, part, 0.0), axis=1, keepdims=True)
            stats = jnp.where(lane == heads + h, inner, stats)
        stats_t.append(jnp.transpose(stats))
        keys, values = spread_heads(k_ref[at, :].astype(wide)), spread_heads(v_ref[at, :].astype(wide))
        for g in range(2):
            for off in range(2):
                kz_s[2 * g + off, at, :] = keys[g][off].astype(low)
                vz_s[2 * g + off, at, :] = values[g][off].astype(low)
                kt_s[2 * g + off, :, at] = jnp.transpose(keys[g][off]).astype(low)
    d_key_s[...] = jnp.zeros_like(d_key_s)
    d_value_s[...] = jnp.zeros_like(d_value_s)
    for i, start in enumerate(range(0, length, BLOCK)):
        at = pl.ds(start, BLOCK)
        first = max(0, start - REACH)
        span = start + BLOCK - first
        keys_at = pl.ds(first, span)
        key_id = lax.broadcasted_iota(jnp.int32, (span, BLOCK), 0) + first
        query_id = lax.broadcasted_iota(jnp.int32, (span, BLOCK), 1) + start
        allowed = (column_of(row_ref, first, span) == row_ref[:, at]) & (query_id >= key_id)
        bias = jnp.where(allowed, 0.0, NEG)
        for j in range(pairs):
            query = q_ref[at, j * LANES : (j + 1) * LANES]
            d_att = d_att_s[at, j * LANES : (j + 1) * LANES]
            total = None
            for off in range(2):
                h = 2 * j + off
                slot = 2 * (h // pairs) + off
                scores = dot(kz_s[slot, keys_at, :], query, NT) + bias
                probs = jnp.exp(scores - stats_t[i][h : h + 1, :])
                d_probs = dot(vz_s[slot, keys_at, :], d_att, NT)
                d_scores = probs * (d_probs - stats_t[i][heads + h : heads + h + 1, :])
                d_scores = d_scores.astype(low)
                d_value_s[slot, keys_at, :] += dot(probs.astype(low), d_att, NN)
                d_key_s[slot, keys_at, :] += dot(d_scores, query, NN)
                part = dot(kt_s[slot, :, keys_at], d_scores, NN)
                total = part if total is None else total + part
            d_query_s[j * LANES : (j + 1) * LANES, at] = total
    for start in range(0, length, BLOCK):
        at = pl.ds(start, BLOCK)
        cos, sin = cos_ref[at, :], sin_ref[at, :]
        for j in range(pairs):
            part = jnp.transpose(d_query_s[j * LANES : (j + 1) * LANES, at]) * scale
            turned = part * cos - half_turn(part) * sin
            d_lin_ref[at, j * LANES : (j + 1) * LANES] = turned.astype(low)
        both_of = []
        for ref in (d_key_s, d_value_s):
            first_head = ref[0, at, :] + pltpu.roll(ref[1, at, :], HEAD_WIDTH, 1)
            second_head = ref[3, at, :] + pltpu.roll(ref[2, at, :], HEAD_WIDTH, 1)
            both_of.append(jnp.where(lane < HEAD_WIDTH, first_head, second_head))
        d_key, d_value = both_of
        d_lin_ref[at, q_width : q_width + LANES] = (d_key * cos - half_turn(d_key) * sin).astype(low)
        d_lin_ref[at, q_width + LANES :] = d_value.astype(low)


def attend_back(place, blocks, wo, att, q, k, v, lse, cos, sin, segs, after):
    rows, width = blocks[0].shape
    length, q_width = att.shape
    return call(
        attend_back_body,
        (place, *blocks, wo, att, q, k, v, lse, cos, sin, segs.reshape(1, length)),
        [SMEM] + [ANY] * 4 + [VMEM] * 9,
        VMEM,
        Shape((length, q_width + 2 * LANES), low),
        [
            pltpu.VMEM((length, width), low),
            pltpu.VMEM((4, length, LANES), low),
            pltpu.VMEM((4, LANES, length), low),
            pltpu.VMEM((4, length, LANES), low),
            pltpu.VMEM((length, q_width), low),
            pltpu.VMEM((4, length, LANES), wide),
            pltpu.VMEM((4, length, LANES), wide),
            pltpu.VMEM((q_width, length), wide),
            pltpu.SemaphoreType.DMA((4,)),
        ],
        after=after,
        name="attend_back",
        cost=(15e-6 * 1.1e15, 12e6),
    )


def split_add_body(place_ref, mine_ref, got_ref, kept_ref, sent_ref):
    far = place_ref[0] // 2
    kept_ref[...] = (mine_ref[far].astype(wide) + got_ref[far].astype(wide)).astype(low)
    sent_ref[...] = (mine_ref[1 - far].astype(wide) + got_ref[1 - far].astype(wide)).astype(low)


def tensor_scatter(place, mine, other, after):
    rows, width = mine.shape[1:]
    got = swap(other, "tensor", 1)
    kept, sent = call(
        split_add_body,
        (place, mine, got),
        [SMEM, VMEM, VMEM],
        [VMEM, VMEM],
        [Shape((rows, width), low)] * 2,
        after=after,
        name="split_add",
        cost=(1e9, 6e6),
    )
    return kept, swap(sent, "tensor", 2)


def expert_body(pieces, cuts, local, *refs):
    rows_refs = refs[:pieces]
    up_refs = refs[pieces : 2 * pieces]
    sel_ref, router_ref, gate_ref, up_w_ref, down_ref = refs[2 * pieces : 2 * pieces + 5]
    outs = refs[2 * pieces + 5 :]
    d_rows_refs, mixed_refs = outs[:pieces], outs[pieces : 2 * pieces]
    hidden_ref, d_gate_ref, d_up_ref = outs[2 * pieces : 2 * pieces + 3]
    rows_s, ups_s, d_rows_s, mixed_s, gates_s, d_gates_s, sems = outs[2 * pieces + 3 :]
    step = pl.program_id(0)
    width = rows_s.shape[1]

    @pl.when(step == 0)
    def _():
        copies = []
        for side, (sources, target) in enumerate(((rows_refs, rows_s), (up_refs, ups_s))):
            start = 0
            for i, source in enumerate(sources):
                size = source.shape[0]
                copies.append(
                    pltpu.make_async_copy(
                        source, target.at[pl.ds(start, size), :], sems.at[side * pieces + i]
                    )
                )
                start += size
        for copy in copies:
            copy.start()
        wait_all(copies)
        chosen = ups_s[:, width:] > 0.0
        logits = jnp.where(chosen, dot(rows_s[...], router_ref[...], NN), NEG)
        largest = jnp.max(logits, axis=1, keepdims=True)
        shifted = jnp.where(chosen, jnp.exp(logits - largest), 0.0)
        gates_s[...] = shifted / jnp.sum(shifted, axis=1, keepdims=True)
        d_gates_s[...] = jnp.zeros_like(d_gates_s)

    expert = step // cuts
    pick = sel_ref[0:1, :]
    for e in range(1, local):
        pick = jnp.where(expert == e, sel_ref[e : e + 1, :], pick)
    gate = jnp.sum(gates_s[...] * pick, axis=1, keepdims=True)
    rows = rows_s[...]
    ups = ups_s[:, :width]
    gate_w, up_w, down_w = gate_ref[0], up_w_ref[0], down_ref[0]
    gate_pre = dot(rows, gate_w, NN)
    up_pre = dot(rows, up_w, NN)
    d_act = dot(ups, down_w, NT)
    sig = 1.0 / (1.0 + jnp.exp(-gate_pre))
    act = gate_pre * sig
    hidden = act * up_pre
    d_gates_s[...] += jnp.sum(hidden * d_act, axis=1, keepdims=True) * pick
    hidden = (gate * hidden).astype(low)
    d_act = gate * d_act
    d_gate = (d_act * up_pre * sig * (1.0 + gate_pre * (1.0 - sig))).astype(low)
    d_up = (d_act * act).astype(low)
    hidden_ref[...] = hidden
    d_gate_ref[...] = d_gate
    d_up_ref[...] = d_up
    d_rows = dot(d_gate, gate_w, NT) + dot(d_up, up_w, NT)
    mixed = dot(hidden, down_w, NN)

    @pl.when(step == 0)
    def _():
        d_rows_s[...] = d_rows
        mixed_s[...] = mixed

    @pl.when(step > 0)
    def _():
        d_rows_s[...] += d_rows
        mixed_s[...] += mixed

    @pl.when(step == pl.num_programs(0) - 1)
    def _():
        lane = lax.broadcasted_iota(jnp.int32, d_gates_s.shape, 1)
        d_gates = d_gates_s[...]
        d_gates = jnp.where(lane < LANES // 2, d_gates, pltpu.roll(d_gates, LANES // 2, 1))
        rounded = d_gates.astype(low).astype(wide)
        d_gates = jnp.where(lane < LANES // 2, rounded, d_gates - rounded).astype(low)
        start = 0
        for d_rows_ref, mixed_ref in zip(d_rows_refs, mixed_refs):
            size = d_rows_ref.shape[0]
            d_rows_ref[:, :width] = d_rows_s[start : start + size, :].astype(low)
            d_rows_ref[:, width:] = d_gates[start : start + size, :]
            mixed_ref[...] = mixed_s[start : start + size, :].astype(low)
            start += size


def expert_block(rows_list, ups_list, sel, w_router, w_gate, w_up, w_down, after=()):
    pieces = len(rows_list)
    sizes = [rows.shape[0] for rows in rows_list]
    rows = sum(sizes)
    local, width, ff = w_gate.shape
    cut = min(512, ff)
    cuts = ff // cut
    whole = lambda shape: pl.BlockSpec(shape, lambda j: (0,) * len(shape))
    across = pl.BlockSpec((1, width, cut), lambda j: (j // cuts, 0, j % cuts))
    tall = pl.BlockSpec((1, cut, width), lambda j: (j // cuts, j % cuts, 0))
    part = pl.BlockSpec((rows, cut), lambda j: (0, j))
    outs = call(
        functools.partial(expert_body, pieces, cuts, local),
        (*rows_list, *ups_list, sel, w_router, w_gate, w_up, w_down),
        [ANY] * (2 * pieces) + [whole((local, LANES)), whole((width, LANES)), across, across, tall],
        [whole((size, width + LANES)) for size in sizes]
        + [whole((size, width)) for size in sizes]
        + [part, part, part],
        [Shape((size, width + LANES), low) for size in sizes]
        + [Shape((size, width), low) for size in sizes]
        + [Shape((rows, local * ff), low)] * 3,
        [
            pltpu.VMEM((rows, width), low),
            pltpu.VMEM((rows, width + LANES), low),
            pltpu.VMEM((rows, width), wide),
            pltpu.VMEM((rows, width), wide),
            pltpu.VMEM((rows, LANES), wide),
            pltpu.VMEM((rows, LANES), wide),
            pltpu.SemaphoreType.DMA((2 * pieces,)),
        ],
        grid=(local * cuts,),
        after=after,
        name="experts",
        cost=(19 * rows * width * local * ff, 6 * local * width * ff + 8 * rows * width),
    )
    return outs[:pieces], outs[pieces : 2 * pieces], outs[2 * pieces :]


def outer_body(pieces, seconds, split, *refs):
    first_refs = refs[:pieces]
    second_refs = refs[pieces : pieces + seconds]
    out_ref, first_s, second_s, first_sems, second_sems = refs[pieces + seconds :]
    step = pl.program_id(0)
    cut = first_s.shape[2]
    width = second_s.shape[1]

    def load(at, slot):
        copies, start = [], 0
        for i, ref in enumerate(first_refs):
            size = ref.shape[0]
            copies.append(
                pltpu.make_async_copy(
                    ref.at[:, pl.ds(pl.multiple_of(at * cut, cut), cut)],
                    first_s.at[slot, pl.ds(start, size), :],
                    first_sems.at[slot, i],
                )
            )
            start += size
        return copies

    slot = step % 2

    @pl.when(step == 0)
    def _():
        for copy in load(0, 0):
            copy.start()
        copies, start = [], 0
        for i, ref in enumerate(second_refs):
            size = ref.shape[0]
            copies.append(
                pltpu.make_async_copy(
                    ref.at[:, pl.ds(0, width)], second_s.at[pl.ds(start, size), :], second_sems.at[i]
                )
            )
            start += size
        for copy in copies:
            copy.start()
        wait_all(copies)

    @pl.when(step + 1 < pl.num_programs(0))
    def _():
        for copy in load(step + 1, 1 - slot):
            copy.start()

    wait_all(load(step, slot))
    product = dot(first_s[slot], second_s[...], TN).astype(low)
    if split == 1:
        out_ref[0] = product
    else:
        part = width // split
        for e in range(split):
            out_ref[e] = product[:, e * part : (e + 1) * part]


def outer_products(first, second, first_width, second_width, split, after=()):
    cut = 512
    steps = first_width // cut
    rows = sum(piece.shape[0] for piece in first)
    if split == 1:
        out_shape = Shape((steps, cut, second_width), low)
        out_spec = pl.BlockSpec((1, cut, second_width), lambda i: (i, 0, 0))
    else:
        part = second_width // split
        out_shape = Shape((split, first_width, part), low)
        out_spec = pl.BlockSpec((split, cut, part), lambda i: (0, i, 0))
    return call(
        functools.partial(outer_body, len(first), len(second), split),
        (*first, *second),
        [ANY] * (len(first) + len(second)),
        out_spec,
        out_shape,
        [
            pltpu.VMEM((2, rows, cut), low),
            pltpu.VMEM((rows, second_width), low),
            pltpu.SemaphoreType.DMA((2, len(first))),
            pltpu.SemaphoreType.DMA((len(second),)),
        ],
        grid=(steps,),
        after=after,
        name="outer_products",
        cost=(3.5 * rows * first_width * second_width, 12e6),
    )


def head_grads_body(count, place_ref, ids_ref, *refs):
    rows_refs, d_refs = refs[:4], refs[4:8]
    att_ref, d_lin_ref, wq_ref, wk_ref, wv_ref, gain_ref = refs[8:14]
    outs = refs[14 : 14 + count + 1]
    gain_out, rows_s, d_s, flat_s, sems = refs[15 + count :]
    place = place_ref[0]
    copies = load_blocks(place, rows_refs, rows_s, sems)
    start = pl.multiple_of
    rows = rows_refs[0].shape[0]
    more = []
    for mask, block in enumerate(d_refs):
        at = pl.ds(start((place ^ mask) * rows, rows), rows)
        more.append(pltpu.make_async_copy(block, d_s.at[at, :], sems.at[4 + mask]))
    for copy in more:
        copy.start()
    wait_all(copies)
    q_width, kv_width = wq_ref.shape[1], wk_ref.shape[1]
    lin_width = d_lin_ref.shape[1]
    width = rows_s.shape[1]
    for at in range(0, width, 512):
        here = pl.ds(at, 512)
        grads = dot(rows_s[:, here], d_lin_ref[...], TN)
        for c in range(0, lin_width, LANES):
            flat_s[c // LANES * width + at : c // LANES * width + at + 512, :] = grads[:, c : c + LANES].astype(low)
        inner = jnp.sum(wq_ref[here, :].astype(wide) * grads[:, :q_width], axis=1, keepdims=True)
        inner += jnp.sum(
            wk_ref[here, :].astype(wide) * grads[:, q_width : q_width + kv_width], axis=1, keepdims=True
        )
        inner += jnp.sum(
            wv_ref[here, :].astype(wide) * grads[:, q_width + kv_width :], axis=1, keepdims=True
        )
        inner = jnp.transpose(jnp.broadcast_to(inner, (512, LANES)))[:1]
        gain_out[:, here] = inner / gain_ref[:, here]
    wait_all(more)
    base = lin_width // LANES * width
    for at in range(0, width, 512):
        grads = dot(att_ref[...], d_s[:, at : at + 512], TN).astype(low)
        for c in range(0, 512, LANES):
            row = base + (at + c) // LANES * q_width
            flat_s[row : row + q_width, :] = grads[:, c : c + LANES]
    for o, ref in enumerate(outs):
        size = ref.shape[0]
        part = flat_s.shape[0] // count
        if o < count // 2:
            at = ids_ref[o] * part
        elif o > count // 2 + 1:
            at = ids_ref[o - 1] * part
        else:
            at = ids_ref[count // 2] * part + (o - count // 2) * size
        ref[...] = flat_s[pl.ds(start(at, size), size), :]


def head_grads(place, ids, rows_blocks, d_blocks, att, d_lin, wq, wk, wv, gain):
    count = lax.axis_size("dp")
    rows, width = rows_blocks[0].shape
    length, q_width = att.shape
    flat = width * (d_lin.shape[1] + q_width) // LANES
    part = flat // count
    sizes = [part] * (count // 2) + [part // 2] * 2 + [part] * (count // 2 - 1)
    outs = call(
        functools.partial(head_grads_body, count),
        (place, ids, *rows_blocks, *d_blocks, att, d_lin, wq, wk, wv, gain),
        [SMEM, SMEM] + [ANY] * 8 + [VMEM] * 6,
        [VMEM] * (count + 2),
        [Shape((size, LANES), low) for size in sizes] + [Shape((1, width), wide)],
        [
            pltpu.VMEM((length, width), low),
            pltpu.VMEM((length, width), low),
            pltpu.VMEM((flat, LANES), low),
            pltpu.SemaphoreType.DMA((8,)),
        ],
        name="head_grads",
        cost=(6e-6 * 1.1e15, 12e6),
    )
    parts = list(outs[: count // 2]) + [(outs[count // 2], outs[count // 2 + 1])] + list(outs[count // 2 + 2 : -1])
    return parts, outs[-1]


def head_place_body(count, ids_ref, *refs):
    blocks = refs[: count + 1]
    grad_q, grad_k, grad_v, grad_o, flat_s = refs[count + 1 :]
    width, q_width = grad_q.shape
    part = flat_s.shape[0] // count
    for o, ref in enumerate(blocks):
        size = ref.shape[0]
        if o < count // 2:
            at = ids_ref[o] * part
        elif o > count // 2 + 1:
            at = ids_ref[o - 1] * part
        else:
            at = ids_ref[count // 2] * part + (o - count // 2) * size
        flat_s[pl.ds(pl.multiple_of(at, size), size), :] = ref[...]
    row = 0
    for ref in (grad_q, grad_k, grad_v, grad_o):
        rows, columns = ref.shape
        for c in range(0, columns, LANES):
            ref[:, c : c + LANES] = flat_s[row : row + rows, :].astype(wide)
            row += rows


def head_place(ids, blocks, width, q_width, kv_width):
    count = lax.axis_size("dp")
    return call(
        functools.partial(head_place_body, count),
        (ids, *blocks),
        [SMEM] + [VMEM] * (count + 1),
        [VMEM] * 4,
        [
            Shape((width, q_width), wide),
            Shape((width, kv_width), wide),
            Shape((width, kv_width), wide),
            Shape((q_width, width), wide),
        ],
        [pltpu.VMEM((width * (2 * q_width + 2 * kv_width) // LANES, LANES), low)],
        name="head_place",
        cost=(1e9, 8e6),
    )


def widen_body(in_ref, out_ref):
    out_ref[...] = in_ref[...].astype(wide)


def widen(array, after):
    count, rows, columns = array.shape
    spec = pl.BlockSpec((1, 256, columns), lambda i: (i * 256 // rows, i % (rows // 256), 0))
    return call(
        widen_body, (array,), [spec], spec, Shape(array.shape, wide), grid=(count * rows // 256,),
        after=after, name="widen", cost=(1e8, 10e6),
    )


def lin_back_body(place_ref, d_lin_ref, wq_ref, wk_ref, wv_ref, mine_ref, other_ref):
    rows = mine_ref.shape[1]
    core = place_ref[0] % 2
    q_width, kv_width = wq_ref.shape[1], wk_ref.shape[1]
    for x in range(2):
        for ref, c in ((other_ref, 1 - core), (mine_ref, core)):
            at = pl.ds(pl.multiple_of((2 * x + c) * rows, rows), rows)
            total = dot(d_lin_ref[at, :q_width], wq_ref[...], NT)
            total += dot(d_lin_ref[at, q_width : q_width + kv_width], wk_ref[...], NT)
            total += dot(d_lin_ref[at, q_width + kv_width :], wv_ref[...], NT)
            ref[x] = total.astype(low)


def lin_back(place, d_lin, wq, wk, wv, after):
    rows, width = d_lin.shape[0] // 4, wq.shape[0]
    return call(
        lin_back_body,
        (place, d_lin, wq, wk, wv),
        [SMEM] + [VMEM] * 4,
        [VMEM] * 2,
        [Shape((2, rows, width), low)] * 2,
        after=after,
        name="lin_back",
        cost=(4e-6 * 1.1e15, 9e6),
    )


def first_norm_body(tokens_ref, gain_ref, normed_ref):
    inputs = tokens_ref[...].astype(wide)
    inverse = lax.rsqrt(jnp.mean(inputs * inputs, axis=1, keepdims=True) + EPS)
    normed_ref[...] = (inputs * inverse * gain_ref[...]).astype(low)


def second_norm_body(tokens_ref, kept_ref, got_ref, gain_ref, residual_ref, normed_ref):
    residual = tokens_ref[...].astype(wide) + (kept_ref[...].astype(wide) + got_ref[...].astype(wide))
    inverse = lax.rsqrt(jnp.mean(residual * residual, axis=1, keepdims=True) + EPS)
    residual_ref[...] = residual
    normed_ref[...] = (residual * inverse * gain_ref[...]).astype(low)


def middle_body(
    own_ref, up_ref, down_ref, residual_ref, normed_ref, ups_ref, router_ref, gain_ref, passed_ref,
    d_residual_ref, d_low_ref, gain_out, router_out, passed_out,
):
    del passed_ref, passed_out
    width = residual_ref.shape[1]
    total = own_ref[...].astype(wide) + up_ref[...].astype(wide) + down_ref[...].astype(wide)
    d_gates = total[:, width:]
    d_gates = d_gates + pltpu.roll(d_gates, LANES // 2, 1)
    lane = lax.broadcasted_iota(jnp.int32, d_gates.shape, 1)
    chosen = ups_ref[:, width:] > 0.0
    normed = normed_ref[...]
    logits = jnp.where(chosen, dot(normed, router_ref[...], NN), NEG)
    largest = jnp.max(logits, axis=1, keepdims=True)
    shifted = jnp.where(chosen, jnp.exp(logits - largest), 0.0)
    gates = shifted / jnp.sum(shifted, axis=1, keepdims=True)
    inner = jnp.sum(gates * d_gates, axis=1, keepdims=True)
    d_logits = (gates * (d_gates - inner)).astype(low)
    router_out[...] = dot(d_logits, normed, TN)[: router_out.shape[0]]
    d_normed = total[:, :width] + dot(d_logits, router_ref[...], NT)
    residual = residual_ref[...]
    inverse = lax.rsqrt(jnp.mean(residual * residual, axis=1, keepdims=True) + EPS)
    scaled = d_normed * gain_ref[...]
    mean = jnp.mean(scaled * residual, axis=1, keepdims=True)
    upstream = ups_ref[:, :width].astype(wide)
    d_residual = upstream + inverse * scaled - residual * (inverse * inverse * inverse * mean)
    gain_out[...] = jnp.sum(d_normed * residual * inverse, axis=0, keepdims=True)
    d_residual_ref[...] = d_residual
    d_low_ref[...] = d_residual.astype(low)


def last_body(tokens_ref, kept_ref, got_ref, d_residual_ref, gain_ref, out_ref):
    inputs = tokens_ref[...].astype(wide)
    inverse = lax.rsqrt(jnp.mean(inputs * inputs, axis=1, keepdims=True) + EPS)
    scaled = (kept_ref[...].astype(wide) + got_ref[...].astype(wide)) * gain_ref[...]
    mean = jnp.mean(scaled * inputs, axis=1, keepdims=True)
    d_inputs = inverse * scaled - inputs * (inverse * inverse * inverse * mean)
    out_ref[...] = (d_inputs + d_residual_ref[...]).astype(low)


def on_device(
    tokens,
    gain_attn,
    query_weight,
    key_weight,
    value_weight,
    w_output,
    gain_ffn,
    w_router,
    w_gate,
    w_up,
    w_down,
    segments,
    routes,
    cotangent,
):
    rows_dev, width = tokens.shape
    data_count = lax.axis_size("dp")
    half_count = data_count // 2
    local_experts, _, ff = w_gate.shape
    expert_count = local_experts * data_count
    q_width, kv_width = query_weight.shape[1], key_weight.shape[1]
    place = lax.axis_index("tensor").astype(jnp.int32).reshape(1)
    ids = ring_places()
    cos, sin = rope_tables(segments.shape[1])
    gain_one, gain_two = gain_attn.reshape(1, width), gain_ffn.reshape(1, width)
    lanes = jnp.arange(LANES, dtype=jnp.int32)
    own_experts = lax.axis_index("dp") * local_experts + jnp.arange(local_experts, dtype=jnp.int32)
    sel = (own_experts[:, None] == lanes[None, :]).astype(wide)
    router = jnp.pad(w_router, ((0, 0), (0, LANES - expert_count)))
    chosen = jnp.any(routes[:, :, None] == lanes[None, None, :], axis=1).astype(low)
    ups = jnp.concatenate([cotangent, chosen], axis=1)

    normed_one = call(
        first_norm_body, (tokens, gain_one), [VMEM] * 2, VMEM, Shape((rows_dev, width), low),
        name="first_norm", cost=(1e9, 2e6),
    )
    ups_below, ups_above, ups_far = ring_gather(ups)
    rows_blocks = tensor_blocks(normed_one)
    att, q, k, v, lse = attend(
        place, rows_blocks, query_weight, key_weight, value_weight, cos, sin, segments,
        after=(ups_below[0], ups_above[0]),
    )
    other = branch_half(place, att, w_output, True)
    mine = branch_half(place, att, w_output, False, after=(ups_below[1], ups_above[1]))
    kept, got = tensor_scatter(place, mine, other, after=())
    residual, normed_two = call(
        second_norm_body, (tokens, kept, got, gain_two), [VMEM] * 4, [VMEM] * 2,
        [Shape((rows_dev, width), wide), Shape((rows_dev, width), low)],
        after=(ups_below[2], ups_above[2]), name="second_norm", cost=(1e9, 4e6),
    )
    rows_below, rows_above, rows_far = ring_gather(normed_two)
    groups = [((normed_two,), (ups,))]
    for k_ in range(half_count - 1):
        groups.append(((rows_below[k_], rows_above[k_]), (ups_below[k_], ups_above[k_])))
    groups.append((rows_far, ups_far))
    done = []
    for rows, up in groups:
        after = () if not done else (done[-1][2][0],)
        if len(done) == 1:
            after += tuple(ups_far)
        done.append(expert_block(rows, up, sel, router, w_gate, w_up, w_down, after))
    d_rows_up, d_rows_down = ring_scatter(
        [outs[0][0] for outs in done[1:-1]], [outs[0][1] for outs in done[1:-1]], done[-1][0]
    )
    far_mixed = list(done[-1][1])
    d_residual, d_low, gain_ffn_part, router_part, far_mixed[0] = call(
        middle_body,
        (done[0][0][0], d_rows_up, d_rows_down, residual, normed_two, ups, router, gain_two, far_mixed[0]),
        [VMEM] * 8 + [ANY],
        [VMEM] * 4 + [ANY],
        [
            Shape((rows_dev, width), wide),
            Shape((rows_dev, width), low),
            Shape((1, width), wide),
            Shape((expert_count, width), wide),
            Shape(far_mixed[0].shape, low),
        ],
        name="middle", cost=(4e-6 * 1.1e15, 4e6), alias={8: 4},
    )
    rows_all = [piece for rows, _ in groups for piece in rows]
    ups_all = [piece for _, up in groups for piece in up]
    hidden_all, d_gate_all, d_up_all = ([outs[2][i] for outs in done] for i in range(3))
    inner = local_experts * ff
    grad_down = outer_products(hidden_all, ups_all, inner, width, 1).reshape(local_experts, ff, width)
    grad_gate = outer_products(rows_all, d_gate_all, width, inner, local_experts)
    grad_up = outer_products(rows_all, d_up_all, width, inner, local_experts)
    grad_gate, grad_up, grad_down = (
        lax.psum(grad, "tensor") for grad in (grad_gate, grad_up, grad_down)
    )
    mixed_up, mixed_down = ring_scatter(
        [outs[1][0] for outs in done[1:-1]], [outs[1][1] for outs in done[1:-1]], far_mixed
    )
    mixed = (
        residual + done[0][1][0].astype(wide) + mixed_up.astype(wide) + mixed_down.astype(wide)
    ).astype(low)

    d_blocks = tensor_blocks(d_low)
    d_lin = attend_back(place, d_blocks, w_output, att, q, k, v, lse, cos, sin, segments, after=())
    parts, gain_attn_part = head_grads(
        place, ids, rows_blocks, d_blocks, att, d_lin, query_weight, key_weight, value_weight, gain_one
    )
    mine, other = lin_back(place, d_lin, query_weight, key_weight, value_weight, after=())
    kept, got = tensor_scatter(place, mine, other, after=())
    grad_tokens = call(
        last_body, (tokens, kept, got, d_residual, gain_one), [VMEM] * 5, VMEM,
        Shape((rows_dev, width), low), name="last", cost=(1e9, 4e6),
    )
    up, down = ring_scatter(
        [parts[data_count - 1 - i] for i in range(half_count - 1)],
        [parts[1 + i] for i in range(half_count - 1)],
        parts[half_count],
    )
    total = (parts[0].astype(wide) + up.astype(wide) + down.astype(wide)).astype(low)
    below, above, far = ring_gather(total)
    grad_q, grad_k, grad_v, grad_o = head_place(
        ids, [total] + above + list(far) + below[::-1], width, q_width, kv_width
    )
    grad_gate = widen(grad_gate, (below[0], above[0]))
    grad_up = widen(grad_up, (below[0], above[0]))
    grad_down = widen(grad_down, (below[0], above[0]))
    small = jnp.concatenate([gain_ffn_part, gain_attn_part, router_part], axis=0)
    small = cube_sum(small, ("tensor", "dp"))
    return (
        mixed,
        grad_tokens,
        small[1],
        grad_q,
        grad_k,
        grad_v,
        grad_o,
        small[0],
        small[2:].T,
        grad_gate,
        grad_up,
        grad_down,
    )


def solution(mesh):
    in_specs = (
        P(("dp", "tensor"), None),
        P(),
        P(None, "tensor"),
        P(None, "tensor"),
        P(None, "tensor"),
        P("tensor", None),
        P(),
        P(),
        P("dp", None, None),
        P("dp", None, None),
        P("dp", None, None),
        P("dp", None),
        P(("dp", "tensor"), None),
        P(("dp", "tensor"), None),
    )
    out_specs = (
        P(("dp", "tensor"), None),
        P(("dp", "tensor"), None),
        P(),
        P(None, "tensor"),
        P(None, "tensor"),
        P(None, "tensor"),
        P("tensor", None),
        P(),
        P(),
        P("dp", None, None),
        P("dp", None, None),
        P("dp", None, None),
    )
    return jax.shard_map(
        on_device, mesh=mesh, in_specs=in_specs, out_specs=out_specs, check_vma=False
    )
```

```python
import functools
import math

import jax
import jax.numpy as jnp
import numpy as np
from jax import lax
from jax.experimental import pallas as pl
from jax.experimental.pallas import tpu as pltpu
from jax.sharding import PartitionSpec as P

HEAD_WIDTH = 64
EPS = 1e-06
ROPE_BASE = 10000.0
NEG = -1e30
LANES = 128
BLOCK = 256
REACH = 512
MEGABYTE = 1024 * 1024
low = jnp.bfloat16
wide = jnp.float32
NN = (((1,), (0,)), ((), ()))
NT = (((1,), (1,)), ((), ()))
TN = (((0,), (0,)), ((), ()))
dot = functools.partial(lax.dot_general, preferred_element_type=jnp.float32)
Shape = jax.ShapeDtypeStruct
ANY = pl.BlockSpec(memory_space=pl.ANY)
VMEM = pl.BlockSpec(memory_space=pltpu.VMEM)
SMEM = pl.BlockSpec(memory_space=pltpu.SMEM)


def rope_tables(length):
    half = HEAD_WIDTH // 2
    freq = np.exp(-(np.arange(half, dtype=np.float32) * (2.0 / HEAD_WIDTH)) * math.log(ROPE_BASE))
    angle = np.arange(length, dtype=np.float32)[:, None] * freq.astype(np.float32)[None, :]
    cos, sin = np.cos(angle), np.sin(angle)
    cos = np.concatenate([cos] * 4, axis=1).astype(np.float32)
    sin = np.concatenate([-sin, sin, -sin, sin], axis=1).astype(np.float32)
    return jnp.asarray(cos), jnp.asarray(sin)


def ring_order(count):
    return list(range(0, count, 2)) + list(range(count - 1, 0, -2))


def ring_send(array, step):
    count = lax.axis_size("dp")
    order = ring_order(count)
    return lax.ppermute(
        array, "dp", [(order[i], order[(i + step) % count]) for i in range(count)]
    )


def ring_places():
    count = lax.axis_size("dp")
    order = ring_order(count)
    table = [[(order.index(i) + o) % count for o in range(count)] for i in range(count)]
    table = jnp.asarray(np.asarray(table, np.int32))
    return lax.dynamic_index_in_dim(table, lax.axis_index("dp"), 0, keepdims=False)


def ring_gather(array, last=None):
    count = lax.axis_size("dp")
    half = array.shape[0] // 2
    below, above = [], []
    up, down = array, array
    for _ in range(count // 2 - 1):
        up = ring_send(up, 1)
        down = ring_send(down, -1)
        below.append(up)
        above.append(down)
    if last is not None:
        up, down = last(below, above)
    top = ring_send(up[:half], 1)
    bottom = ring_send(down[half:], -1)
    return below, above, (top, bottom)


def swap(array, axis, mask):
    return lax.ppermute(array, axis, [(i, i ^ mask) for i in range(lax.axis_size(axis))])


def cube_sum(array, axes):
    for axis in axes:
        mask = 1
        while mask < lax.axis_size(axis):
            array = array + swap(array, axis, mask)
            mask *= 2
    return array


def tensor_blocks(array):
    far = swap(array, "tensor", 2)
    return array, swap(array, "tensor", 1), far, swap(far, "tensor", 1)


def call(body, operands, in_specs, out_specs, out_shape, scratch=(), grid=None, after=(), name=None, cost=None, alias=None, vmem=10):
    count = len(after)
    position = len(operands)

    def kernel(*refs):
        body(*refs[:position], *refs[position + count :])

    extra = {} if grid is None else {"grid": grid}
    if cost is not None:
        extra["cost_estimate"] = pl.CostEstimate(
            flops=int(cost[0]), bytes_accessed=int(cost[1]), transcendentals=0
        )
    if alias is not None:
        extra["input_output_aliases"] = alias
    return pl.pallas_call(
        kernel,
        in_specs=list(in_specs) + [ANY] * count,
        out_specs=out_specs,
        out_shape=out_shape,
        scratch_shapes=list(scratch),
        compiler_params=pltpu.CompilerParams(vmem_limit_bytes=vmem * MEGABYTE),
        name=name,
        **extra,
    )(*operands, *after)


def ring_add_body(first, held, up_ref, part_up_ref, down_ref, part_down_ref, *refs):
    up_out, down_out = refs[held : held + 2]

    def add(got_ref, part_ref, out_ref):
        out_ref[...] = (got_ref[...].astype(wide) + part_ref[...].astype(wide)).astype(low)

    def keep(part_ref, out_ref):
        out_ref[...] = part_ref[...]

    if not first:
        add(up_ref, part_up_ref, up_out)
        add(down_ref, part_down_ref, down_out)
        return

    @pl.when(pl.program_id(0) == 0)
    def _():
        add(up_ref, part_up_ref, up_out)
        keep(part_down_ref, down_out)

    @pl.when(pl.program_id(0) == 1)
    def _():
        keep(part_up_ref, up_out)
        add(down_ref, part_down_ref, down_out)


def ring_add(first, up, part_up, down, part_down, after, held):
    rows, width = part_up.shape
    part = pl.BlockSpec((rows // 2, width), lambda i: (i, 0))
    got = pl.BlockSpec((rows // 2, width), lambda i: (0, 0)) if first else part
    return call(
        functools.partial(ring_add_body, first, len(held)),
        (up, part_up, down, part_down, *held),
        [got, part, got, part] + [ANY] * len(held),
        [part, part] + [ANY] * len(held),
        [Shape((rows, width), low)] * 2 + [Shape(array.shape, array.dtype) for array in held],
        grid=(2,),
        after=after,
        name="ring_add",
        cost=(1e8, 4e6),
        alias={4 + i: 2 + i for i in range(len(held))},
    )


def hold_body(*refs):
    del refs


def hold(arrays, after):
    return call(
        hold_body, arrays, [ANY] * len(arrays), [ANY] * len(arrays),
        [Shape(array.shape, array.dtype) for array in arrays], after=after, name="hold", cost=(1e6, 1e5),
        alias={i: i for i in range(len(arrays))},
    )


def ring_scatter(below, above, opposite, before=None, then=None):
    up = ring_send(opposite[0], 1)
    down = ring_send(opposite[1], -1)
    for index, k in enumerate(range(len(above), 0, -1)):
        after, held = before(index) if before else ((), ())
        up, down, *held = ring_add(index == 0, up, above[k - 1], down, below[k - 1], after, held)
        if then:
            then(index, up, held)
        up = ring_send(up, 1)
        down = ring_send(down, -1)
    return up, down


def half_turn(array):
    width = array.shape[-1]
    half = HEAD_WIDTH // 2
    lane = lax.broadcasted_iota(jnp.int32, array.shape, 1)
    return jnp.where(
        lane % HEAD_WIDTH < half, pltpu.roll(array, width - half, 1), pltpu.roll(array, half, 1)
    )


def spread_heads(array):
    lane = lax.broadcasted_iota(jnp.int32, array.shape, 1)
    first = lane < HEAD_WIDTH
    other = pltpu.roll(array, HEAD_WIDTH, 1)
    zero = jnp.zeros_like(array)
    return [
        [jnp.where(first, array, zero), jnp.where(first, zero, other)],
        [jnp.where(first, other, zero), jnp.where(first, zero, array)],
    ]


def load_blocks(place, blocks, target, sems):
    rows = blocks[0].shape[0]
    copies = []
    for mask, block in enumerate(blocks):
        start = pl.multiple_of((place ^ mask) * rows, rows)
        copies.append(pltpu.make_async_copy(block, target.at[pl.ds(start, rows), :], sems.at[mask]))
    for copy in copies:
        copy.start()
    return copies


def wait_all(copies):
    for copy in copies:
        copy.wait()


def column_of(row_ref, start, size):
    row = jnp.broadcast_to(row_ref[:, start : start + size].astype(wide), (LANES, size))
    return jnp.transpose(row)[:, :1].astype(jnp.int32)


def attend_body(
    place_ref, own, near, far, both, wq_ref, wk_ref, wv_ref, cos_ref, sin_ref, row_ref,
    att_ref, q_ref, k_ref, v_ref, lse_ref, rows_s, kz_s, vz_s, sems,
):
    place = place_ref[0]
    wait_all(load_blocks(place, (own, near, far, both), rows_s, sems))
    length = rows_s.shape[0]
    pairs = wq_ref.shape[1] // LANES
    scale = HEAD_WIDTH**-0.5
    for start in range(0, length, BLOCK):
        at = pl.ds(start, BLOCK)
        rows = rows_s[at, :]
        cos, sin = cos_ref[at, :], sin_ref[at, :]
        query = dot(rows, wq_ref[...], NN)
        for j in range(pairs):
            part = query[:, j * LANES : (j + 1) * LANES]
            turned = (part * cos + half_turn(part) * sin).astype(low)
            q_ref[at, j * LANES : (j + 1) * LANES] = (turned.astype(wide) * scale).astype(low)
        key = dot(rows, wk_ref[...], NN)
        key = (key * cos + half_turn(key) * sin).astype(low)
        k_ref[at, :] = key
        value = dot(rows, wv_ref[...], NN).astype(low)
        v_ref[at, :] = value
        keys, values = spread_heads(key.astype(wide)), spread_heads(value.astype(wide))
        for g in range(2):
            for off in range(2):
                kz_s[2 * g + off, at, :] = keys[g][off].astype(low)
                vz_s[2 * g + off, at, :] = values[g][off].astype(low)
    lane = lax.broadcasted_iota(jnp.int32, (BLOCK, LANES), 1)
    for start in range(0, length, BLOCK):
        at = pl.ds(start, BLOCK)
        first = max(0, start - REACH)
        span = start + BLOCK - first
        keys_at = pl.ds(first, span)
        row_id = lax.broadcasted_iota(jnp.int32, (BLOCK, span), 0) + start
        col_id = lax.broadcasted_iota(jnp.int32, (BLOCK, span), 1) + first
        allowed = (column_of(row_ref, start, BLOCK) == row_ref[:, keys_at]) & (row_id >= col_id)
        bias = jnp.where(allowed, 0.0, NEG)
        stats = jnp.zeros((BLOCK, LANES), wide)
        for j in range(pairs):
            query = q_ref[at, j * LANES : (j + 1) * LANES]
            total = None
            for off in range(2):
                h = 2 * j + off
                slot = 2 * (h // pairs) + off
                scores = dot(query, kz_s[slot, keys_at, :], NT) + bias
                largest = jnp.max(scores, axis=1, keepdims=True)
                shifted = jnp.exp(scores - largest)
                summed = jnp.sum(shifted, axis=1, keepdims=True)
                probs = (shifted * (1.0 / summed)).astype(low)
                part = dot(probs, vz_s[slot, keys_at, :], NN)
                total = part if total is None else total + part
                stats = jnp.where(lane == h, largest + jnp.log(summed), stats)
            att_ref[at, j * LANES : (j + 1) * LANES] = total.astype(low)
        lse_ref[at, :] = stats


def attend(place, blocks, wq, wk, wv, cos, sin, segs, after):
    rows, width = blocks[0].shape
    length = 4 * rows
    return call(
        attend_body,
        (place, *blocks, wq, wk, wv, cos, sin, segs.reshape(1, length)),
        [SMEM] + [ANY] * 4 + [VMEM] * 6,
        [VMEM] * 5,
        [
            Shape((length, wq.shape[1]), low),
            Shape((length, wq.shape[1]), low),
            Shape((length, wk.shape[1]), low),
            Shape((length, wk.shape[1]), low),
            Shape((length, LANES), wide),
        ],
        [
            pltpu.VMEM((length, width), low),
            pltpu.VMEM((4, length, LANES), low),
            pltpu.VMEM((4, length, LANES), low),
            pltpu.SemaphoreType.DMA((4,)),
        ],
        after=after,
        name="attend", vmem=28,
        cost=(15e-6 * 1.1e15, 12e6),
    )


def branch_body(flip, place_ref, att_ref, wo_ref, out_ref):
    rows = out_ref.shape[1]
    core = place_ref[0] % 2
    core = 1 - core if flip else core
    for x in range(2):
        at = pl.ds(pl.multiple_of((2 * x + core) * rows, rows), rows)
        out_ref[x] = dot(att_ref[at, :], wo_ref[...], NN).astype(low)


def branch_half(place, att, wo, flip, after=()):
    rows, width = att.shape[0] // 4, wo.shape[1]
    return call(
        functools.partial(branch_body, flip),
        (place, att, wo),
        [SMEM] + [VMEM] * 2,
        VMEM,
        Shape((2, rows, width), low),
        after=after,
        name="branch", vmem=14,
        cost=(2e9, 4e6),
    )


def attend_back_body(
    place_ref, own, near, far, both, wo_ref, att_ref, q_ref, k_ref, v_ref, lse_ref, cos_ref, sin_ref, row_ref,
    d_lin_ref, rows_s, kz_s, kt_s, vz_s, d_att_s, d_key_s, d_value_s, d_query_s, sems,
):
    place = place_ref[0]
    wait_all(load_blocks(place, (own, near, far, both), rows_s, sems))
    length, q_width = att_ref.shape
    heads = q_width // HEAD_WIDTH
    pairs = heads // 2
    scale = HEAD_WIDTH**-0.5
    lane = lax.broadcasted_iota(jnp.int32, (BLOCK, LANES), 1)
    stats_t = []
    for start in range(0, length, BLOCK):
        at = pl.ds(start, BLOCK)
        d_att = dot(rows_s[at, :], wo_ref[...], NT).astype(low)
        d_att_s[at, :] = d_att
        product = d_att.astype(wide) * att_ref[at, :].astype(wide)
        stats = lse_ref[at, :]
        for h in range(heads):
            part = product[:, (h // 2) * LANES : (h // 2 + 1) * LANES]
            mine = lane // HEAD_WIDTH == h % 2
            inner = jnp.sum(jnp.where(mine, part, 0.0), axis=1, keepdims=True)
            stats = jnp.where(lane == heads + h, inner, stats)
        stats_t.append(jnp.transpose(stats))
        keys, values = spread_heads(k_ref[at, :].astype(wide)), spread_heads(v_ref[at, :].astype(wide))
        for g in range(2):
            for off in range(2):
                kz_s[2 * g + off, at, :] = keys[g][off].astype(low)
                vz_s[2 * g + off, at, :] = values[g][off].astype(low)
                kt_s[2 * g + off, :, at] = jnp.transpose(keys[g][off]).astype(low)
    d_key_s[...] = jnp.zeros_like(d_key_s)
    d_value_s[...] = jnp.zeros_like(d_value_s)
    for i, start in enumerate(range(0, length, BLOCK)):
        at = pl.ds(start, BLOCK)
        first = max(0, start - REACH)
        span = start + BLOCK - first
        keys_at = pl.ds(first, span)
        key_id = lax.broadcasted_iota(jnp.int32, (span, BLOCK), 0) + first
        query_id = lax.broadcasted_iota(jnp.int32, (span, BLOCK), 1) + start
        allowed = (column_of(row_ref, first, span) == row_ref[:, at]) & (query_id >= key_id)
        bias = jnp.where(allowed, 0.0, NEG)
        for j in range(pairs):
            query = q_ref[at, j * LANES : (j + 1) * LANES]
            d_att = d_att_s[at, j * LANES : (j + 1) * LANES]
            total = None
            for off in range(2):
                h = 2 * j + off
                slot = 2 * (h // pairs) + off
                scores = dot(kz_s[slot, keys_at, :], query, NT) + bias
                probs = jnp.exp(scores - stats_t[i][h : h + 1, :])
                d_probs = dot(vz_s[slot, keys_at, :], d_att, NT)
                d_scores = probs * (d_probs - stats_t[i][heads + h : heads + h + 1, :])
                d_scores = d_scores.astype(low)
                d_value_s[slot, keys_at, :] += dot(probs.astype(low), d_att, NN)
                d_key_s[slot, keys_at, :] += dot(d_scores, query, NN)
                part = dot(kt_s[slot, :, keys_at], d_scores, NN)
                total = part if total is None else total + part
            d_query_s[j * LANES : (j + 1) * LANES, at] = total
    for start in range(0, length, BLOCK):
        at = pl.ds(start, BLOCK)
        cos, sin = cos_ref[at, :], sin_ref[at, :]
        for j in range(pairs):
            part = jnp.transpose(d_query_s[j * LANES : (j + 1) * LANES, at]) * scale
            turned = part * cos - half_turn(part) * sin
            d_lin_ref[at, j * LANES : (j + 1) * LANES] = turned.astype(low)
        both_of = []
        for ref in (d_key_s, d_value_s):
            first_head = ref[0, at, :] + pltpu.roll(ref[1, at, :], HEAD_WIDTH, 1)
            second_head = ref[3, at, :] + pltpu.roll(ref[2, at, :], HEAD_WIDTH, 1)
            both_of.append(jnp.where(lane < HEAD_WIDTH, first_head, second_head))
        d_key, d_value = both_of
        d_lin_ref[at, q_width : q_width + LANES] = (d_key * cos - half_turn(d_key) * sin).astype(low)
        d_lin_ref[at, q_width + LANES :] = d_value.astype(low)


def attend_back(place, blocks, wo, att, q, k, v, lse, cos, sin, segs, after):
    rows, width = blocks[0].shape
    length, q_width = att.shape
    return call(
        attend_back_body,
        (place, *blocks, wo, att, q, k, v, lse, cos, sin, segs.reshape(1, length)),
        [SMEM] + [ANY] * 4 + [VMEM] * 9,
        VMEM,
        Shape((length, q_width + 2 * LANES), low),
        [
            pltpu.VMEM((length, width), low),
            pltpu.VMEM((4, length, LANES), low),
            pltpu.VMEM((4, LANES, length), low),
            pltpu.VMEM((4, length, LANES), low),
            pltpu.VMEM((length, q_width), low),
            pltpu.VMEM((4, length, LANES), wide),
            pltpu.VMEM((4, length, LANES), wide),
            pltpu.VMEM((q_width, length), wide),
            pltpu.SemaphoreType.DMA((4,)),
        ],
        after=after,
        name="attend_back", vmem=32,
        cost=(15e-6 * 1.1e15, 12e6),
    )


def split_add_body(place_ref, mine_ref, got_ref, kept_ref, sent_ref):
    far = place_ref[0] // 2
    kept_ref[...] = (mine_ref[far].astype(wide) + got_ref[far].astype(wide)).astype(low)
    sent_ref[...] = (mine_ref[1 - far].astype(wide) + got_ref[1 - far].astype(wide)).astype(low)


def tensor_scatter(place, mine, other, after):
    kept, sent = split_add(place, mine, swap(other, "tensor", 1), after)
    return kept, swap(sent, "tensor", 2)


def split_add(place, mine, got, after=()):
    rows, width = mine.shape[1:]
    return call(
        split_add_body,
        (place, mine, got),
        [SMEM] + [pl.BlockSpec((2, rows // 2, width), lambda i: (0, i, 0))] * 2,
        [pl.BlockSpec((rows // 2, width), lambda i: (i, 0))] * 2,
        [Shape((rows, width), low)] * 2,
        grid=(2,),
        after=after,
        name="split_add", vmem=12,
        cost=(1e9, 6e6),
    )


def expert_body(pieces, cuts, local, with_mixed, *refs):
    rows_refs = refs[:pieces]
    up_refs = refs[pieces : 2 * pieces]
    d_act_ref, sel_ref, router_ref, gate_ref, up_w_ref = refs[2 * pieces : 2 * pieces + 5]
    outs = refs[2 * pieces + 5 :]
    if with_mixed:
        down_ref, outs = outs[0], outs[1:]
        mixed_refs, outs = outs[:pieces], outs[pieces:]
        mixed_s, outs = outs[-1], outs[:-1]
    d_rows_refs, outs = outs[:pieces], outs[pieces:]
    hidden_ref, d_gate_ref, d_up_ref, rows_s, mask_s, d_rows_s, gates_s, d_gates_s, sems = outs
    step = pl.program_id(0)
    width = rows_s.shape[1]

    @pl.when(step == 0)
    def _():
        copies, start = [], 0
        for i in range(pieces):
            at = pl.ds(start, rows_refs[i].shape[0])
            start += rows_refs[i].shape[0]
            copies.append(pltpu.make_async_copy(rows_refs[i], rows_s.at[at, :], sems.at[i]))
            copies.append(
                pltpu.make_async_copy(
                    up_refs[i].at[:, pl.ds(width, LANES)], mask_s.at[at, :], sems.at[pieces + i]
                )
            )
        for copy in copies:
            copy.start()
        wait_all(copies)
        chosen = mask_s[...] > 0.0
        logits = jnp.where(chosen, dot(rows_s[...], router_ref[...], NN), NEG)
        largest = jnp.max(logits, axis=1, keepdims=True)
        shifted = jnp.where(chosen, jnp.exp(logits - largest), 0.0)
        gates_s[...] = shifted / jnp.sum(shifted, axis=1, keepdims=True)
        d_gates_s[...] = jnp.zeros_like(d_gates_s)

    expert = step // cuts
    pick = sel_ref[0:1, :]
    for e in range(1, local):
        pick = jnp.where(expert == e, sel_ref[e : e + 1, :], pick)
    gate = jnp.sum(gates_s[...] * pick, axis=1, keepdims=True)
    rows = rows_s[...]
    gate_w, up_w = gate_ref[0], up_w_ref[0]
    gate_pre = dot(rows, gate_w, NN)
    up_pre = dot(rows, up_w, NN)
    d_act = d_act_ref[...].astype(wide)
    sig = 1.0 / (1.0 + jnp.exp(-gate_pre))
    act = gate_pre * sig
    hidden = act * up_pre
    d_gates_s[...] += jnp.sum(hidden * d_act, axis=1, keepdims=True) * pick
    hidden = (gate * hidden).astype(low)
    d_act = gate * d_act
    d_gate = (d_act * up_pre * sig * (1.0 + gate_pre * (1.0 - sig))).astype(low)
    d_up = (d_act * act).astype(low)
    hidden_ref[...] = hidden
    d_gate_ref[...] = d_gate
    d_up_ref[...] = d_up
    sums = [(d_rows_s, dot(d_gate, gate_w, NT) + dot(d_up, up_w, NT))]
    if with_mixed:
        sums.append((mixed_s, dot(hidden, down_ref[0], NN)))

    @pl.when(step == 0)
    def _():
        for ref, value in sums:
            ref[...] = value

    @pl.when(step > 0)
    def _():
        for ref, value in sums:
            ref[...] += value

    @pl.when(step == pl.num_programs(0) - 1)
    def _():
        lane = lax.broadcasted_iota(jnp.int32, d_gates_s.shape, 1)
        d_gates = d_gates_s[...]
        d_gates = jnp.where(lane < LANES // 2, d_gates, pltpu.roll(d_gates, LANES // 2, 1))
        rounded = d_gates.astype(low).astype(wide)
        d_gates = jnp.where(lane < LANES // 2, rounded, d_gates - rounded).astype(low)
        start = 0
        for i, d_rows_ref in enumerate(d_rows_refs):
            size = d_rows_ref.shape[0]
            d_rows_ref[:, :width] = d_rows_s[start : start + size, :].astype(low)
            d_rows_ref[:, width:] = d_gates[start : start + size, :]
            if with_mixed:
                mixed_refs[i][...] = mixed_s[start : start + size, :].astype(low)
            start += size


def expert_block(rows_list, ups_list, d_act, sel, w_router, w_gate, w_up, w_down, with_mixed, after=()):
    pieces = len(rows_list)
    sizes = [rows.shape[0] for rows in rows_list]
    rows = sum(sizes)
    local, width, ff = w_gate.shape
    cut = min(512, ff)
    cuts = ff // cut
    whole = lambda shape: pl.BlockSpec(shape, lambda j: (0,) * len(shape))
    across = pl.BlockSpec((1, width, cut), lambda j: (j // cuts, 0, j % cuts))
    tall = pl.BlockSpec((1, cut, width), lambda j: (j // cuts, j % cuts, 0))
    part = pl.BlockSpec((rows, cut), lambda j: (0, j))
    mixed_out = with_mixed * pieces
    outs = call(
        functools.partial(expert_body, pieces, cuts, local, with_mixed),
        (*rows_list, *ups_list, d_act, sel, w_router, w_gate, w_up) + (w_down,) * with_mixed,
        [ANY] * (2 * pieces)
        + [part, whole((local, LANES)), whole((width, LANES)), across, across]
        + [tall] * with_mixed,
        [whole((size, width)) for size in sizes[:mixed_out]]
        + [whole((size, width + LANES)) for size in sizes]
        + [part, part, part],
        [Shape((size, width), low) for size in sizes[:mixed_out]]
        + [Shape((size, width + LANES), low) for size in sizes]
        + [Shape((rows, local * ff), low)] * 3,
        [
            pltpu.VMEM((rows, width), low),
            pltpu.VMEM((rows, LANES), low),
            pltpu.VMEM((rows, width), wide),
            pltpu.VMEM((rows, LANES), wide),
            pltpu.VMEM((rows, LANES), wide),
            pltpu.SemaphoreType.DMA((2 * pieces,)),
        ]
        + [pltpu.VMEM((rows, width), wide)] * with_mixed,
        grid=(local * cuts,),
        after=after,
        name="experts", vmem=40,
        cost=(14 * rows * width * local * ff, 6 * local * width * ff + 8 * rows * width),
    )
    return list(outs[mixed_out : mixed_out + pieces]), list(outs[:mixed_out]), list(outs[mixed_out + pieces :])


def d_act_body(pieces, *refs):
    up_refs = refs[:pieces]
    down_ref, out_ref, ups_s, sems = refs[pieces:]

    @pl.when(pl.program_id(0) == 0)
    def _():
        copies, start = [], 0
        for i, ref in enumerate(up_refs):
            size = ref.shape[0]
            copies.append(
                pltpu.make_async_copy(
                    ref.at[:, pl.ds(0, ups_s.shape[1])], ups_s.at[pl.ds(start, size), :], sems.at[i]
                )
            )
            start += size
        for copy in copies:
            copy.start()
        wait_all(copies)

    out_ref[...] = dot(ups_s[...], down_ref[0], NT).astype(low)


def d_act_block(ups_list, w_down, after=()):
    local, ff, width = w_down.shape
    rows = sum(ups.shape[0] for ups in ups_list)
    return call(
        functools.partial(d_act_body, len(ups_list)),
        (*ups_list, w_down),
        [ANY] * len(ups_list) + [pl.BlockSpec((1, ff, width), lambda e: (e, 0, 0))],
        pl.BlockSpec((rows, ff), lambda e: (0, e)),
        Shape((rows, local * ff), low),
        [pltpu.VMEM((rows, width), low), pltpu.SemaphoreType.DMA((len(ups_list),))],
        grid=(local,),
        after=after,
        name="d_act", vmem=20,
        cost=(5e8, 1e6),
    )


def mixed_body(pieces, hidden_ref, down_ref, *refs):
    outs, total_s = refs[:pieces], refs[pieces]
    step = pl.program_id(0)
    product = dot(hidden_ref[...], down_ref[0], NN)

    @pl.when(step == 0)
    def _():
        total_s[...] = product

    @pl.when(step == pl.num_programs(0) - 1)
    def _():
        total = product if pl.num_programs(0) == 1 else total_s[...] + product
        start = 0
        for ref in outs:
            ref[...] = total[start : start + ref.shape[0]].astype(low)
            start += ref.shape[0]


def mixed_block(hidden, w_down, sizes, after=()):
    local, ff, width = w_down.shape
    rows = sum(sizes)
    return call(
        functools.partial(mixed_body, len(sizes)),
        (hidden, w_down),
        [pl.BlockSpec((rows, ff), lambda e: (0, e)), pl.BlockSpec((1, ff, width), lambda e: (e, 0, 0))],
        [pl.BlockSpec((size, width), lambda e: (0, 0)) for size in sizes],
        [Shape((size, width), low) for size in sizes],
        [pltpu.VMEM((rows, width), wide)],
        grid=(local,),
        after=after,
        name="mixed", vmem=24,
        cost=(3 * rows * width * local * ff, 5e6),
    )


def outer_body(pieces, seconds, split, place_ref, *refs):
    first_refs = refs[:pieces]
    second_refs = refs[pieces : pieces + seconds]
    mine_ref, other_ref, first_s, second_s, first_sems, second_sems = refs[pieces + seconds :]
    core = place_ref[0] % 2
    step = pl.program_id(0)
    cut = first_s.shape[2]
    width = second_s.shape[1]

    def load(at, slot):
        copies, start = [], 0
        for i, ref in enumerate(first_refs):
            size = ref.shape[0]
            copies.append(
                pltpu.make_async_copy(
                    ref.at[:, pl.ds(pl.multiple_of(at * cut, cut), cut)],
                    first_s.at[slot, pl.ds(start, size), :],
                    first_sems.at[slot, i],
                )
            )
            start += size
        return copies

    slot = step % 2

    @pl.when(step == 0)
    def _():
        for copy in load(0, 0):
            copy.start()
        copies, start = [], 0
        for i, ref in enumerate(second_refs):
            size = ref.shape[0]
            copies.append(
                pltpu.make_async_copy(
                    ref.at[:, pl.ds(0, width)], second_s.at[pl.ds(start, size), :], second_sems.at[i]
                )
            )
            start += size
        for copy in copies:
            copy.start()
        wait_all(copies)

    @pl.when(step + 1 < pl.num_programs(0))
    def _():
        for copy in load(step + 1, 1 - slot):
            copy.start()

    wait_all(load(step, slot))
    product = dot(first_s[slot], second_s[...], TN).astype(low)
    if split == 1:

        @pl.when(step == core)
        def _():
            mine_ref[...] = product

        @pl.when(step != core)
        def _():
            other_ref[...] = product
    else:
        first, last = product[:, : width // 2], product[:, width // 2 :]
        mine_ref[...] = jnp.where(core == 0, first, last)
        other_ref[...] = jnp.where(core == 0, last, first)


def outer_products(place, first, second, first_width, second_width, split, after=()):
    cut = 512
    steps = first_width // cut
    rows = sum(piece.shape[0] for piece in first)
    if split == 1:
        out_shape = Shape((cut, second_width), low)
        out_spec = pl.BlockSpec((cut, second_width), lambda i: (0, 0))
    else:
        out_shape = Shape((first_width, second_width // 2), low)
        out_spec = pl.BlockSpec((cut, second_width // 2), lambda i: (i, 0))
    return call(
        functools.partial(outer_body, len(first), len(second), split),
        (place, *first, *second),
        [SMEM] + [ANY] * (len(first) + len(second)),
        [out_spec] * 2,
        [out_shape] * 2,
        [
            pltpu.VMEM((2, rows, cut), low),
            pltpu.VMEM((rows, second_width), low),
            pltpu.SemaphoreType.DMA((2, len(first))),
            pltpu.SemaphoreType.DMA((len(second),)),
        ],
        grid=(steps,),
        after=after,
        name="outer_products", vmem=24 if rows <= 4096 else 58,
        cost=(3.5 * rows * first_width * second_width, 12e6),
    )


def ring_parts_of(count, ids_ref, flat_s, outs):
    part = flat_s.shape[0] // count
    for o, ref in enumerate(outs):
        size = ref.shape[0]
        if o < count // 2:
            at = ids_ref[o] * part
        elif o > count // 2 + 1:
            at = ids_ref[o - 1] * part
        else:
            at = ids_ref[count // 2] * part + (o - count // 2) * size
        ref[...] = flat_s[pl.ds(pl.multiple_of(at, size), size), :]


def ring_part_sizes(count, flat):
    part = flat // count
    return [part] * (count // 2) + [part // 2] * 2 + [part] * (count // 2 - 1)


def ring_part_list(count, outs):
    half = count // 2
    return list(outs[:half]) + [tuple(outs[half : half + 2])] + list(outs[half + 2 :])


def head_grads_body(count, place_ref, ids_ref, *refs):
    rows_refs, d_refs = refs[:4], refs[4:8]
    att_ref, d_lin_ref, wq_ref, wk_ref, wv_ref, gain_ref = refs[8:14]
    outs = refs[14 : 14 + count + 1]
    gain_out, rows_s, d_s, flat_s, sems, d_sems = refs[15 + count :]
    copies = load_blocks(place_ref[0], rows_refs, rows_s, sems)
    d_copies = load_blocks(place_ref[0], d_refs, d_s, d_sems)
    wait_all(copies)
    q_width, kv_width = wq_ref.shape[1], wk_ref.shape[1]
    lin_width = d_lin_ref.shape[1]
    width = rows_s.shape[1]
    for at in range(0, width, 512):
        here = pl.ds(at, 512)
        grads = dot(rows_s[:, here], d_lin_ref[...], TN)
        for c in range(0, lin_width, LANES):
            row = c // LANES * width + at
            flat_s[row : row + 512, :] = grads[:, c : c + LANES].astype(low)
        inner = jnp.sum(wq_ref[here, :].astype(wide) * grads[:, :q_width], axis=1, keepdims=True)
        inner += jnp.sum(
            wk_ref[here, :].astype(wide) * grads[:, q_width : q_width + kv_width], axis=1, keepdims=True
        )
        inner += jnp.sum(
            wv_ref[here, :].astype(wide) * grads[:, q_width + kv_width :], axis=1, keepdims=True
        )
        inner = jnp.transpose(jnp.broadcast_to(inner, (512, LANES)))[:1]
        gain_out[:, here] = inner / gain_ref[:, here]
    wait_all(d_copies)
    base = lin_width // LANES * width
    for at in range(0, width, 512):
        grads = dot(att_ref[...], d_s[:, at : at + 512], TN).astype(low)
        for c in range(0, 512, LANES):
            row = base + (at + c) // LANES * q_width
            flat_s[row : row + q_width, :] = grads[:, c : c + LANES]
    ring_parts_of(count, ids_ref, flat_s, outs)


def head_grads(place, ids, rows_blocks, d_blocks, att, d_lin, wq, wk, wv, gain, after=()):
    count = lax.axis_size("dp")
    rows, width = rows_blocks[0].shape
    length, lin_width = d_lin.shape
    flat = width * (lin_width + att.shape[1]) // LANES
    outs = call(
        functools.partial(head_grads_body, count),
        (place, ids, *rows_blocks, *d_blocks, att, d_lin, wq, wk, wv, gain),
        [SMEM, SMEM] + [ANY] * 8 + [VMEM] * 6,
        [VMEM] * (count + 2),
        [Shape((size, LANES), low) for size in ring_part_sizes(count, flat)] + [Shape((1, width), wide)],
        [
            pltpu.VMEM((length, width), low),
            pltpu.VMEM((length, width), low),
            pltpu.VMEM((flat, LANES), low),
            pltpu.SemaphoreType.DMA((4,)),
            pltpu.SemaphoreType.DMA((4,)),
        ],
        after=after,
        name="head_grads", vmem=30,
        cost=(8e-6 * 1.1e15, 12e6),
    )
    return ring_part_list(count, outs[:-1]), outs[-1]


def ring_sum_body(own_ref, up_ref, down_ref, out_ref):
    out_ref[...] = (
        own_ref[...].astype(wide) + up_ref[...].astype(wide) + down_ref[...].astype(wide)
    ).astype(low)


def ring_total(parts, before, last):
    half = len(parts) // 2
    up, down = ring_scatter(
        [parts[len(parts) - 1 - i] for i in range(half - 1)],
        [parts[1 + i] for i in range(half - 1)],
        parts[half],
        before,
    )
    total = call(
        ring_sum_body, (parts[0], up, down), [VMEM] * 3, VMEM, Shape(parts[0].shape, low),
        after=last, name="ring_sum", cost=(1e8, 1e6),
    )
    below, above, far = ring_gather(total)
    return [total] + above + list(far) + below[::-1]


def head_place_body(count, ids_ref, *refs):
    blocks = refs[: count + 1]
    grads, flat_s = refs[count + 1 : -1], refs[-1]
    part = flat_s.shape[0] // count
    for o, ref in enumerate(blocks):
        size = ref.shape[0]
        if o < count // 2:
            at = ids_ref[o] * part
        elif o > count // 2 + 1:
            at = ids_ref[o - 1] * part
        else:
            at = ids_ref[count // 2] * part + (o - count // 2) * size
        flat_s[pl.ds(pl.multiple_of(at, size), size), :] = ref[...]
    row = 0
    for ref in grads:
        rows, columns = ref.shape
        for c in range(0, columns, LANES):
            ref[:, c : c + LANES] = flat_s[row : row + rows, :].astype(wide)
            row += rows


def head_place(ids, blocks, shapes):
    count = lax.axis_size("dp")
    flat = sum(rows * columns for rows, columns in shapes) // LANES
    return call(
        functools.partial(head_place_body, count),
        (ids, *blocks),
        [SMEM] + [VMEM] * (count + 1),
        [VMEM] * len(shapes),
        [Shape(shape, wide) for shape in shapes],
        [pltpu.VMEM((flat, LANES), low)],
        name="head_place", vmem=24,
        cost=(1e9, 6e6),
    )


def add_body(first_ref, second_ref, out_ref):
    out_ref[...] = (first_ref[...].astype(wide) + second_ref[...].astype(wide)).astype(low)


def add_rows(first, second, after=()):
    return call(
        add_body, (first, second), [VMEM] * 2, VMEM, Shape(first.shape, low), after=after,
        name="add_rows", cost=(1e8, 3e6),
    )


def place_quarters_body(place_ref, *refs):
    del place_ref
    pieces, out_ref = refs[:4], refs[-1]
    step = pl.program_id(0)
    for i, ref in enumerate(pieces):

        @pl.when(step == i)
        def _():
            out_ref[0] = ref[...].astype(wide)


def place_quarters(place, pieces, after=()):
    rows, columns = pieces[0].shape
    count = len(after)
    fixed = pl.BlockSpec((rows, columns), lambda i, place_ref: (0, 0))
    out = pl.BlockSpec(
        (1, rows, columns),
        lambda i, place_ref: (i // 2 ^ place_ref[0] % 2, i % 2 ^ place_ref[0] // 2, 0),
    )
    return pl.pallas_call(
        place_quarters_body,
        grid_spec=pltpu.PrefetchScalarGridSpec(
            num_scalar_prefetch=1, grid=(4,), in_specs=[fixed] * 4 + [ANY] * count, out_specs=out
        ),
        out_shape=Shape((2, 2 * rows, columns), wide),
        compiler_params=pltpu.CompilerParams(vmem_limit_bytes=16 * MEGABYTE),
        cost_estimate=pl.CostEstimate(flops=10**8, bytes_accessed=10**7, transcendentals=0),
        name="place_quarters",
    )(place, *pieces, *after)


def lin_back_body(place_ref, d_lin_ref, wq_ref, wk_ref, wv_ref, mine_ref, other_ref):
    rows = mine_ref.shape[1]
    core = place_ref[0] % 2
    q_width, kv_width = wq_ref.shape[1], wk_ref.shape[1]
    for x in range(2):
        for ref, c in ((other_ref, 1 - core), (mine_ref, core)):
            at = pl.ds(pl.multiple_of((2 * x + c) * rows, rows), rows)
            total = dot(d_lin_ref[at, :q_width], wq_ref[...], NT)
            total += dot(d_lin_ref[at, q_width : q_width + kv_width], wk_ref[...], NT)
            total += dot(d_lin_ref[at, q_width + kv_width :], wv_ref[...], NT)
            ref[x] = total.astype(low)


def lin_back(place, d_lin, wq, wk, wv, after):
    rows, width = d_lin.shape[0] // 4, wq.shape[0]
    return call(
        lin_back_body,
        (place, d_lin, wq, wk, wv),
        [SMEM] + [VMEM] * 4,
        [VMEM] * 2,
        [Shape((2, rows, width), low)] * 2,
        after=after,
        name="lin_back", vmem=20,
        cost=(4e-6 * 1.1e15, 9e6),
    )


def first_norm_body(tokens_ref, gain_ref, normed_ref):
    inputs = tokens_ref[...].astype(wide)
    inverse = lax.rsqrt(jnp.mean(inputs * inputs, axis=1, keepdims=True) + EPS)
    normed_ref[...] = (inputs * inverse * gain_ref[...]).astype(low)


def second_norm_body(tokens_ref, kept_ref, got_ref, gain_ref, residual_ref, normed_ref):
    residual = tokens_ref[...].astype(wide) + (kept_ref[...].astype(wide) + got_ref[...].astype(wide))
    inverse = lax.rsqrt(jnp.mean(residual * residual, axis=1, keepdims=True) + EPS)
    residual_ref[...] = residual
    normed_ref[...] = (residual * inverse * gain_ref[...]).astype(low)


def middle_body(
    own_ref, up_ref, down_ref, residual_ref, normed_ref, ups_ref, router_ref, gain_ref, first_ref, second_ref,
    d_residual_ref, d_low_ref, gain_out, router_out, first_out, second_out,
):
    del first_ref, second_ref, first_out, second_out
    width = residual_ref.shape[1]
    total = own_ref[...].astype(wide) + up_ref[...].astype(wide) + down_ref[...].astype(wide)
    d_gates = total[:, width:]
    d_gates = d_gates + pltpu.roll(d_gates, LANES // 2, 1)
    lane = lax.broadcasted_iota(jnp.int32, d_gates.shape, 1)
    chosen = ups_ref[:, width:] > 0.0
    normed = normed_ref[...]
    logits = jnp.where(chosen, dot(normed, router_ref[...], NN), NEG)
    largest = jnp.max(logits, axis=1, keepdims=True)
    shifted = jnp.where(chosen, jnp.exp(logits - largest), 0.0)
    gates = shifted / jnp.sum(shifted, axis=1, keepdims=True)
    inner = jnp.sum(gates * d_gates, axis=1, keepdims=True)
    d_logits = (gates * (d_gates - inner)).astype(low)
    router_part = dot(d_logits, normed, TN)[: router_out.shape[0]]
    d_normed = total[:, :width] + dot(d_logits, router_ref[...], NT)
    residual = residual_ref[...]
    inverse = lax.rsqrt(jnp.mean(residual * residual, axis=1, keepdims=True) + EPS)
    scaled = d_normed * gain_ref[...]
    mean = jnp.mean(scaled * residual, axis=1, keepdims=True)
    upstream = ups_ref[:, :width].astype(wide)
    d_residual = upstream + inverse * scaled - residual * (inverse * inverse * inverse * mean)
    gain_part = jnp.sum(d_normed * residual * inverse, axis=0, keepdims=True)

    @pl.when(pl.program_id(0) == 0)
    def _():
        gain_out[...] = gain_part
        router_out[...] = router_part

    @pl.when(pl.program_id(0) > 0)
    def _():
        gain_out[...] += gain_part
        router_out[...] += router_part

    d_residual_ref[...] = d_residual
    d_low_ref[...] = d_residual.astype(low)


def last_body(tokens_ref, kept_ref, got_ref, d_residual_ref, gain_ref, out_ref):
    inputs = tokens_ref[...].astype(wide)
    inverse = lax.rsqrt(jnp.mean(inputs * inputs, axis=1, keepdims=True) + EPS)
    scaled = (kept_ref[...].astype(wide) + got_ref[...].astype(wide)) * gain_ref[...]
    mean = jnp.mean(scaled * inputs, axis=1, keepdims=True)
    d_inputs = inverse * scaled - inputs * (inverse * inverse * inverse * mean)
    out_ref[...] = (d_inputs + d_residual_ref[...]).astype(low)


def on_device(
    tokens,
    gain_attn,
    query_weight,
    key_weight,
    value_weight,
    w_output,
    gain_ffn,
    w_router,
    w_gate,
    w_up,
    w_down,
    segments,
    routes,
    cotangent,
):
    rows_dev, width = tokens.shape
    data_count = lax.axis_size("dp")
    half_count = data_count // 2
    local_experts, _, ff = w_gate.shape
    expert_count = local_experts * data_count
    q_width, kv_width = query_weight.shape[1], key_weight.shape[1]
    place = lax.axis_index("tensor").astype(jnp.int32).reshape(1)
    ids = ring_places()
    cos, sin = rope_tables(segments.shape[1])
    gain_one, gain_two = gain_attn.reshape(1, width), gain_ffn.reshape(1, width)
    lanes = jnp.arange(LANES, dtype=jnp.int32)
    own_experts = lax.axis_index("dp") * local_experts + jnp.arange(local_experts, dtype=jnp.int32)
    sel = (own_experts[:, None] == lanes[None, :]).astype(wide)
    router = jnp.pad(w_router, ((0, 0), (0, LANES - expert_count)))
    chosen = jnp.any(routes[:, :, None] == lanes[None, None, :], axis=1).astype(low)
    ups = jnp.concatenate([cotangent, chosen], axis=1)

    half_rows = rows_dev // 2
    row_spec = pl.BlockSpec((half_rows, width), lambda i: (i, 0))
    wide_spec = pl.BlockSpec((half_rows, width + LANES), lambda i: (i, 0))
    gain_spec = pl.BlockSpec((1, width), lambda i: (0, 0))
    normed_one = call(
        first_norm_body, (tokens, gain_one), [row_spec, gain_spec], row_spec,
        Shape((rows_dev, width), low), grid=(2,), name="first_norm", cost=(1e9, 2e6),
    )
    d_acts = [d_act_block((ups,), w_down)]

    def early_acts(below, above):
        for pair in list(zip(below, above))[: half_count - 2]:
            d_acts.append(d_act_block(pair, w_down))
        below[-1], above[-1] = hold((below[-1], above[-1]), d_acts[1:])
        return below[-1], above[-1]

    ups_below, ups_above, ups_far = ring_gather(ups, early_acts)
    rows_blocks = tensor_blocks(normed_one)
    ups_groups = [(ups,)] + list(zip(ups_below, ups_above)) + [ups_far]
    d_acts += [d_act_block(group, w_down) for group in ups_groups[-2:]]
    att, q, k, v, lse = attend(
        place, rows_blocks, query_weight, key_weight, value_weight, cos, sin, segments,
        after=(ups_below[0], ups_above[0], d_acts[0], router),
    )
    other = branch_half(place, att, w_output, True, after=(ups_below[1], ups_above[1]))
    mine = branch_half(place, att, w_output, False)
    kept, got = tensor_scatter(place, mine, other, after=())
    residual, normed_two = call(
        second_norm_body, (tokens, kept, got, gain_two), [row_spec] * 3 + [gain_spec], [row_spec] * 2,
        [Shape((rows_dev, width), wide), Shape((rows_dev, width), low)],
        after=(ups_below[-1], ups_above[-1]), grid=(2,), name="second_norm", cost=(1e9, 4e6),
    )
    rows_below, rows_above, rows_far = ring_gather(normed_two)
    rows_groups = [(normed_two,)] + list(zip(rows_below, rows_above)) + [rows_far]
    done = []
    for index, (rows, up) in enumerate(zip(rows_groups, ups_groups)):
        after = () if not done else (done[-1][2][0],)
        if len(done) in (1, 2):
            after += (d_acts[len(done) - 3],)
        done.append(
            expert_block(
                rows, up, d_acts[index], sel, router, w_gate, w_up, w_down,
                False, after,
            )
        )
    rows_all = [piece for rows in rows_groups for piece in rows]
    ups_all = [piece for up in ups_groups for piece in up]
    hidden_all, d_gate_all, d_up_all = ([outs[2][i] for outs in done] for i in range(3))
    inner = local_experts * ff
    split_rows = {"down": ff // 2, "gate": width // 2, "up": width // 2}
    grads = {
        "down": outer_products(place, hidden_all, ups_all, inner, width, 1),
        "gate": outer_products(place, rows_all, d_gate_all, width, inner, 2),
        "up": outer_products(place, rows_all, d_up_all, width, inner, 2),
    }
    names = ("down", "gate", "up")
    halves, quarters = {}, {}

    def quarter(name):
        quarters[name] = add_rows(halves[name][0], swap(halves[name][1], "tensor", 2))
        return quarters[name]

    def before(index):
        if index > 2:
            return (), ()
        after = (halves[names[index - 1]][0],) if index else ()
        if index == 2:
            after += (quarter("down"),)
        return after, (grads[names[index]][1],)

    def then(index, _, held):
        if index > 2:
            return
        name = names[index]
        mine, other = (array.reshape(2, split_rows[name], -1) for array in (grads[name][0], held[0]))
        halves[name] = split_add(place, mine, swap(other, "tensor", 1))

    d_rows_up, d_rows_down = ring_scatter(
        [outs[0][0] for outs in done[1:-1]], [outs[0][1] for outs in done[1:-1]], done[-1][0], before, then
    )
    late = [
        mixed_block(done[i][2][0], w_down, [rows.shape[0] for rows in rows_groups[i]], (halves["up"][0],))
        for i in (-2, -1)
    ]
    early = [
        mixed_block(outs[2][0], w_down, [rows.shape[0] for rows in group])
        for outs, group in zip(done[:-2], rows_groups)
    ]
    mixed_parts = early + late
    far_mixed = [None, None]
    d_residual, d_low, gain_ffn_part, router_part, far_mixed[0], far_mixed[1] = call(
        middle_body,
        (done[0][0][0], d_rows_up, d_rows_down, residual, normed_two, ups, router, gain_two, *late[1]),
        [wide_spec] * 3
        + [row_spec] * 2
        + [wide_spec, pl.BlockSpec((width, LANES), lambda i: (0, 0)), gain_spec]
        + [ANY] * 2,
        [row_spec] * 2 + [gain_spec, pl.BlockSpec((expert_count, width), lambda i: (0, 0))] + [ANY] * 2,
        [
            Shape((rows_dev, width), wide),
            Shape((rows_dev, width), low),
            Shape((1, width), wide),
            Shape((expert_count, width), wide),
        ]
        + [Shape(part.shape, low) for part in late[1]],
        grid=(2,),
        after=(late[0][0], quarter("gate")),
        name="middle", vmem=16, cost=(4e-6 * 1.1e15, 4e6), alias={8: 4, 9: 5},
    )
    d_blocks = tensor_blocks(d_low)
    marks = []
    mixed_up, mixed_down = ring_scatter(
        [parts[0] for parts in mixed_parts[1:-1]], [parts[1] for parts in mixed_parts[1:-1]], far_mixed,
        then=lambda index, up, held: marks.append(up),
    )
    quarter("up")
    pieces = {}
    for name in names:
        second = swap(quarters[name], "tensor", 2)
        pieces[name] = (
            quarters[name], second, swap(quarters[name], "tensor", 1), swap(second, "tensor", 1)
        )
    d_lin = attend_back(
        place, d_blocks, w_output, att, q, k, v, lse, cos, sin, segments,
        after=(quarters["up"], marks[0]),
    )
    parts, gain_attn_part = head_grads(
        place, ids, rows_blocks, d_blocks, att, d_lin, query_weight, key_weight, value_weight, gain_one,
        after=(pieces["down"][1],),
    )
    mine, other = lin_back(place, d_lin, query_weight, key_weight, value_weight, after=(marks[1], parts[0]))
    kept, got = tensor_scatter(place, mine, other, after=())
    grad_gate, grad_up, grad_down = (place_quarters(place, pieces[name]) for name in ("gate", "up", "down"))

    def before_total(index):
        ties = ((pieces["gate"][1], mine), (marks[2], kept, grad_down), (grad_gate,))
        return (ties[index] if index < 3 else ()), ()

    blocks = ring_total(parts, before_total, (grad_up,))
    mixed = (
        residual + mixed_parts[0][0].astype(wide) + mixed_up.astype(wide) + mixed_down.astype(wide)
    ).astype(low)
    grad_tokens = call(
        last_body, (tokens, kept, got, d_residual, gain_one), [row_spec] * 4 + [gain_spec], row_spec,
        Shape((rows_dev, width), low), grid=(2,), name="last", cost=(1e9, 4e6),
    )
    grad_q, grad_k, grad_v, grad_o = head_place(
        ids, blocks, [(width, q_width), (width, kv_width), (width, kv_width), (q_width, width)]
    )
    small = jnp.concatenate([gain_ffn_part, gain_attn_part, router_part], axis=0)
    small = cube_sum(small, ("tensor", "dp"))
    return (
        mixed,
        grad_tokens,
        small[1],
        grad_q,
        grad_k,
        grad_v,
        grad_o,
        small[0],
        small[2:].T,
        grad_gate,
        grad_up,
        grad_down,
    )


def solution(mesh):
    in_specs = (
        P(("dp", "tensor"), None),
        P(),
        P(None, "tensor"),
        P(None, "tensor"),
        P(None, "tensor"),
        P("tensor", None),
        P(),
        P(),
        P("dp", None, None),
        P("dp", None, None),
        P("dp", None, None),
        P("dp", None),
        P(("dp", "tensor"), None),
        P(("dp", "tensor"), None),
    )
    out_specs = (
        P(("dp", "tensor"), None),
        P(("dp", "tensor"), None),
        P(),
        P(None, "tensor"),
        P(None, "tensor"),
        P(None, "tensor"),
        P("tensor", None),
        P(),
        P(),
        P("dp", None, None),
        P("dp", None, None),
        P("dp", None, None),
    )
    return jax.shard_map(
        on_device, mesh=mesh, in_specs=in_specs, out_specs=out_specs, check_vma=False
    )
```

```python
import functools
import math

import jax
import jax.numpy as jnp
import numpy as np
from jax import lax
from jax.experimental import pallas as pl
from jax.experimental.pallas import tpu as pltpu
from jax.sharding import PartitionSpec as P

HEAD_WIDTH = 64
EPS = 1e-06
ROPE_BASE = 10000.0
NEG = -1e30
LANES = 128
BLOCK = 256
REACH = 512
MEGABYTE = 1024 * 1024
low = jnp.bfloat16
wide = jnp.float32
NN = (((1,), (0,)), ((), ()))
NT = (((1,), (1,)), ((), ()))
TN = (((0,), (0,)), ((), ()))
dot = functools.partial(lax.dot_general, preferred_element_type=jnp.float32)
Shape = jax.ShapeDtypeStruct
ANY = pl.BlockSpec(memory_space=pl.ANY)
VMEM = pl.BlockSpec(memory_space=pltpu.VMEM)
SMEM = pl.BlockSpec(memory_space=pltpu.SMEM)


def rope_tables(length):
    half = HEAD_WIDTH // 2
    freq = np.exp(-(np.arange(half, dtype=np.float32) * (2.0 / HEAD_WIDTH)) * math.log(ROPE_BASE))
    angle = np.arange(length, dtype=np.float32)[:, None] * freq.astype(np.float32)[None, :]
    cos, sin = np.cos(angle), np.sin(angle)
    cos = np.concatenate([cos] * 4, axis=1).astype(np.float32)
    sin = np.concatenate([-sin, sin, -sin, sin], axis=1).astype(np.float32)
    return jnp.asarray(cos), jnp.asarray(sin)


def ring_order(count):
    return list(range(0, count, 2)) + list(range(count - 1, 0, -2))


def ring_send(array, step):
    count = lax.axis_size("dp")
    order = ring_order(count)
    return lax.ppermute(
        array, "dp", [(order[i], order[(i + step) % count]) for i in range(count)]
    )


def ring_places():
    count = lax.axis_size("dp")
    order = ring_order(count)
    table = [[(order.index(i) + o) % count for o in range(count)] for i in range(count)]
    table = jnp.asarray(np.asarray(table, np.int32))
    return lax.dynamic_index_in_dim(table, lax.axis_index("dp"), 0, keepdims=False)


def ring_gather(array, last=None):
    count = lax.axis_size("dp")
    half = array.shape[0] // 2
    below, above = [], []
    up, down = array, array
    for _ in range(count // 2 - 1):
        up = ring_send(up, 1)
        down = ring_send(down, -1)
        below.append(up)
        above.append(down)
    if last is not None:
        up, down = last(below, above)
    top = ring_send(up[:half], 1)
    bottom = ring_send(down[half:], -1)
    return below, above, (top, bottom)


def swap(array, axis, mask):
    return lax.ppermute(array, axis, [(i, i ^ mask) for i in range(lax.axis_size(axis))])


def tensor_blocks(array):
    far = swap(array, "tensor", 2)
    return array, swap(array, "tensor", 1), far, swap(far, "tensor", 1)


class Token:
    def __init__(self, array):
        self.array = array


TOKEN = (8, LANES)


def call(body, operands, in_specs, out_specs, out_shape, scratch=(), grid=None, after=(), name=None, cost=None, alias=None, vmem=10):
    count = len(after)
    position = len(operands)
    single = not isinstance(out_shape, (list, tuple))
    shapes = [out_shape] if single else list(out_shape)
    specs = [out_specs] if single else list(out_specs)

    def kernel(*refs):
        outs = position + count + len(shapes)
        body(*refs[:position], *refs[position + count : outs], *refs[outs + 1 :])

    extra = {} if grid is None else {"grid": grid}
    if cost is not None:
        extra["cost_estimate"] = pl.CostEstimate(
            flops=int(cost[0]), bytes_accessed=int(cost[1]), transcendentals=0
        )
    if alias is not None:
        extra["input_output_aliases"] = alias
    waits = [entry.array if isinstance(entry, Token) else entry for entry in after]
    results = pl.pallas_call(
        kernel,
        in_specs=list(in_specs) + [ANY] * count,
        out_specs=specs + [VMEM],
        out_shape=shapes + [pltpu.VMEM(TOKEN, wide)],
        scratch_shapes=list(scratch),
        compiler_params=pltpu.CompilerParams(vmem_limit_bytes=vmem * MEGABYTE),
        name=name,
        **extra,
    )(*operands, *waits)
    token = Token(results[-1])
    return (results[0] if single else list(results[:-1])), token


def ring_add_body(first, held, up_ref, part_up_ref, down_ref, part_down_ref, *refs):
    up_out, down_out = refs[held : held + 2]

    def add(got_ref, part_ref, out_ref):
        out_ref[...] = (got_ref[...].astype(wide) + part_ref[...].astype(wide)).astype(low)

    def keep(part_ref, out_ref):
        out_ref[...] = part_ref[...]

    if not first:
        add(up_ref, part_up_ref, up_out)
        add(down_ref, part_down_ref, down_out)
        return

    @pl.when(pl.program_id(0) == 0)
    def _():
        add(up_ref, part_up_ref, up_out)
        keep(part_down_ref, down_out)

    @pl.when(pl.program_id(0) == 1)
    def _():
        keep(part_up_ref, up_out)
        add(down_ref, part_down_ref, down_out)


def ring_add(first, up, part_up, down, part_down, after, held):
    rows, width = part_up.shape
    part = pl.BlockSpec((rows // 2, width), lambda i: (i, 0))
    got = pl.BlockSpec((rows // 2, width), lambda i: (0, 0)) if first else part
    return call(
        functools.partial(ring_add_body, first, len(held)),
        (up, part_up, down, part_down, *held),
        [got, part, got, part] + [ANY] * len(held),
        [part, part] + [ANY] * len(held),
        [Shape((rows, width), low)] * 2 + [Shape(array.shape, array.dtype) for array in held],
        grid=(2,),
        after=after,
        name="ring_add",
        cost=(1e8, 4e6),
        alias={4 + i: 2 + i for i in range(len(held))},
    )


def hold_body(*refs):
    del refs


def hold(arrays, after):
    return call(
        hold_body, arrays, [ANY] * len(arrays), [ANY] * len(arrays),
        [Shape(array.shape, array.dtype) for array in arrays], after=after, name="hold", cost=(1e6, 1e5),
        alias={i: i for i in range(len(arrays))},
    )[0]


def ring_scatter(below, above, opposite, before=None, then=None):
    up = ring_send(opposite[0], 1)
    down = ring_send(opposite[1], -1)
    for index, k in enumerate(range(len(above), 0, -1)):
        after, held = before(index) if before else ((), ())
        (up, down, *held), token = ring_add(index == 0, up, above[k - 1], down, below[k - 1], after, held)
        if then:
            then(index, token, held)
        up = ring_send(up, 1)
        down = ring_send(down, -1)
    return up, down


def half_turn(array):
    width = array.shape[-1]
    half = HEAD_WIDTH // 2
    lane = lax.broadcasted_iota(jnp.int32, array.shape, 1)
    return jnp.where(
        lane % HEAD_WIDTH < half, pltpu.roll(array, width - half, 1), pltpu.roll(array, half, 1)
    )


def spread_heads(array):
    lane = lax.broadcasted_iota(jnp.int32, array.shape, 1)
    first = lane < HEAD_WIDTH
    other = pltpu.roll(array, HEAD_WIDTH, 1)
    zero = jnp.zeros_like(array)
    return [
        [jnp.where(first, array, zero), jnp.where(first, zero, other)],
        [jnp.where(first, other, zero), jnp.where(first, zero, array)],
    ]


def load_blocks(place, blocks, target, sems):
    rows = blocks[0].shape[0]
    copies = []
    for mask, block in enumerate(blocks):
        start = pl.multiple_of((place ^ mask) * rows, rows)
        copies.append(pltpu.make_async_copy(block, target.at[pl.ds(start, rows), :], sems.at[mask]))
    for copy in copies:
        copy.start()
    return copies


def fetch(pairs, sems):
    copies = [pltpu.make_async_copy(source, target, sems.at[i]) for i, (source, target) in enumerate(pairs)]
    for copy in copies:
        copy.start()
    return copies


def wait_all(copies):
    for copy in copies:
        copy.wait()


def column_of(row_ref, start, size):
    row = jnp.broadcast_to(row_ref[:, start : start + size].astype(wide), (LANES, size))
    return jnp.transpose(row)[:, :1].astype(jnp.int32)


def attend_body(
    place_ref, own, near, far, both, wq_any, wk_any, wv_any, cos_any, sin_any, row_ref,
    att_ref, q_ref, k_ref, v_ref, lse_ref, rows_s, wq_ref, wk_ref, wv_ref, cos_ref, sin_ref, kz_s, vz_s,
    sems, more_sems,
):
    place = place_ref[0]
    copies = load_blocks(place, (own, near, far, both), rows_s, sems)
    copies += fetch(
        ((wq_any, wq_ref), (cos_any, cos_ref), (sin_any, sin_ref), (wk_any, wk_ref), (wv_any, wv_ref)),
        more_sems,
    )
    wait_all(copies)
    length = rows_s.shape[0]
    pairs = wq_ref.shape[1] // LANES
    scale = HEAD_WIDTH**-0.5
    for start in range(0, length, BLOCK):
        at = pl.ds(start, BLOCK)
        rows = rows_s[at, :]
        cos, sin = cos_ref[at, :], sin_ref[at, :]
        query = dot(rows, wq_ref[...], NN)
        for j in range(pairs):
            part = query[:, j * LANES : (j + 1) * LANES]
            turned = (part * cos + half_turn(part) * sin).astype(low)
            q_ref[at, j * LANES : (j + 1) * LANES] = (turned.astype(wide) * scale).astype(low)
        key = dot(rows, wk_ref[...], NN)
        key = (key * cos + half_turn(key) * sin).astype(low)
        k_ref[at, :] = key
        value = dot(rows, wv_ref[...], NN).astype(low)
        v_ref[at, :] = value
        keys, values = spread_heads(key.astype(wide)), spread_heads(value.astype(wide))
        for g in range(2):
            for off in range(2):
                kz_s[2 * g + off, at, :] = keys[g][off].astype(low)
                vz_s[2 * g + off, at, :] = values[g][off].astype(low)
    lane = lax.broadcasted_iota(jnp.int32, (BLOCK, LANES), 1)
    for start in range(0, length, BLOCK):
        at = pl.ds(start, BLOCK)
        first = max(0, start - REACH)
        span = start + BLOCK - first
        keys_at = pl.ds(first, span)
        row_id = lax.broadcasted_iota(jnp.int32, (BLOCK, span), 0) + start
        col_id = lax.broadcasted_iota(jnp.int32, (BLOCK, span), 1) + first
        allowed = (column_of(row_ref, start, BLOCK) == row_ref[:, keys_at]) & (row_id >= col_id)
        bias = jnp.where(allowed, 0.0, NEG)
        stats = jnp.zeros((BLOCK, LANES), wide)
        for j in range(pairs):
            query = q_ref[at, j * LANES : (j + 1) * LANES]
            total = None
            for off in range(2):
                h = 2 * j + off
                slot = 2 * (h // pairs) + off
                scores = dot(query, kz_s[slot, keys_at, :], NT) + bias
                largest = jnp.max(scores, axis=1, keepdims=True)
                shifted = jnp.exp(scores - largest)
                summed = jnp.sum(shifted, axis=1, keepdims=True)
                probs = (shifted * (1.0 / summed)).astype(low)
                part = dot(probs, vz_s[slot, keys_at, :], NN)
                total = part if total is None else total + part
                stats = jnp.where(lane == h, largest + jnp.log(summed), stats)
            att_ref[at, j * LANES : (j + 1) * LANES] = total.astype(low)
        lse_ref[at, :] = stats


def attend(place, blocks, wq, wk, wv, cos, sin, segs, after):
    rows, width = blocks[0].shape
    length = 4 * rows
    return call(
        attend_body,
        (place, *blocks, wq, wk, wv, cos, sin, segs.reshape(1, length)),
        [SMEM] + [ANY] * 9 + [VMEM],
        [VMEM] * 5,
        [
            Shape((length, wq.shape[1]), low),
            Shape((length, wq.shape[1]), low),
            Shape((length, wk.shape[1]), low),
            Shape((length, wk.shape[1]), low),
            Shape((length, LANES), wide),
        ],
        [
            pltpu.VMEM((length, width), low),
            pltpu.VMEM(wq.shape, low),
            pltpu.VMEM(wk.shape, low),
            pltpu.VMEM(wv.shape, low),
            pltpu.VMEM(cos.shape, wide),
            pltpu.VMEM(sin.shape, wide),
            pltpu.VMEM((4, length, LANES), low),
            pltpu.VMEM((4, length, LANES), low),
            pltpu.SemaphoreType.DMA((4,)),
            pltpu.SemaphoreType.DMA((5,)),
        ],
        after=after,
        name="attend", vmem=62,
        cost=(15e-6 * 1.1e15, 12e6),
    )


def branch_body(flip, place_ref, att_ref, wo_ref, out_ref):
    rows = out_ref.shape[1]
    core = place_ref[0] % 2
    core = 1 - core if flip else core
    for x in range(2):
        at = pl.ds(pl.multiple_of((2 * x + core) * rows, rows), rows)
        out_ref[x] = dot(att_ref[at, :], wo_ref[...], NN).astype(low)


def branch_half(place, att, wo, flip, after=()):
    rows, width = att.shape[0] // 4, wo.shape[1]
    return call(
        functools.partial(branch_body, flip),
        (place, att, wo),
        [SMEM] + [VMEM] * 2,
        VMEM,
        Shape((2, rows, width), low),
        after=after,
        name="branch", vmem=14,
        cost=(2e9, 4e6),
    )[0]


def attend_back_body(
    place_ref, own, near, far, both, wo_any, att_any, q_any, k_any, v_any, lse_any, cos_any, sin_any, row_ref,
    d_lin_ref, rows_s, wo_ref, att_ref, q_ref, k_ref, v_ref, lse_ref, cos_ref, sin_ref,
    kz_s, kt_s, vz_s, d_att_s, d_key_s, d_value_s, d_query_s, sems, more_sems,
):
    place = place_ref[0]
    copies = load_blocks(place, (own, near, far, both), rows_s, sems)
    copies += fetch(
        ((wo_any, wo_ref), (att_any, att_ref), (lse_any, lse_ref), (k_any, k_ref), (v_any, v_ref)), more_sems
    )
    later = fetch(((q_any, q_ref), (cos_any, cos_ref), (sin_any, sin_ref)), more_sems.at[pl.ds(5, 3)])
    wait_all(copies)
    length, q_width = att_ref.shape
    heads = q_width // HEAD_WIDTH
    pairs = heads // 2
    scale = HEAD_WIDTH**-0.5
    lane = lax.broadcasted_iota(jnp.int32, (BLOCK, LANES), 1)
    stats_t = []
    for start in range(0, length, BLOCK):
        at = pl.ds(start, BLOCK)
        d_att = dot(rows_s[at, :], wo_ref[...], NT).astype(low)
        d_att_s[at, :] = d_att
        product = d_att.astype(wide) * att_ref[at, :].astype(wide)
        stats = lse_ref[at, :]
        for h in range(heads):
            part = product[:, (h // 2) * LANES : (h // 2 + 1) * LANES]
            mine = lane // HEAD_WIDTH == h % 2
            inner = jnp.sum(jnp.where(mine, part, 0.0), axis=1, keepdims=True)
            stats = jnp.where(lane == heads + h, inner, stats)
        stats_t.append(jnp.transpose(stats))
        keys, values = spread_heads(k_ref[at, :].astype(wide)), spread_heads(v_ref[at, :].astype(wide))
        for g in range(2):
            for off in range(2):
                kz_s[2 * g + off, at, :] = keys[g][off].astype(low)
                vz_s[2 * g + off, at, :] = values[g][off].astype(low)
                kt_s[2 * g + off, :, at] = jnp.transpose(keys[g][off]).astype(low)
    d_key_s[...] = jnp.zeros_like(d_key_s)
    d_value_s[...] = jnp.zeros_like(d_value_s)
    wait_all(later)
    for i, start in enumerate(range(0, length, BLOCK)):
        at = pl.ds(start, BLOCK)
        first = max(0, start - REACH)
        span = start + BLOCK - first
        keys_at = pl.ds(first, span)
        key_id = lax.broadcasted_iota(jnp.int32, (span, BLOCK), 0) + first
        query_id = lax.broadcasted_iota(jnp.int32, (span, BLOCK), 1) + start
        allowed = (column_of(row_ref, first, span) == row_ref[:, at]) & (query_id >= key_id)
        bias = jnp.where(allowed, 0.0, NEG)
        for j in range(pairs):
            query = q_ref[at, j * LANES : (j + 1) * LANES]
            d_att = d_att_s[at, j * LANES : (j + 1) * LANES]
            total = None
            for off in range(2):
                h = 2 * j + off
                slot = 2 * (h // pairs) + off
                scores = dot(kz_s[slot, keys_at, :], query, NT) + bias
                probs = jnp.exp(scores - stats_t[i][h : h + 1, :])
                d_probs = dot(vz_s[slot, keys_at, :], d_att, NT)
                d_scores = probs * (d_probs - stats_t[i][heads + h : heads + h + 1, :])
                d_scores = d_scores.astype(low)
                d_value_s[slot, keys_at, :] += dot(probs.astype(low), d_att, NN)
                d_key_s[slot, keys_at, :] += dot(d_scores, query, NN)
                part = dot(kt_s[slot, :, keys_at], d_scores, NN)
                total = part if total is None else total + part
            d_query_s[j * LANES : (j + 1) * LANES, at] = total
    for start in range(0, length, BLOCK):
        at = pl.ds(start, BLOCK)
        cos, sin = cos_ref[at, :], sin_ref[at, :]
        for j in range(pairs):
            part = jnp.transpose(d_query_s[j * LANES : (j + 1) * LANES, at]) * scale
            turned = part * cos - half_turn(part) * sin
            d_lin_ref[at, j * LANES : (j + 1) * LANES] = turned.astype(low)
        both_of = []
        for ref in (d_key_s, d_value_s):
            first_head = ref[0, at, :] + pltpu.roll(ref[1, at, :], HEAD_WIDTH, 1)
            second_head = ref[3, at, :] + pltpu.roll(ref[2, at, :], HEAD_WIDTH, 1)
            both_of.append(jnp.where(lane < HEAD_WIDTH, first_head, second_head))
        d_key, d_value = both_of
        d_lin_ref[at, q_width : q_width + LANES] = (d_key * cos - half_turn(d_key) * sin).astype(low)
        d_lin_ref[at, q_width + LANES :] = d_value.astype(low)


def attend_back(place, blocks, wo, att, q, k, v, lse, cos, sin, segs, after):
    rows, width = blocks[0].shape
    length, q_width = att.shape
    return call(
        attend_back_body,
        (place, *blocks, wo, att, q, k, v, lse, cos, sin, segs.reshape(1, length)),
        [SMEM] + [ANY] * 12 + [VMEM],
        VMEM,
        Shape((length, q_width + 2 * LANES), low),
        [
            pltpu.VMEM((length, width), low),
            pltpu.VMEM(wo.shape, low),
            pltpu.VMEM(att.shape, low),
            pltpu.VMEM(q.shape, low),
            pltpu.VMEM(k.shape, low),
            pltpu.VMEM(v.shape, low),
            pltpu.VMEM(lse.shape, wide),
            pltpu.VMEM(cos.shape, wide),
            pltpu.VMEM(sin.shape, wide),
            pltpu.VMEM((4, length, LANES), low),
            pltpu.VMEM((4, LANES, length), low),
            pltpu.VMEM((4, length, LANES), low),
            pltpu.VMEM((length, q_width), low),
            pltpu.VMEM((4, length, LANES), wide),
            pltpu.VMEM((4, length, LANES), wide),
            pltpu.VMEM((q_width, length), wide),
            pltpu.SemaphoreType.DMA((4,)),
            pltpu.SemaphoreType.DMA((8,)),
        ],
        after=after,
        name="attend_back", vmem=62,
        cost=(15e-6 * 1.1e15, 12e6),
    )


def split_add_body(place_ref, mine_ref, got_ref, kept_ref, sent_ref):
    far = place_ref[0] // 2
    kept_ref[...] = (mine_ref[far].astype(wide) + got_ref[far].astype(wide)).astype(low)
    sent_ref[...] = (mine_ref[1 - far].astype(wide) + got_ref[1 - far].astype(wide)).astype(low)


def tensor_scatter(place, mine, other, after):
    (kept, sent), token = split_add(place, mine, swap(other, "tensor", 1), after)
    return kept, swap(sent, "tensor", 2), token


def split_add(place, mine, got, after=()):
    rows, width = mine.shape[1:]
    return call(
        split_add_body,
        (place, mine, got),
        [SMEM] + [pl.BlockSpec((2, rows // 2, width), lambda i: (0, i, 0))] * 2,
        [pl.BlockSpec((rows // 2, width), lambda i: (i, 0))] * 2,
        [pltpu.HBM((rows, width), low)] * 2,
        grid=(2,),
        after=after,
        name="split_add", vmem=12,
        cost=(1e9, 6e6),
    )


def expert_body(pieces, cuts, local, with_mixed, *refs):
    rows_refs = refs[:pieces]
    up_refs = refs[pieces : 2 * pieces]
    d_act_ref, sel_ref, router_ref, gate_ref, up_w_ref = refs[2 * pieces : 2 * pieces + 5]
    outs = refs[2 * pieces + 5 :]
    if with_mixed:
        down_ref, outs = outs[0], outs[1:]
        mixed_refs, outs = outs[:pieces], outs[pieces:]
        mixed_s, outs = outs[-1], outs[:-1]
    d_rows_refs, outs = outs[:pieces], outs[pieces:]
    hidden_ref, d_gate_ref, d_up_ref, rows_s, mask_s, d_rows_s, gates_s, d_gates_s, sems = outs
    step = pl.program_id(0)
    width = rows_s.shape[1]

    @pl.when(step == 0)
    def _():
        copies, start = [], 0
        for i in range(pieces):
            at = pl.ds(start, rows_refs[i].shape[0])
            start += rows_refs[i].shape[0]
            copies.append(pltpu.make_async_copy(rows_refs[i], rows_s.at[at, :], sems.at[i]))
            copies.append(
                pltpu.make_async_copy(
                    up_refs[i].at[:, pl.ds(width, LANES)], mask_s.at[at, :], sems.at[pieces + i]
                )
            )
        for copy in copies:
            copy.start()
        wait_all(copies)
        chosen = mask_s[...] > 0.0
        logits = jnp.where(chosen, dot(rows_s[...], router_ref[...], NT), NEG)
        largest = jnp.max(logits, axis=1, keepdims=True)
        shifted = jnp.where(chosen, jnp.exp(logits - largest), 0.0)
        gates_s[...] = shifted / jnp.sum(shifted, axis=1, keepdims=True)
        d_gates_s[...] = jnp.zeros_like(d_gates_s)

    expert = step // cuts
    pick = sel_ref[0:1, :]
    for e in range(1, local):
        pick = jnp.where(expert == e, sel_ref[e : e + 1, :], pick)
    gate = jnp.sum(gates_s[...] * pick, axis=1, keepdims=True)
    rows = rows_s[...]
    gate_w, up_w = gate_ref[0], up_w_ref[0]
    gate_pre = dot(rows, gate_w, NN)
    up_pre = dot(rows, up_w, NN)
    d_act = d_act_ref[...].astype(wide)
    sig = 1.0 / (1.0 + jnp.exp(-gate_pre))
    act = gate_pre * sig
    hidden = act * up_pre
    d_gates_s[...] += jnp.sum(hidden * d_act, axis=1, keepdims=True) * pick
    hidden = (gate * hidden).astype(low)
    d_act = gate * d_act
    d_gate = (d_act * up_pre * sig * (1.0 + gate_pre * (1.0 - sig))).astype(low)
    d_up = (d_act * act).astype(low)
    hidden_ref[...] = hidden
    d_gate_ref[...] = d_gate
    d_up_ref[...] = d_up
    sums = [(d_rows_s, dot(d_gate, gate_w, NT) + dot(d_up, up_w, NT))]
    if with_mixed:
        sums.append((mixed_s, dot(hidden, down_ref[0], NN)))

    @pl.when(step == 0)
    def _():
        for ref, value in sums:
            ref[...] = value

    @pl.when(step > 0)
    def _():
        for ref, value in sums:
            ref[...] += value

    @pl.when(step == pl.num_programs(0) - 1)
    def _():
        lane = lax.broadcasted_iota(jnp.int32, d_gates_s.shape, 1)
        d_gates = d_gates_s[...]
        d_gates = jnp.where(lane < LANES // 2, d_gates, pltpu.roll(d_gates, LANES // 2, 1))
        rounded = d_gates.astype(low).astype(wide)
        d_gates = jnp.where(lane < LANES // 2, rounded, d_gates - rounded).astype(low)
        start = 0
        for i, d_rows_ref in enumerate(d_rows_refs):
            size = d_rows_ref.shape[0]
            d_rows_ref[:, :width] = d_rows_s[start : start + size, :].astype(low)
            d_rows_ref[:, width:] = d_gates[start : start + size, :]
            if with_mixed:
                mixed_refs[i][...] = mixed_s[start : start + size, :].astype(low)
            start += size


def expert_block(rows_list, ups_list, d_act, sel, w_router, w_gate, w_up, w_down, with_mixed, after=()):
    pieces = len(rows_list)
    sizes = [rows.shape[0] for rows in rows_list]
    rows = sum(sizes)
    local, width, ff = w_gate.shape
    cut = min(512, ff)
    cuts = ff // cut
    whole = lambda shape: pl.BlockSpec(shape, lambda j: (0,) * len(shape))
    across = pl.BlockSpec((1, width, cut), lambda j: (j // cuts, 0, j % cuts))
    tall = pl.BlockSpec((1, cut, width), lambda j: (j // cuts, j % cuts, 0))
    part = pl.BlockSpec((rows, cut), lambda j: (0, j))
    mixed_out = with_mixed * pieces
    outs, token = call(
        functools.partial(expert_body, pieces, cuts, local, with_mixed),
        (*rows_list, *ups_list, d_act, sel, w_router, w_gate, w_up) + (w_down,) * with_mixed,
        [ANY] * (2 * pieces)
        + [part, whole((local, LANES)), whole((LANES, width)), across, across]
        + [tall] * with_mixed,
        [whole((size, width)) for size in sizes[:mixed_out]]
        + [whole((size, width + LANES)) for size in sizes]
        + [part, part, part],
        [pltpu.HBM((size, width), low) for size in sizes[:mixed_out]]
        + [pltpu.HBM((size, width + LANES), low) for size in sizes]
        + [pltpu.HBM((rows, local * ff), low)] * 3,
        [
            pltpu.VMEM((rows, width), low),
            pltpu.VMEM((rows, LANES), low),
            pltpu.VMEM((rows, width), wide),
            pltpu.VMEM((rows, LANES), wide),
            pltpu.VMEM((rows, LANES), wide),
            pltpu.SemaphoreType.DMA((2 * pieces,)),
        ]
        + [pltpu.VMEM((rows, width), wide)] * with_mixed,
        grid=(local * cuts,),
        after=after,
        name="experts", vmem=40,
        cost=(14 * rows * width * local * ff, 6 * local * width * ff + 8 * rows * width),
    )
    return (
        outs[mixed_out : mixed_out + pieces], outs[:mixed_out], outs[mixed_out + pieces :], token
    )


def d_act_body(pieces, *refs):
    up_refs = refs[:pieces]
    down_ref, out_ref, ups_s, sems = refs[pieces:]

    @pl.when(pl.program_id(0) == 0)
    def _():
        copies, start = [], 0
        for i, ref in enumerate(up_refs):
            size = ref.shape[0]
            copies.append(
                pltpu.make_async_copy(
                    ref.at[:, pl.ds(0, ups_s.shape[1])], ups_s.at[pl.ds(start, size), :], sems.at[i]
                )
            )
            start += size
        for copy in copies:
            copy.start()
        wait_all(copies)

    out_ref[...] = dot(ups_s[...], down_ref[0], NT).astype(low)


def d_act_block(ups_list, w_down, after=()):
    local, ff, width = w_down.shape
    rows = sum(ups.shape[0] for ups in ups_list)
    return call(
        functools.partial(d_act_body, len(ups_list)),
        (*ups_list, w_down),
        [ANY] * len(ups_list) + [pl.BlockSpec((1, ff, width), lambda e: (e, 0, 0))],
        pl.BlockSpec((rows, ff), lambda e: (0, e)),
        Shape((rows, local * ff), low),
        [pltpu.VMEM((rows, width), low), pltpu.SemaphoreType.DMA((len(ups_list),))],
        grid=(local,),
        after=after,
        name="d_act", vmem=20,
        cost=(5e8, 1e6),
    )


def mixed_body(pieces, hidden_ref, down_ref, *refs):
    outs, total_s = refs[:pieces], refs[pieces]
    step = pl.program_id(0)
    product = dot(hidden_ref[...], down_ref[0], NN)

    @pl.when(step == 0)
    def _():
        total_s[...] = product

    @pl.when(step == pl.num_programs(0) - 1)
    def _():
        total = product if pl.num_programs(0) == 1 else total_s[...] + product
        start = 0
        for ref in outs:
            ref[...] = total[start : start + ref.shape[0]].astype(low)
            start += ref.shape[0]


def mixed_block(hidden, w_down, sizes, after=()):
    local, ff, width = w_down.shape
    rows = sum(sizes)
    return call(
        functools.partial(mixed_body, len(sizes)),
        (hidden, w_down),
        [pl.BlockSpec((rows, ff), lambda e: (0, e)), pl.BlockSpec((1, ff, width), lambda e: (e, 0, 0))],
        [pl.BlockSpec((size, width), lambda e: (0, 0)) for size in sizes],
        [Shape((size, width), low) for size in sizes],
        [pltpu.VMEM((rows, width), wide)],
        grid=(local,),
        after=after,
        name="mixed", vmem=24,
        cost=(3 * rows * width * local * ff, 5e6),
    )


def outer_body(pieces, seconds, split, place_ref, *refs):
    first_refs = refs[:pieces]
    second_refs = refs[pieces : pieces + seconds]
    mine_ref, other_ref, first_s, second_s, first_sems, second_sems = refs[pieces + seconds :]
    core = place_ref[0] % 2
    step = pl.program_id(0)
    cut = first_s.shape[2]
    width = second_s.shape[1]

    def load(at, slot):
        copies, start = [], 0
        for i, ref in enumerate(first_refs):
            size = ref.shape[0]
            copies.append(
                pltpu.make_async_copy(
                    ref.at[:, pl.ds(pl.multiple_of(at * cut, cut), cut)],
                    first_s.at[slot, pl.ds(start, size), :],
                    first_sems.at[slot, i],
                )
            )
            start += size
        return copies

    slot = step % 2

    @pl.when(step == 0)
    def _():
        for copy in load(0, 0):
            copy.start()
        copies, start = [], 0
        for i, ref in enumerate(second_refs):
            size = ref.shape[0]
            copies.append(
                pltpu.make_async_copy(
                    ref.at[:, pl.ds(0, width)], second_s.at[pl.ds(start, size), :], second_sems.at[i]
                )
            )
            start += size
        for copy in copies:
            copy.start()
        wait_all(copies)

    @pl.when(step + 1 < pl.num_programs(0))
    def _():
        for copy in load(step + 1, 1 - slot):
            copy.start()

    wait_all(load(step, slot))
    product = dot(first_s[slot], second_s[...], TN).astype(low)
    if split == 1:

        @pl.when(step == core)
        def _():
            mine_ref[...] = product

        @pl.when(step != core)
        def _():
            other_ref[...] = product
    else:
        first, last = product[:, : width // 2], product[:, width // 2 :]
        mine_ref[...] = jnp.where(core == 0, first, last)
        other_ref[...] = jnp.where(core == 0, last, first)


def outer_products(place, first, second, first_width, second_width, split, after=()):
    cut = 512
    steps = first_width // cut
    rows = sum(piece.shape[0] for piece in first)
    if split == 1:
        out_shape = Shape((cut, second_width), low)
        out_spec = pl.BlockSpec((cut, second_width), lambda i: (0, 0))
    else:
        out_shape = Shape((first_width, second_width // 2), low)
        out_spec = pl.BlockSpec((cut, second_width // 2), lambda i: (i, 0))
    return call(
        functools.partial(outer_body, len(first), len(second), split),
        (place, *first, *second),
        [SMEM] + [ANY] * (len(first) + len(second)),
        [out_spec] * 2,
        [out_shape] * 2,
        [
            pltpu.VMEM((2, rows, cut), low),
            pltpu.VMEM((rows, second_width), low),
            pltpu.SemaphoreType.DMA((2, len(first))),
            pltpu.SemaphoreType.DMA((len(second),)),
        ],
        grid=(steps,),
        after=after,
        name="outer_products", vmem=24 if rows <= 4096 else 58,
        cost=(3.5 * rows * first_width * second_width, 12e6),
    )


def ring_parts_of(count, ids_ref, flat_s, outs):
    part = flat_s.shape[0] // count
    for o, ref in enumerate(outs):
        size = ref.shape[0]
        if o < count // 2:
            at = ids_ref[o] * part
        elif o > count // 2 + 1:
            at = ids_ref[o - 1] * part
        else:
            at = ids_ref[count // 2] * part + (o - count // 2) * size
        ref[...] = flat_s[pl.ds(pl.multiple_of(at, size), size), :]


def ring_part_sizes(count, flat):
    part = flat // count
    return [part] * (count // 2) + [part // 2] * 2 + [part] * (count // 2 - 1)


def small_rows(count):
    return 4 * count


def ring_part_list(count, outs):
    half = count // 2
    return list(outs[:half]) + [tuple(outs[half : half + 2])] + list(outs[half + 2 :])


def head_grads_body(count, place_ref, ids_ref, *refs):
    rows_refs, d_refs = refs[:4], refs[4:8]
    att_ref, d_lin_ref, wq_ref, wk_ref, wv_ref, gain_ref, gain_ffn_ref, router_ref = refs[8:16]
    outs = refs[16 : 16 + count + 1]
    rows_s, d_s, flat_s, small_s, sems, d_sems = refs[17 + count :]
    small_s[...] = jnp.zeros_like(small_s)
    small_s[:1, :] = gain_ffn_ref[...]
    small_s[2 : 2 + router_ref.shape[0], :] = router_ref[...]
    copies = load_blocks(place_ref[0], rows_refs, rows_s, sems)
    d_copies = load_blocks(place_ref[0], d_refs, d_s, d_sems)
    wait_all(copies)
    q_width, kv_width = wq_ref.shape[1], wk_ref.shape[1]
    lin_width = d_lin_ref.shape[1]
    width = rows_s.shape[1]
    for at in range(0, width, 512):
        here = pl.ds(at, 512)
        grads = dot(rows_s[:, here], d_lin_ref[...], TN)
        for c in range(0, lin_width, LANES):
            row = c // LANES * width + at
            flat_s[row : row + 512, :] = grads[:, c : c + LANES].astype(low)
        inner = jnp.sum(wq_ref[here, :].astype(wide) * grads[:, :q_width], axis=1, keepdims=True)
        inner += jnp.sum(
            wk_ref[here, :].astype(wide) * grads[:, q_width : q_width + kv_width], axis=1, keepdims=True
        )
        inner += jnp.sum(
            wv_ref[here, :].astype(wide) * grads[:, q_width + kv_width :], axis=1, keepdims=True
        )
        inner = jnp.transpose(jnp.broadcast_to(inner, (512, LANES)))[:1]
        small_s[1:2, here] = inner / gain_ref[:, here]
    wait_all(d_copies)
    base = lin_width // LANES * width
    for at in range(0, width, 512):
        grads = dot(att_ref[...], d_s[:, at : at + 512], TN).astype(low)
        for c in range(0, 512, LANES):
            row = base + (at + c) // LANES * q_width
            flat_s[row : row + q_width, :] = grads[:, c : c + LANES]
    base = base + width // LANES * q_width
    size = small_s.shape[0]
    for c in range(0, width, LANES):
        row = base + c // LANES * size
        flat_s[row : row + size, :] = small_s[:, c : c + LANES].astype(low)
    row = base + width // LANES * size
    flat_s[row:, :] = jnp.zeros((flat_s.shape[0] - row, LANES), low)
    ring_parts_of(count, ids_ref, flat_s, outs)


def head_grads(
    place, ids, rows_blocks, d_blocks, att, d_lin, wq, wk, wv, gain, gain_ffn_part, router_part, after=()
):
    count = lax.axis_size("dp")
    rows, width = rows_blocks[0].shape
    length, lin_width = d_lin.shape
    flat = width * (lin_width + att.shape[1]) // LANES + 64 * count
    outs, token = call(
        functools.partial(head_grads_body, count),
        (place, ids, *rows_blocks, *d_blocks, att, d_lin, wq, wk, wv, gain, gain_ffn_part, router_part),
        [SMEM, SMEM] + [ANY] * 8 + [VMEM] * 8,
        [VMEM] * (count + 1),
        [Shape((size, LANES), low) for size in ring_part_sizes(count, flat)],
        [
            pltpu.VMEM((length, width), low),
            pltpu.VMEM((length, width), low),
            pltpu.VMEM((flat, LANES), low),
            pltpu.VMEM((small_rows(count), width), wide),
            pltpu.SemaphoreType.DMA((4,)),
            pltpu.SemaphoreType.DMA((4,)),
        ],
        after=after,
        name="head_grads", vmem=30,
        cost=(8e-6 * 1.1e15, 12e6),
    )
    return ring_part_list(count, outs), token


def ring_sum_body(own_ref, up_ref, down_ref, out_ref):
    out_ref[...] = (
        own_ref[...].astype(wide) + up_ref[...].astype(wide) + down_ref[...].astype(wide)
    ).astype(low)


def ring_total(parts, before, then, last):
    half = len(parts) // 2
    up, down = ring_scatter(
        [parts[len(parts) - 1 - i] for i in range(half - 1)],
        [parts[1 + i] for i in range(half - 1)],
        parts[half],
        before,
        then,
    )
    total, _ = call(
        ring_sum_body, (parts[0], up, down), [VMEM] * 3, VMEM, Shape(parts[0].shape, low),
        after=last(), name="ring_sum", cost=(1e8, 1e6),
    )
    below, above, far = ring_gather(total)
    return [total] + above + list(far) + below[::-1]


def head_place_body(count, ids_ref, *refs):
    blocks = refs[: count + 1]
    grads, small_ref, flat_s = refs[count + 1 : -2], refs[-2], refs[-1]
    part = flat_s.shape[0] // count
    for o, ref in enumerate(blocks):
        size = ref.shape[0]
        if o < count // 2:
            at = ids_ref[o] * part
        elif o > count // 2 + 1:
            at = ids_ref[o - 1] * part
        else:
            at = ids_ref[count // 2] * part + (o - count // 2) * size
        flat_s[pl.ds(pl.multiple_of(at, size), size), :] = ref[...]
    row = 0
    for ref in grads:
        rows, columns = ref.shape
        for c in range(0, columns, LANES):
            ref[:, c : c + LANES] = flat_s[row : row + rows, :].astype(wide)
            row += rows
    rows, columns = small_ref.shape
    for c in range(0, columns, LANES):
        small_ref[:, c : c + LANES] = flat_s[row : row + rows, :].astype(wide)
        row += rows


def head_place(ids, blocks, shapes, small_shape):
    count = lax.axis_size("dp")
    flat = sum(rows * columns for rows, columns in shapes) // LANES + 64 * count
    return call(
        functools.partial(head_place_body, count),
        (ids, *blocks),
        [SMEM] + [VMEM] * (count + 1),
        [VMEM] * (len(shapes) + 1),
        [Shape(shape, wide) for shape in (*shapes, small_shape)],
        [pltpu.VMEM((flat, LANES), low)],
        name="head_place", vmem=24,
        cost=(1e9, 6e6),
    )[0]


def add_body(first_ref, second_ref, out_ref):
    out_ref[...] = (first_ref[...].astype(wide) + second_ref[...].astype(wide)).astype(low)


def add_rows(first, second, after=()):
    return call(
        add_body, (first, second), [VMEM] * 2, VMEM, Shape(first.shape, low), after=after,
        name="add_rows", cost=(1e8, 3e6),
    )


def place_quarters_body(place_ref, *refs):
    del place_ref
    pieces, out_ref = refs[:4], refs[4]
    step = pl.program_id(0)
    for i, ref in enumerate(pieces):

        @pl.when(step == i)
        def _():
            out_ref[0] = ref[...].astype(wide)


def place_quarters(place, pieces):
    rows, columns = pieces[0].shape
    fixed = pl.BlockSpec((rows, columns), lambda i, place_ref: (0, 0))
    out = pl.BlockSpec(
        (1, rows, columns),
        lambda i, place_ref: (i // 2 ^ place_ref[0] % 2, i % 2 ^ place_ref[0] // 2, 0),
    )
    result, token = pl.pallas_call(
        place_quarters_body,
        grid_spec=pltpu.PrefetchScalarGridSpec(
            num_scalar_prefetch=1, grid=(4,), in_specs=[fixed] * 4, out_specs=[out, VMEM]
        ),
        out_shape=[pltpu.HBM((2, 2 * rows, columns), wide), pltpu.VMEM(TOKEN, wide)],
        compiler_params=pltpu.CompilerParams(vmem_limit_bytes=16 * MEGABYTE),
        cost_estimate=pl.CostEstimate(flops=10**8, bytes_accessed=10**7, transcendentals=0),
        name="place_quarters",
    )(place, *pieces)
    return result, Token(token)


def lin_back_body(place_ref, d_lin_ref, wq_ref, wk_ref, wv_ref, mine_ref, other_ref):
    rows = mine_ref.shape[1]
    core = place_ref[0] % 2
    q_width, kv_width = wq_ref.shape[1], wk_ref.shape[1]
    for x in range(2):
        for ref, c in ((other_ref, 1 - core), (mine_ref, core)):
            at = pl.ds(pl.multiple_of((2 * x + c) * rows, rows), rows)
            total = dot(d_lin_ref[at, :q_width], wq_ref[...], NT)
            total += dot(d_lin_ref[at, q_width : q_width + kv_width], wk_ref[...], NT)
            total += dot(d_lin_ref[at, q_width + kv_width :], wv_ref[...], NT)
            ref[x] = total.astype(low)


def lin_back(place, d_lin, wq, wk, wv, after):
    rows, width = d_lin.shape[0] // 4, wq.shape[0]
    return call(
        lin_back_body,
        (place, d_lin, wq, wk, wv),
        [SMEM] + [VMEM] * 4,
        [VMEM] * 2,
        [Shape((2, rows, width), low)] * 2,
        after=after,
        name="lin_back", vmem=20,
        cost=(4e-6 * 1.1e15, 9e6),
    )


def first_norm_body(tokens_ref, gain_ref, cotangent_ref, routes_ref, normed_ref, ups_ref):
    width = cotangent_ref.shape[1]
    routes = routes_ref[...]
    lane = lax.broadcasted_iota(jnp.int32, (LANES, routes.shape[1]), 0)
    chosen = routes[:1, :] == lane
    for k in range(1, routes.shape[0]):
        chosen = chosen | (routes[k : k + 1, :] == lane)
    ups_ref[:, :width] = cotangent_ref[...]
    ups_ref[:, width:] = jnp.transpose(jnp.where(chosen, 1.0, 0.0)).astype(low)
    inputs = tokens_ref[...].astype(wide)
    inverse = lax.rsqrt(jnp.mean(inputs * inputs, axis=1, keepdims=True) + EPS)
    normed_ref[...] = (inputs * inverse * gain_ref[...]).astype(low)


def second_norm_body(tokens_ref, kept_ref, got_ref, gain_ref, residual_ref, normed_ref):
    residual = tokens_ref[...].astype(wide) + (kept_ref[...].astype(wide) + got_ref[...].astype(wide))
    inverse = lax.rsqrt(jnp.mean(residual * residual, axis=1, keepdims=True) + EPS)
    residual_ref[...] = residual
    normed_ref[...] = (residual * inverse * gain_ref[...]).astype(low)


def middle_body(
    own_ref, up_ref, down_ref, residual_ref, normed_ref, ups_ref, router_ref, gain_ref, first_ref, second_ref,
    d_residual_ref, d_low_ref, gain_out, router_out, first_out, second_out,
):
    del first_ref, second_ref, first_out, second_out
    width = residual_ref.shape[1]
    total = own_ref[...].astype(wide) + up_ref[...].astype(wide) + down_ref[...].astype(wide)
    d_gates = total[:, width:]
    d_gates = d_gates + pltpu.roll(d_gates, LANES // 2, 1)
    lane = lax.broadcasted_iota(jnp.int32, d_gates.shape, 1)
    chosen = ups_ref[:, width:] > 0.0
    normed = normed_ref[...]
    logits = jnp.where(chosen, dot(normed, router_ref[...], NT), NEG)
    largest = jnp.max(logits, axis=1, keepdims=True)
    shifted = jnp.where(chosen, jnp.exp(logits - largest), 0.0)
    gates = shifted / jnp.sum(shifted, axis=1, keepdims=True)
    inner = jnp.sum(gates * d_gates, axis=1, keepdims=True)
    d_logits = (gates * (d_gates - inner)).astype(low)
    router_part = dot(d_logits, normed, TN)[: router_out.shape[0]]
    d_normed = total[:, :width] + dot(d_logits, router_ref[...], NN)
    residual = residual_ref[...]
    inverse = lax.rsqrt(jnp.mean(residual * residual, axis=1, keepdims=True) + EPS)
    scaled = d_normed * gain_ref[...]
    mean = jnp.mean(scaled * residual, axis=1, keepdims=True)
    upstream = ups_ref[:, :width].astype(wide)
    d_residual = upstream + inverse * scaled - residual * (inverse * inverse * inverse * mean)
    gain_part = jnp.sum(d_normed * residual * inverse, axis=0, keepdims=True)

    @pl.when(pl.program_id(0) == 0)
    def _():
        gain_out[...] = gain_part
        router_out[...] = router_part

    @pl.when(pl.program_id(0) > 0)
    def _():
        gain_out[...] += gain_part
        router_out[...] += router_part

    d_residual_ref[...] = d_residual
    d_low_ref[...] = d_residual.astype(low)


def last_body(tokens_ref, kept_ref, got_ref, d_residual_ref, gain_ref, out_ref):
    inputs = tokens_ref[...].astype(wide)
    inverse = lax.rsqrt(jnp.mean(inputs * inputs, axis=1, keepdims=True) + EPS)
    scaled = (kept_ref[...].astype(wide) + got_ref[...].astype(wide)) * gain_ref[...]
    mean = jnp.mean(scaled * inputs, axis=1, keepdims=True)
    d_inputs = inverse * scaled - inputs * (inverse * inverse * inverse * mean)
    out_ref[...] = (d_inputs + d_residual_ref[...]).astype(low)


def on_device(
    tokens,
    gain_attn,
    query_weight,
    key_weight,
    value_weight,
    w_output,
    gain_ffn,
    w_router,
    w_gate,
    w_up,
    w_down,
    segments,
    routes,
    cotangent,
):
    rows_dev, width = tokens.shape
    data_count = lax.axis_size("dp")
    half_count = data_count // 2
    local_experts, _, ff = w_gate.shape
    expert_count = local_experts * data_count
    q_width, kv_width = query_weight.shape[1], key_weight.shape[1]
    place = lax.axis_index("tensor").astype(jnp.int32).reshape(1)
    ids = ring_places()
    cos, sin = rope_tables(segments.shape[1])
    gain_one, gain_two = gain_attn.reshape(1, width), gain_ffn.reshape(1, width)
    lanes = jnp.arange(LANES, dtype=jnp.int32)
    own_experts = lax.axis_index("dp") * local_experts + jnp.arange(local_experts, dtype=jnp.int32)
    sel = (own_experts[:, None] == lanes[None, :]).astype(wide)
    router = jnp.pad(w_router.T, ((0, LANES - expert_count), (0, 0)))

    half_rows = rows_dev // 2
    row_spec = pl.BlockSpec((half_rows, width), lambda i: (i, 0))
    wide_spec = pl.BlockSpec((half_rows, width + LANES), lambda i: (i, 0))
    gain_spec = pl.BlockSpec((1, width), lambda i: (0, 0))
    (normed_one, ups), _ = call(
        first_norm_body,
        (tokens, gain_one, cotangent, routes.T),
        [row_spec, gain_spec, row_spec, pl.BlockSpec((routes.shape[1], half_rows), lambda i: (0, i))],
        [row_spec, wide_spec],
        [Shape((rows_dev, width), low), Shape((rows_dev, width + LANES), low)],
        grid=(2,), name="first_norm", cost=(1e9, 2e6), vmem=60,
    )
    d_acts = [d_act_block((ups,), w_down)]

    def early_acts(below, above):
        for pair in list(zip(below, above))[: half_count - 2]:
            d_acts.append(d_act_block(pair, w_down))
        below[-1], above[-1] = hold((below[-1], above[-1]), [token for _, token in d_acts])
        return below[-1], above[-1]

    ups_below, ups_above, ups_far = ring_gather(ups, early_acts)
    rows_blocks = tensor_blocks(normed_one)
    ups_groups = [(ups,)] + list(zip(ups_below, ups_above)) + [ups_far]
    d_acts += [d_act_block(group, w_down) for group in ups_groups[-2:]]
    (att, q, k, v, lse), _ = attend(
        place, rows_blocks, query_weight, key_weight, value_weight, cos, sin, segments,
        after=(ups_below[0], ups_above[0]),
    )
    other = branch_half(place, att, w_output, True, after=(ups_below[1], ups_above[1]))
    mine = branch_half(place, att, w_output, False)
    kept, got, _ = tensor_scatter(place, mine, other, after=())
    (residual, normed_two), _ = call(
        second_norm_body, (tokens, kept, got, gain_two), [row_spec] * 3 + [gain_spec], [row_spec] * 2,
        [pltpu.HBM((rows_dev, width), wide), pltpu.HBM((rows_dev, width), low)],
        after=(ups_below[-1], ups_above[-1]), grid=(2,), name="second_norm", cost=(1e9, 4e6),
    )
    rows_below, rows_above, rows_far = ring_gather(normed_two)
    rows_groups = [(normed_two,)] + list(zip(rows_below, rows_above)) + [rows_far]
    done = []
    for index, (rows, up) in enumerate(zip(rows_groups, ups_groups)):
        after = () if not done else (done[-1][3],)
        if len(done) in (1, 2):
            after += (d_acts[len(done) - 3][1],)
        done.append(
            expert_block(
                rows, up, d_acts[index][0], sel, router, w_gate, w_up, w_down,
                index < len(rows_groups) - 2, after,
            )
        )
    rows_all = [piece for rows in rows_groups for piece in rows]
    ups_all = [piece for up in ups_groups for piece in up]
    hidden_all, d_gate_all, d_up_all = ([outs[2][i] for outs in done] for i in range(3))
    inner = local_experts * ff
    split_rows = {"down": ff // 2, "gate": width // 2, "up": width // 2}
    grads = {
        "down": outer_products(place, hidden_all, ups_all, inner, width, 1)[0],
        "gate": outer_products(place, rows_all, d_gate_all, width, inner, 2)[0],
        "up": outer_products(place, rows_all, d_up_all, width, inner, 2)[0],
    }
    names = ("down", "gate", "up")
    halves, half_tokens, quarters = {}, {}, {}

    def quarter(name, after=()):
        quarters[name], token = add_rows(halves[name][0], swap(halves[name][1], "tensor", 2), after)
        return token

    def before(index):
        if index > 2:
            return (), ()
        after = (half_tokens[names[index - 1]],) if index else ()
        if index == 2:
            after += (quarter("down"),)
        return after, (grads[names[index]][1],)

    def then(index, _, held):
        if index > 2:
            return
        name = names[index]
        mine, other = (array.reshape(2, split_rows[name], -1) for array in (grads[name][0], held[0]))
        halves[name], half_tokens[name] = split_add(place, mine, swap(other, "tensor", 1))

    d_rows_up, d_rows_down = ring_scatter(
        [outs[0][0] for outs in done[1:-1]], [outs[0][1] for outs in done[1:-1]], done[-1][0], before, then
    )
    late = [
        mixed_block(done[i][2][0], w_down, [rows.shape[0] for rows in rows_groups[i]]) for i in (-2, -1)
    ]
    mixed_parts = [outs[1] for outs in done[:-2]] + [parts for parts, _ in late]
    (d_residual, d_low, gain_ffn_part, router_part, *far_mixed), _ = call(
        middle_body,
        (done[0][0][0], d_rows_up, d_rows_down, residual, normed_two, ups, router, gain_two, *late[1][0]),
        [wide_spec] * 3
        + [row_spec] * 2
        + [wide_spec, pl.BlockSpec((LANES, width), lambda i: (0, 0)), gain_spec]
        + [ANY] * 2,
        [row_spec] * 2 + [gain_spec, pl.BlockSpec((expert_count, width), lambda i: (0, 0))] + [ANY] * 2,
        [
            pltpu.HBM((rows_dev, width), wide),
            pltpu.HBM((rows_dev, width), low),
            Shape((1, width), wide),
            Shape((expert_count, width), wide),
        ]
        + [Shape(part.shape, low) for part in late[1][0]],
        grid=(2,),
        after=(late[0][1], quarter("gate")),
        name="middle", vmem=16, cost=(4e-6 * 1.1e15, 4e6), alias={8: 4, 9: 5},
    )
    d_near, d_far = swap(d_low, "tensor", 1), swap(d_low, "tensor", 2)
    marks, back, d_blocks, pieces = [], [], [], {}

    def gather_pieces(name):
        second = swap(quarters[name], "tensor", 2)
        pieces[name] = (
            quarters[name], second, swap(quarters[name], "tensor", 1), swap(second, "tensor", 1)
        )

    def before_mixed(index):
        if index == 0:
            return (), (halves["up"][1],)
        if index == 1:
            return (back[1],), (quarters["down"],)
        return (), ()

    def then_mixed(index, token, held):
        marks.append(token)
        if index == 0:
            halves["up"][1] = held[0]
            (far,) = hold((d_far,), (token,))
            d_blocks.extend((d_low, d_near, far, swap(far, "tensor", 1)))
            back.extend(
                attend_back(place, d_blocks, w_output, att, q, k, v, lse, cos, sin, segments, after=(token,))
            )
        if index == 1:
            quarters["down"] = held[0]
            gather_pieces("down")

    mixed_up, mixed_down = ring_scatter(
        [parts[0] for parts in mixed_parts[1:-1]], [parts[1] for parts in mixed_parts[1:-1]], far_mixed,
        before_mixed, then_mixed,
    )
    d_lin = back[0]
    parts, parts_token = head_grads(
        place, ids, rows_blocks, d_blocks, att, d_lin, query_weight, key_weight, value_weight, gain_one,
        gain_ffn_part, router_part, after=(marks[1],),
    )
    up_token = quarter("up", (parts_token,))
    (mine, other), lin_token = lin_back(
        place, d_lin, query_weight, key_weight, value_weight, after=(parts_token,)
    )
    sums, totals = {}, {}

    def before_total(index):
        if index == 0:
            return (marks[2], pieces["down"][1], up_token), (other, quarters["gate"])
        if index == 1:
            return (totals["down"][1], sums["token"]), (quarters["up"],)
        if index == 2:
            return (mixed_up, mixed_down, pieces["gate"][1]), ()
        return (), ()

    def then_total(index, token, held):
        if index == 0:
            quarters["gate"] = held[1]
            gather_pieces("gate")
            totals["down"] = place_quarters(place, pieces["down"])
            sums["kept"], sums["got"], sums["token"] = tensor_scatter(place, mine, held[0], ())
        if index == 1:
            (quarters["up"],) = held
            gather_pieces("up")
        if index == 2:
            totals["gate"] = place_quarters(place, pieces["gate"])

    blocks = ring_total(parts, before_total, then_total, lambda: (totals["gate"][1], sums["got"]))
    totals["up"] = place_quarters(place, pieces["up"])
    kept, got = sums["kept"], sums["got"]
    mixed = (
        residual + mixed_parts[0][0].astype(wide) + mixed_up.astype(wide) + mixed_down.astype(wide)
    ).astype(low)
    grad_tokens, _ = call(
        last_body, (tokens, kept, got, d_residual, gain_one), [row_spec] * 4 + [gain_spec], row_spec,
        Shape((rows_dev, width), low), grid=(2,), name="last", cost=(1e9, 4e6),
    )
    grad_q, grad_k, grad_v, grad_o, small = head_place(
        ids, blocks, [(width, q_width), (width, kv_width), (width, kv_width), (q_width, width)],
        (small_rows(data_count), width),
    )
    small = small + swap(small, "tensor", 1)
    small = small + swap(small, "tensor", 2)
    return (
        mixed,
        grad_tokens,
        small[1],
        grad_q,
        grad_k,
        grad_v,
        grad_o,
        small[0],
        small[2 : 2 + expert_count].T,
        totals["gate"][0],
        totals["up"][0],
        totals["down"][0],
    )


def solution(mesh):
    in_specs = (
        P(("dp", "tensor"), None),
        P(),
        P(None, "tensor"),
        P(None, "tensor"),
        P(None, "tensor"),
        P("tensor", None),
        P(),
        P(),
        P("dp", None, None),
        P("dp", None, None),
        P("dp", None, None),
        P("dp", None),
        P(("dp", "tensor"), None),
        P(("dp", "tensor"), None),
    )
    out_specs = (
        P(("dp", "tensor"), None),
        P(("dp", "tensor"), None),
        P(),
        P(None, "tensor"),
        P(None, "tensor"),
        P(None, "tensor"),
        P("tensor", None),
        P(),
        P(),
        P("dp", None, None),
        P("dp", None, None),
        P("dp", None, None),
    )
    return jax.shard_map(
        on_device, mesh=mesh, in_specs=in_specs, out_specs=out_specs, check_vma=False
    )
```

```python
import functools
import math

import jax
import jax.numpy as jnp
import numpy as np
from jax import lax
from jax.experimental import pallas as pl
from jax.experimental.pallas import tpu as pltpu
from jax.sharding import PartitionSpec as P

HEAD_WIDTH = 64
EPS = 1e-06
ROPE_BASE = 10000.0
NEG = -1e30
LANES = 128
BLOCK = 256
REACH = 512
MEGABYTE = 1024 * 1024
low = jnp.bfloat16
wide = jnp.float32
NN = (((1,), (0,)), ((), ()))
NT = (((1,), (1,)), ((), ()))
TN = (((0,), (0,)), ((), ()))
dot = functools.partial(lax.dot_general, preferred_element_type=jnp.float32)
Shape = jax.ShapeDtypeStruct
ANY = pl.BlockSpec(memory_space=pl.ANY)
VMEM = pl.BlockSpec(memory_space=pltpu.VMEM)
SMEM = pl.BlockSpec(memory_space=pltpu.SMEM)


def rope_tables(length):
    half = HEAD_WIDTH // 2
    freq = np.exp(-(np.arange(half, dtype=np.float32) * (2.0 / HEAD_WIDTH)) * math.log(ROPE_BASE))
    angle = np.arange(length, dtype=np.float32)[:, None] * freq.astype(np.float32)[None, :]
    cos, sin = np.cos(angle), np.sin(angle)
    cos = np.concatenate([cos] * 4, axis=1).astype(np.float32)
    sin = np.concatenate([-sin, sin, -sin, sin], axis=1).astype(np.float32)
    return jnp.asarray(cos), jnp.asarray(sin)


def ring_order(count):
    return list(range(0, count, 2)) + list(range(count - 1, 0, -2))


def ring_send(array, step):
    count = lax.axis_size("dp")
    order = ring_order(count)
    return lax.ppermute(
        array, "dp", [(order[i], order[(i + step) % count]) for i in range(count)]
    )


def ring_places():
    count = lax.axis_size("dp")
    order = ring_order(count)
    table = [[(order.index(i) + o) % count for o in range(count)] for i in range(count)]
    table = jnp.asarray(np.asarray(table, np.int32))
    return lax.dynamic_index_in_dim(table, lax.axis_index("dp"), 0, keepdims=False)


def ring_gather(array, last=None, ties=()):
    count = lax.axis_size("dp")
    below, above = [], []
    up, down = array, array
    for step in range(1, count // 2):
        if ties and step == count // 2 - 1:
            up, down = hold((up, down), ties)
        up = ring_send(up, 1)
        down = ring_send(down, -1)
        below.append(up)
        above.append(down)
    if last is None:
        half = array.shape[0] // 2
        up, down = up[:half], down[half:]
    else:
        up, down = halves_of(up, down, last(below, above))
    return below, above, (ring_send(up, 1), ring_send(down, -1))


def swap(array, axis, mask):
    return lax.ppermute(array, axis, [(i, i ^ mask) for i in range(lax.axis_size(axis))])


def tensor_blocks(array):
    far = swap(array, "tensor", 2)
    return array, swap(array, "tensor", 1), far, swap(far, "tensor", 1)


class Token:
    def __init__(self, array):
        self.array = array


TOKEN = (8, LANES)


def call(body, operands, in_specs, out_specs, out_shape, scratch=(), grid=None, after=(), name=None, cost=None, alias=None, vmem=10):
    count = len(after)
    position = len(operands)
    single = not isinstance(out_shape, (list, tuple))
    shapes = [out_shape] if single else list(out_shape)
    specs = [out_specs] if single else list(out_specs)

    def kernel(*refs):
        outs = position + count + len(shapes)
        body(*refs[:position], *refs[position + count : outs], *refs[outs + 1 :])

    extra = {} if grid is None else {"grid": grid}
    if cost is not None:
        extra["cost_estimate"] = pl.CostEstimate(
            flops=int(cost[0]), bytes_accessed=int(cost[1]), transcendentals=0
        )
    if alias is not None:
        extra["input_output_aliases"] = alias
    waits = [entry.array if isinstance(entry, Token) else entry for entry in after]
    results = pl.pallas_call(
        kernel,
        in_specs=list(in_specs) + [ANY] * count,
        out_specs=specs + [VMEM],
        out_shape=shapes + [pltpu.VMEM(TOKEN, wide)],
        scratch_shapes=list(scratch),
        compiler_params=pltpu.CompilerParams(vmem_limit_bytes=vmem * MEGABYTE),
        name=name,
        **extra,
    )(*operands, *waits)
    token = Token(results[-1])
    return (results[0] if single else list(results[:-1])), token


def ring_add_body(first, held, up_ref, part_up_ref, down_ref, part_down_ref, *refs):
    up_out, down_out = refs[held : held + 2]

    def add(got_ref, part_ref, out_ref):
        out_ref[...] = (got_ref[...].astype(wide) + part_ref[...].astype(wide)).astype(low)

    def keep(part_ref, out_ref):
        out_ref[...] = part_ref[...]

    if not first:
        add(up_ref, part_up_ref, up_out)
        add(down_ref, part_down_ref, down_out)
        return

    @pl.when(pl.program_id(0) == 0)
    def _():
        add(up_ref, part_up_ref, up_out)
        keep(part_down_ref, down_out)

    @pl.when(pl.program_id(0) == 1)
    def _():
        keep(part_up_ref, up_out)
        add(down_ref, part_down_ref, down_out)


def ring_add(first, up, part_up, down, part_down, after, held, vmem=10):
    rows, width = part_up.shape
    part = pl.BlockSpec((rows // 2, width), lambda i: (i, 0))
    got = pl.BlockSpec((rows // 2, width), lambda i: (0, 0)) if first else part
    return call(
        functools.partial(ring_add_body, first, len(held)),
        (up, part_up, down, part_down, *held),
        [got, part, got, part] + [ANY] * len(held),
        [part, part] + [ANY] * len(held),
        [Shape((rows, width), low)] * 2 + [Shape(array.shape, array.dtype) for array in held],
        grid=(2,),
        after=after,
        name="ring_add", vmem=vmem,
        cost=(1e8, 4e6),
        alias={4 + i: 2 + i for i in range(len(held))},
    )


def halves_body(up_ref, down_ref, top_ref, bottom_ref):
    top_ref[...] = up_ref[...]
    bottom_ref[...] = down_ref[...]


def halves_of(up, down, after):
    half, width = up.shape[0] // 2, up.shape[1]
    rows = half // 2
    out = pl.BlockSpec((rows, width), lambda i: (i, 0))
    return call(
        halves_body, (up, down), [out, pl.BlockSpec((rows, width), lambda i: (i + 2, 0))], [out] * 2,
        [pltpu.HBM((half, width), low)] * 2, grid=(2,), after=after, name="halves", cost=(1e6, 1e5),
    )[0]


def hold_body(*refs):
    del refs


def hold(arrays, after):
    return call(
        hold_body, arrays, [ANY] * len(arrays), [ANY] * len(arrays),
        [Shape(array.shape, array.dtype) for array in arrays], after=after, name="hold", cost=(1e6, 1e5),
        alias={i: i for i in range(len(arrays))},
    )[0]


def ring_steps(below, above, opposite):
    up = ring_send(opposite[0], 1)
    down = ring_send(opposite[1], -1)
    for k in range(len(above), 0, -1):
        after, held, vmem = yield up, down
        (up, down, *held), token = ring_add(
            k == len(above), up, above[k - 1], down, below[k - 1], after, held, vmem
        )
        up, down = yield token, held, (up, down)
        up = ring_send(up, 1)
        down = ring_send(down, -1)
    yield up, down


def ring_step(steps, after=(), held=(), vmem=10):
    token, held, sums = steps.send((after, held, vmem))
    return token, held, steps.send(sums)


def ring_scatter(below, above, opposite, before=None, then=None):
    steps = ring_steps(below, above, opposite)
    next(steps)
    for index in range(len(above)):
        after, held = before(index) if before else ((), ())
        token, held, arrived = ring_step(steps, after, held)
        if then:
            then(index, token, held)
    return arrived


def swap(array, axis, mask):
    return lax.ppermute(array, axis, [(i, i ^ mask) for i in range(lax.axis_size(axis))])


def tensor_blocks(array):
    far = swap(array, "tensor", 2)
    return array, swap(array, "tensor", 1), far, swap(far, "tensor", 1)


class Token:
    def __init__(self, array):
        self.array = array


TOKEN = (8, LANES)


def call(body, operands, in_specs, out_specs, out_shape, scratch=(), grid=None, after=(), name=None, cost=None, alias=None, vmem=10):
    count = len(after)
    position = len(operands)
    single = not isinstance(out_shape, (list, tuple))
    shapes = [out_shape] if single else list(out_shape)
    specs = [out_specs] if single else list(out_specs)

    def kernel(*refs):
        outs = position + count + len(shapes)
        body(*refs[:position], *refs[position + count : outs], *refs[outs + 1 :])

    extra = {} if grid is None else {"grid": grid}
    if cost is not None:
        extra["cost_estimate"] = pl.CostEstimate(
            flops=int(cost[0]), bytes_accessed=int(cost[1]), transcendentals=0
        )
    if alias is not None:
        extra["input_output_aliases"] = alias
    waits = [entry.array if isinstance(entry, Token) else entry for entry in after]
    results = pl.pallas_call(
        kernel,
        in_specs=list(in_specs) + [ANY] * count,
        out_specs=specs + [VMEM],
        out_shape=shapes + [pltpu.VMEM(TOKEN, wide)],
        scratch_shapes=list(scratch),
        compiler_params=pltpu.CompilerParams(vmem_limit_bytes=vmem * MEGABYTE),
        name=name,
        **extra,
    )(*operands, *waits)
    token = Token(results[-1])
    return (results[0] if single else list(results[:-1])), token


def ring_add_body(first, held, up_ref, part_up_ref, down_ref, part_down_ref, *refs):
    up_out, down_out = refs[held : held + 2]

    def add(got_ref, part_ref, out_ref):
        out_ref[...] = (got_ref[...].astype(wide) + part_ref[...].astype(wide)).astype(low)

    def keep(part_ref, out_ref):
        out_ref[...] = part_ref[...]

    if not first:
        add(up_ref, part_up_ref, up_out)
        add(down_ref, part_down_ref, down_out)
        return

    @pl.when(pl.program_id(0) == 0)
    def _():
        add(up_ref, part_up_ref, up_out)
        keep(part_down_ref, down_out)

    @pl.when(pl.program_id(0) == 1)
    def _():
        keep(part_up_ref, up_out)
        add(down_ref, part_down_ref, down_out)


def ring_add(first, up, part_up, down, part_down, after, held, vmem=10):
    rows, width = part_up.shape
    part = pl.BlockSpec((rows // 2, width), lambda i: (i, 0))
    got = pl.BlockSpec((rows // 2, width), lambda i: (0, 0)) if first else part
    return call(
        functools.partial(ring_add_body, first, len(held)),
        (up, part_up, down, part_down, *held),
        [got, part, got, part] + [ANY] * len(held),
        [part, part] + [ANY] * len(held),
        [Shape((rows, width), low)] * 2 + [Shape(array.shape, array.dtype) for array in held],
        grid=(2,),
        after=after,
        name="ring_add", vmem=vmem,
        cost=(1e8, 4e6),
        alias={4 + i: 2 + i for i in range(len(held))},
    )


def halves_body(up_ref, down_ref, top_ref, bottom_ref):
    top_ref[...] = up_ref[...]
    bottom_ref[...] = down_ref[...]


def halves_of(up, down, after):
    half, width = up.shape[0] // 2, up.shape[1]
    rows = half // 2
    out = pl.BlockSpec((rows, width), lambda i: (i, 0))
    return call(
        halves_body, (up, down), [out, pl.BlockSpec((rows, width), lambda i: (i + 2, 0))], [out] * 2,
        [pltpu.HBM((half, width), low)] * 2, grid=(2,), after=after, name="halves", cost=(1e6, 1e5),
    )[0]


def hold_body(*refs):
    del refs


def hold(arrays, after):
    return call(
        hold_body, arrays, [ANY] * len(arrays), [ANY] * len(arrays),
        [Shape(array.shape, array.dtype) for array in arrays], after=after, name="hold", cost=(1e6, 1e5),
        alias={i: i for i in range(len(arrays))},
    )[0]


def ring_scatter(below, above, opposite, before=None, then=None, vmem=()):
    up = ring_send(opposite[0], 1)
    down = ring_send(opposite[1], -1)
    for index, k in enumerate(range(len(above), 0, -1)):
        after, held = before(index) if before else ((), ())
        (up, down, *held), token = ring_add(
            index == 0, up, above[k - 1], down, below[k - 1], after, held, vmem[index] if index < len(vmem) else 10
        )
        if then:
            then(index, token, held)
        up = ring_send(up, 1)
        down = ring_send(down, -1)
    return up, down


def half_turn(array):
    width = array.shape[-1]
    half = HEAD_WIDTH // 2
    lane = lax.broadcasted_iota(jnp.int32, array.shape, 1)
    return jnp.where(
        lane % HEAD_WIDTH < half, pltpu.roll(array, width - half, 1), pltpu.roll(array, half, 1)
    )


def spread_heads(array):
    lane = lax.broadcasted_iota(jnp.int32, array.shape, 1)
    first = lane < HEAD_WIDTH
    other = pltpu.roll(array, HEAD_WIDTH, 1)
    zero = jnp.zeros_like(array)
    return [
        [jnp.where(first, array, zero), jnp.where(first, zero, other)],
        [jnp.where(first, other, zero), jnp.where(first, zero, array)],
    ]


def load_blocks(place, blocks, target, sems):
    rows = blocks[0].shape[0]
    copies = []
    for mask, block in enumerate(blocks):
        start = pl.multiple_of((place ^ mask) * rows, rows)
        copies.append(pltpu.make_async_copy(block, target.at[pl.ds(start, rows), :], sems.at[mask]))
    for copy in copies:
        copy.start()
    return copies


def fetch(pairs, sems):
    copies = [pltpu.make_async_copy(source, target, sems.at[i]) for i, (source, target) in enumerate(pairs)]
    for copy in copies:
        copy.start()
    return copies


def wait_all(copies):
    for copy in copies:
        copy.wait()


def column_of(row_ref, start, size):
    row = jnp.broadcast_to(row_ref[:, start : start + size].astype(wide), (LANES, size))
    return jnp.transpose(row)[:, :1].astype(jnp.int32)


def attend_body(
    place_ref, own, near, far, both, wq_any, wk_any, wv_any, cos_any, sin_any, row_ref,
    att_ref, q_ref, k_ref, v_ref, lse_ref, rows_s, wq_ref, wk_ref, wv_ref, cos_ref, sin_ref, kz_s, vz_s,
    sems, more_sems,
):
    place = place_ref[0]
    loads = fetch(
        ((wq_any, wq_ref), (cos_any, cos_ref), (sin_any, sin_ref), (wk_any, wk_ref), (wv_any, wv_ref)),
        more_sems,
    )
    copies = load_blocks(place, (own, near, far, both), rows_s, sems)
    length = rows_s.shape[0]
    pairs = wq_ref.shape[1] // LANES
    scale = HEAD_WIDTH**-0.5
    rows_dev = own.shape[0]
    for mask, copy in enumerate(copies):
        at = pl.ds(pl.multiple_of((place ^ mask) * rows_dev, rows_dev), rows_dev)
        copy.wait()
        if mask == 0:
            wait_all(loads)
        rows = rows_s[at, :]
        cos, sin = cos_ref[at, :], sin_ref[at, :]
        query = dot(rows, wq_ref[...], NN)
        for j in range(pairs):
            part = query[:, j * LANES : (j + 1) * LANES]
            turned = (part * cos + half_turn(part) * sin).astype(low)
            q_ref[at, j * LANES : (j + 1) * LANES] = (turned.astype(wide) * scale).astype(low)
        key = dot(rows, wk_ref[...], NN)
        key = (key * cos + half_turn(key) * sin).astype(low)
        k_ref[at, :] = key
        value = dot(rows, wv_ref[...], NN).astype(low)
        v_ref[at, :] = value
        keys, values = spread_heads(key.astype(wide)), spread_heads(value.astype(wide))
        for g in range(2):
            for off in range(2):
                kz_s[2 * g + off, at, :] = keys[g][off].astype(low)
                vz_s[2 * g + off, at, :] = values[g][off].astype(low)
    lane = lax.broadcasted_iota(jnp.int32, (BLOCK, LANES), 1)
    for start in range(0, length, BLOCK):
        at = pl.ds(start, BLOCK)
        first = max(0, start - REACH)
        span = start + BLOCK - first
        keys_at = pl.ds(first, span)
        row_id = lax.broadcasted_iota(jnp.int32, (BLOCK, span), 0) + start
        col_id = lax.broadcasted_iota(jnp.int32, (BLOCK, span), 1) + first
        allowed = (column_of(row_ref, start, BLOCK) == row_ref[:, keys_at]) & (row_id >= col_id)
        bias = jnp.where(allowed, 0.0, NEG)
        stats = jnp.zeros((BLOCK, LANES), wide)
        for j in range(pairs):
            query = q_ref[at, j * LANES : (j + 1) * LANES]
            total = None
            for off in range(2):
                h = 2 * j + off
                slot = 2 * (h // pairs) + off
                scores = dot(query, kz_s[slot, keys_at, :], NT) + bias
                largest = jnp.max(scores, axis=1, keepdims=True)
                shifted = jnp.exp(scores - largest)
                summed = jnp.sum(shifted, axis=1, keepdims=True)
                probs = (shifted * (1.0 / summed)).astype(low)
                part = dot(probs, vz_s[slot, keys_at, :], NN)
                total = part if total is None else total + part
                stats = jnp.where(lane == h, largest + jnp.log(summed), stats)
            att_ref[at, j * LANES : (j + 1) * LANES] = total.astype(low)
        lse_ref[at, :] = stats


def attend(place, blocks, wq, wk, wv, cos, sin, segs, after):
    rows, width = blocks[0].shape
    length = 4 * rows
    return call(
        attend_body,
        (place, *blocks, wq, wk, wv, cos, sin, segs.reshape(1, length)),
        [SMEM] + [ANY] * 9 + [VMEM],
        [VMEM] * 5,
        [
            Shape((length, wq.shape[1]), low),
            Shape((length, wq.shape[1]), low),
            Shape((length, wk.shape[1]), low),
            Shape((length, wk.shape[1]), low),
            Shape((length, LANES), wide),
        ],
        [
            pltpu.VMEM((length, width), low),
            pltpu.VMEM(wq.shape, low),
            pltpu.VMEM(wk.shape, low),
            pltpu.VMEM(wv.shape, low),
            pltpu.VMEM(cos.shape, wide),
            pltpu.VMEM(sin.shape, wide),
            pltpu.VMEM((4, length, LANES), low),
            pltpu.VMEM((4, length, LANES), low),
            pltpu.SemaphoreType.DMA((4,)),
            pltpu.SemaphoreType.DMA((5,)),
        ],
        after=after,
        name="attend", vmem=62,
        cost=(15e-6 * 1.1e15, 12e6),
    )


def branch_body(flip, place_ref, att_ref, wo_ref, out_ref):
    rows = out_ref.shape[1]
    core = place_ref[0] % 2
    core = 1 - core if flip else core
    for x in range(2):
        at = pl.ds(pl.multiple_of((2 * x + core) * rows, rows), rows)
        out_ref[x] = dot(att_ref[at, :], wo_ref[...], NN).astype(low)


def branch_half(place, att, wo, flip, after=()):
    rows, width = att.shape[0] // 4, wo.shape[1]
    return call(
        functools.partial(branch_body, flip),
        (place, att, wo),
        [SMEM] + [VMEM] * 2,
        VMEM,
        Shape((2, rows, width), low),
        after=after,
        name="branch", vmem=14,
        cost=(2e9, 4e6),
    )[0]


def attend_back_body(
    place_ref, own, near, far, both, wo_any, att_any, q_any, k_any, v_any, lse_any, cos_any, sin_any, row_ref,
    d_lin_ref, rows_s, wo_ref, att_ref, q_ref, k_ref, v_ref, lse_ref, cos_ref, sin_ref,
    kz_s, kt_s, vz_s, d_att_s, d_key_s, d_value_s, d_query_s, sems, more_sems,
):
    place = place_ref[0]
    copies = load_blocks(place, (own, near, far, both), rows_s, sems)
    copies += fetch(
        ((wo_any, wo_ref), (att_any, att_ref), (lse_any, lse_ref), (k_any, k_ref), (v_any, v_ref)), more_sems
    )
    later = fetch(((q_any, q_ref), (cos_any, cos_ref), (sin_any, sin_ref)), more_sems.at[pl.ds(5, 3)])
    wait_all(copies)
    length, q_width = att_ref.shape
    heads = q_width // HEAD_WIDTH
    pairs = heads // 2
    scale = HEAD_WIDTH**-0.5
    lane = lax.broadcasted_iota(jnp.int32, (BLOCK, LANES), 1)
    stats_t = []
    for start in range(0, length, BLOCK):
        at = pl.ds(start, BLOCK)
        d_att = dot(rows_s[at, :], wo_ref[...], NT).astype(low)
        d_att_s[at, :] = d_att
        product = d_att.astype(wide) * att_ref[at, :].astype(wide)
        stats = lse_ref[at, :]
        for h in range(heads):
            part = product[:, (h // 2) * LANES : (h // 2 + 1) * LANES]
            mine = lane // HEAD_WIDTH == h % 2
            inner = jnp.sum(jnp.where(mine, part, 0.0), axis=1, keepdims=True)
            stats = jnp.where(lane == heads + h, inner, stats)
        stats_t.append(jnp.transpose(stats))
        keys, values = spread_heads(k_ref[at, :].astype(wide)), spread_heads(v_ref[at, :].astype(wide))
        for g in range(2):
            for off in range(2):
                kz_s[2 * g + off, at, :] = keys[g][off].astype(low)
                vz_s[2 * g + off, at, :] = values[g][off].astype(low)
                kt_s[2 * g + off, :, at] = jnp.transpose(keys[g][off]).astype(low)
    d_key_s[...] = jnp.zeros_like(d_key_s)
    d_value_s[...] = jnp.zeros_like(d_value_s)
    wait_all(later)
    for i, start in enumerate(range(0, length, BLOCK)):
        at = pl.ds(start, BLOCK)
        first = max(0, start - REACH)
        span = start + BLOCK - first
        keys_at = pl.ds(first, span)
        key_id = lax.broadcasted_iota(jnp.int32, (span, BLOCK), 0) + first
        query_id = lax.broadcasted_iota(jnp.int32, (span, BLOCK), 1) + start
        allowed = (column_of(row_ref, first, span) == row_ref[:, at]) & (query_id >= key_id)
        bias = jnp.where(allowed, 0.0, NEG)
        for j in range(pairs):
            query = q_ref[at, j * LANES : (j + 1) * LANES]
            d_att = d_att_s[at, j * LANES : (j + 1) * LANES]
            total = None
            for off in range(2):
                h = 2 * j + off
                slot = 2 * (h // pairs) + off
                scores = dot(kz_s[slot, keys_at, :], query, NT) + bias
                probs = jnp.exp(scores - stats_t[i][h : h + 1, :])
                d_probs = dot(vz_s[slot, keys_at, :], d_att, NT)
                d_scores = probs * (d_probs - stats_t[i][heads + h : heads + h + 1, :])
                d_scores = d_scores.astype(low)
                d_value_s[slot, keys_at, :] += dot(probs.astype(low), d_att, NN)
                d_key_s[slot, keys_at, :] += dot(d_scores, query, NN)
                part = dot(kt_s[slot, :, keys_at], d_scores, NN)
                total = part if total is None else total + part
            d_query_s[j * LANES : (j + 1) * LANES, at] = total
    for start in range(0, length, BLOCK):
        at = pl.ds(start, BLOCK)
        cos, sin = cos_ref[at, :], sin_ref[at, :]
        for j in range(pairs):
            part = jnp.transpose(d_query_s[j * LANES : (j + 1) * LANES, at]) * scale
            turned = part * cos - half_turn(part) * sin
            d_lin_ref[at, j * LANES : (j + 1) * LANES] = turned.astype(low)
        both_of = []
        for ref in (d_key_s, d_value_s):
            first_head = ref[0, at, :] + pltpu.roll(ref[1, at, :], HEAD_WIDTH, 1)
            second_head = ref[3, at, :] + pltpu.roll(ref[2, at, :], HEAD_WIDTH, 1)
            both_of.append(jnp.where(lane < HEAD_WIDTH, first_head, second_head))
        d_key, d_value = both_of
        d_lin_ref[at, q_width : q_width + LANES] = (d_key * cos - half_turn(d_key) * sin).astype(low)
        d_lin_ref[at, q_width + LANES :] = d_value.astype(low)


def attend_back(place, blocks, wo, att, q, k, v, lse, cos, sin, segs, after):
    rows, width = blocks[0].shape
    length, q_width = att.shape
    return call(
        attend_back_body,
        (place, *blocks, wo, att, q, k, v, lse, cos, sin, segs.reshape(1, length)),
        [SMEM] + [ANY] * 12 + [VMEM],
        VMEM,
        Shape((length, q_width + 2 * LANES), low),
        [
            pltpu.VMEM((length, width), low),
            pltpu.VMEM(wo.shape, low),
            pltpu.VMEM(att.shape, low),
            pltpu.VMEM(q.shape, low),
            pltpu.VMEM(k.shape, low),
            pltpu.VMEM(v.shape, low),
            pltpu.VMEM(lse.shape, wide),
            pltpu.VMEM(cos.shape, wide),
            pltpu.VMEM(sin.shape, wide),
            pltpu.VMEM((4, length, LANES), low),
            pltpu.VMEM((4, LANES, length), low),
            pltpu.VMEM((4, length, LANES), low),
            pltpu.VMEM((length, q_width), low),
            pltpu.VMEM((4, length, LANES), wide),
            pltpu.VMEM((4, length, LANES), wide),
            pltpu.VMEM((q_width, length), wide),
            pltpu.SemaphoreType.DMA((4,)),
            pltpu.SemaphoreType.DMA((8,)),
        ],
        after=after,
        name="attend_back", vmem=62,
        cost=(15e-6 * 1.1e15, 12e6),
    )


def split_add_body(place_ref, mine_ref, got_ref, kept_ref, sent_ref):
    far = place_ref[0] // 2
    kept_ref[...] = (mine_ref[far].astype(wide) + got_ref[far].astype(wide)).astype(low)
    sent_ref[...] = (mine_ref[1 - far].astype(wide) + got_ref[1 - far].astype(wide)).astype(low)


def tensor_scatter(place, mine, other, after):
    (kept, sent), token = split_add(place, mine, swap(other, "tensor", 1), after)
    return kept, swap(sent, "tensor", 2), token


def split_add(place, mine, got, after=()):
    rows, width = mine.shape[1:]
    return call(
        split_add_body,
        (place, mine, got),
        [SMEM] + [pl.BlockSpec((2, rows // 2, width), lambda i: (0, i, 0))] * 2,
        [pl.BlockSpec((rows // 2, width), lambda i: (i, 0))] * 2,
        [pltpu.HBM((rows, width), low)] * 2,
        grid=(2,),
        after=after,
        name="split_add", vmem=12,
        cost=(1e9, 6e6),
    )


def expert_body(pieces, cuts, local, with_mixed, *refs):
    rows_refs = refs[:pieces]
    up_refs = refs[pieces : 2 * pieces]
    d_act_ref, sel_ref, router_ref, gate_ref, up_w_ref = refs[2 * pieces : 2 * pieces + 5]
    outs = refs[2 * pieces + 5 :]
    if with_mixed:
        down_ref, outs = outs[0], outs[1:]
        mixed_refs, outs = outs[:pieces], outs[pieces:]
        mixed_s, outs = outs[-1], outs[:-1]
    d_rows_refs, outs = outs[:pieces], outs[pieces:]
    hidden_ref, d_gate_ref, d_up_ref, rows_s, mask_s, d_rows_s, gates_s, d_gates_s, sems = outs
    step = pl.program_id(0)
    width = rows_s.shape[1]

    @pl.when(step == 0)
    def _():
        copies, start = [], 0
        for i in range(pieces):
            at = pl.ds(start, rows_refs[i].shape[0])
            start += rows_refs[i].shape[0]
            copies.append(pltpu.make_async_copy(rows_refs[i], rows_s.at[at, :], sems.at[i]))
            copies.append(
                pltpu.make_async_copy(
                    up_refs[i].at[:, pl.ds(width, LANES)], mask_s.at[at, :], sems.at[pieces + i]
                )
            )
        for copy in copies:
            copy.start()
        wait_all(copies)
        chosen = mask_s[...] > 0.0
        logits = jnp.where(chosen, dot(rows_s[...], router_ref[...], NT), NEG)
        largest = jnp.max(logits, axis=1, keepdims=True)
        shifted = jnp.where(chosen, jnp.exp(logits - largest), 0.0)
        gates_s[...] = shifted / jnp.sum(shifted, axis=1, keepdims=True)
        d_gates_s[...] = jnp.zeros_like(d_gates_s)

    expert = step // cuts
    pick = sel_ref[0:1, :]
    for e in range(1, local):
        pick = jnp.where(expert == e, sel_ref[e : e + 1, :], pick)
    gate = jnp.sum(gates_s[...] * pick, axis=1, keepdims=True)
    rows = rows_s[...]
    gate_w, up_w = gate_ref[0], up_w_ref[0]
    gate_pre = dot(rows, gate_w, NN)
    up_pre = dot(rows, up_w, NN)
    d_act = d_act_ref[...].astype(wide)
    sig = 1.0 / (1.0 + jnp.exp(-gate_pre))
    act = gate_pre * sig
    hidden = act * up_pre
    d_gates_s[...] += jnp.sum(hidden * d_act, axis=1, keepdims=True) * pick
    hidden = (gate * hidden).astype(low)
    d_act = gate * d_act
    d_gate = (d_act * up_pre * sig * (1.0 + gate_pre * (1.0 - sig))).astype(low)
    d_up = (d_act * act).astype(low)
    hidden_ref[...] = hidden
    d_gate_ref[...] = d_gate
    d_up_ref[...] = d_up
    sums = [(d_rows_s, dot(d_gate, gate_w, NT) + dot(d_up, up_w, NT))]
    if with_mixed:
        sums.append((mixed_s, dot(hidden, down_ref[0], NN)))

    @pl.when(step == 0)
    def _():
        for ref, value in sums:
            ref[...] = value

    @pl.when(step > 0)
    def _():
        for ref, value in sums:
            ref[...] += value

    @pl.when(step == pl.num_programs(0) - 1)
    def _():
        lane = lax.broadcasted_iota(jnp.int32, d_gates_s.shape, 1)
        d_gates = d_gates_s[...]
        d_gates = jnp.where(lane < LANES // 2, d_gates, pltpu.roll(d_gates, LANES // 2, 1))
        rounded = d_gates.astype(low).astype(wide)
        d_gates = jnp.where(lane < LANES // 2, rounded, d_gates - rounded).astype(low)
        start = 0
        for i, d_rows_ref in enumerate(d_rows_refs):
            size = d_rows_ref.shape[0]
            d_rows_ref[:, :width] = d_rows_s[start : start + size, :].astype(low)
            d_rows_ref[:, width:] = d_gates[start : start + size, :]
            if with_mixed:
                mixed_refs[i][...] = mixed_s[start : start + size, :].astype(low)
            start += size


def expert_block(rows_list, ups_list, d_act, sel, w_router, w_gate, w_up, w_down, with_mixed, after=()):
    pieces = len(rows_list)
    sizes = [rows.shape[0] for rows in rows_list]
    rows = sum(sizes)
    local, width, ff = w_gate.shape
    cut = min(512, ff)
    cuts = ff // cut
    whole = lambda shape: pl.BlockSpec(shape, lambda j: (0,) * len(shape))
    across = pl.BlockSpec((1, width, cut), lambda j: (j // cuts, 0, j % cuts))
    tall = pl.BlockSpec((1, cut, width), lambda j: (j // cuts, j % cuts, 0))
    part = pl.BlockSpec((rows, cut), lambda j: (0, j))
    mixed_out = with_mixed * pieces
    outs, token = call(
        functools.partial(expert_body, pieces, cuts, local, with_mixed),
        (*rows_list, *ups_list, d_act, sel, w_router, w_gate, w_up) + (w_down,) * with_mixed,
        [ANY] * (2 * pieces)
        + [part, whole((local, LANES)), whole((LANES, width)), across, across]
        + [tall] * with_mixed,
        [whole((size, width)) for size in sizes[:mixed_out]]
        + [whole((size, width + LANES)) for size in sizes]
        + [part, part, part],
        [pltpu.HBM((size, width), low) for size in sizes[:mixed_out]]
        + [pltpu.HBM((size, width + LANES), low) for size in sizes]
        + [pltpu.HBM((rows, local * ff), low)] * 3,
        [
            pltpu.VMEM((rows, width), low),
            pltpu.VMEM((rows, LANES), low),
            pltpu.VMEM((rows, width), wide),
            pltpu.VMEM((rows, LANES), wide),
            pltpu.VMEM((rows, LANES), wide),
            pltpu.SemaphoreType.DMA((2 * pieces,)),
        ]
        + [pltpu.VMEM((rows, width), wide)] * with_mixed,
        grid=(local * cuts,),
        after=after,
        name="experts", vmem=40,
        cost=(14 * rows * width * local * ff, 6 * local * width * ff + 8 * rows * width),
    )
    return (
        outs[mixed_out : mixed_out + pieces], outs[:mixed_out], outs[mixed_out + pieces :], token
    )


def d_act_body(pieces, *refs):
    up_refs = refs[:pieces]
    down_ref, out_ref, ups_s, sems = refs[pieces:]

    @pl.when(pl.program_id(0) == 0)
    def _():
        copies, start = [], 0
        for i, ref in enumerate(up_refs):
            size = ref.shape[0]
            copies.append(
                pltpu.make_async_copy(
                    ref.at[:, pl.ds(0, ups_s.shape[1])], ups_s.at[pl.ds(start, size), :], sems.at[i]
                )
            )
            start += size
        for copy in copies:
            copy.start()
        wait_all(copies)

    out_ref[...] = dot(ups_s[...], down_ref[0], NT).astype(low)


def d_act_block(ups_list, w_down, after=()):
    local, ff, width = w_down.shape
    rows = sum(ups.shape[0] for ups in ups_list)
    return call(
        functools.partial(d_act_body, len(ups_list)),
        (*ups_list, w_down),
        [ANY] * len(ups_list) + [pl.BlockSpec((1, ff, width), lambda e: (e, 0, 0))],
        pl.BlockSpec((rows, ff), lambda e: (0, e)),
        Shape((rows, local * ff), low),
        [pltpu.VMEM((rows, width), low), pltpu.SemaphoreType.DMA((len(ups_list),))],
        grid=(local,),
        after=after,
        name="d_act", vmem=20,
        cost=(5e8, 1e6),
    )


def outer_body(pieces, seconds, split, place_ref, *refs):
    first_refs = refs[:pieces]
    second_refs = refs[pieces : pieces + seconds]
    mine_ref, other_ref, first_s, second_s, first_sems, second_sems = refs[pieces + seconds :]
    core = place_ref[0] % 2
    step = pl.program_id(0)
    cut = first_s.shape[2]
    width = second_s.shape[1]

    def load(at, slot):
        copies, start = [], 0
        for i, ref in enumerate(first_refs):
            size = ref.shape[0]
            copies.append(
                pltpu.make_async_copy(
                    ref.at[:, pl.ds(pl.multiple_of(at * cut, cut), cut)],
                    first_s.at[slot, pl.ds(start, size), :],
                    first_sems.at[slot, i],
                )
            )
            start += size
        return copies

    slot = step % 2

    @pl.when(step == 0)
    def _():
        for copy in load(0, 0):
            copy.start()
        copies, start = [], 0
        for i, ref in enumerate(second_refs):
            size = ref.shape[0]
            copies.append(
                pltpu.make_async_copy(
                    ref.at[:, pl.ds(0, width)], second_s.at[pl.ds(start, size), :], second_sems.at[i]
                )
            )
            start += size
        for copy in copies:
            copy.start()
        wait_all(copies)

    @pl.when(step + 1 < pl.num_programs(0))
    def _():
        for copy in load(step + 1, 1 - slot):
            copy.start()

    wait_all(load(step, slot))
    product = dot(first_s[slot], second_s[...], TN).astype(low)
    if split == 1:

        @pl.when(step == core)
        def _():
            mine_ref[...] = product

        @pl.when(step != core)
        def _():
            other_ref[...] = product
    else:
        first, last = product[:, : width // 2], product[:, width // 2 :]
        mine_ref[...] = jnp.where(core == 0, first, last)
        other_ref[...] = jnp.where(core == 0, last, first)


def outer_products(place, first, second, first_width, second_width, split, after=()):
    cut = 512
    steps = first_width // cut
    rows = sum(piece.shape[0] for piece in first)
    if split == 1:
        out_shape = Shape((cut, second_width), low)
        out_spec = pl.BlockSpec((cut, second_width), lambda i: (0, 0))
    else:
        out_shape = Shape((first_width, second_width // 2), low)
        out_spec = pl.BlockSpec((cut, second_width // 2), lambda i: (i, 0))
    return call(
        functools.partial(outer_body, len(first), len(second), split),
        (place, *first, *second),
        [SMEM] + [ANY] * (len(first) + len(second)),
        [out_spec] * 2,
        [out_shape] * 2,
        [
            pltpu.VMEM((2, rows, cut), low),
            pltpu.VMEM((rows, second_width), low),
            pltpu.SemaphoreType.DMA((2, len(first))),
            pltpu.SemaphoreType.DMA((len(second),)),
        ],
        grid=(steps,),
        after=after,
        name="outer_products", vmem=24 if rows <= 4096 else 58,
        cost=(3.5 * rows * first_width * second_width, 12e6),
    )


def ring_parts_of(count, ids_ref, flat_s, outs):
    part = flat_s.shape[0] // count
    for o, ref in enumerate(outs):
        size = ref.shape[0]
        if o < count // 2:
            at = ids_ref[o] * part
        elif o > count // 2 + 1:
            at = ids_ref[o - 1] * part
        else:
            at = ids_ref[count // 2] * part + (o - count // 2) * size
        ref[...] = flat_s[pl.ds(pl.multiple_of(at, size), size), :]


def ring_part_sizes(count, flat):
    part = flat // count
    return [part] * (count // 2) + [part // 2] * 2 + [part] * (count // 2 - 1)


def small_rows(count):
    return 4 * count


def ring_part_list(count, outs):
    half = count // 2
    return list(outs[:half]) + [tuple(outs[half : half + 2])] + list(outs[half + 2 :])


def head_grads_body(count, place_ref, ids_ref, *refs):
    rows_refs, d_refs, late_refs = refs[:4], refs[4:8], refs[8:13]
    gain_ref, gain_ffn_ref, router_ref = refs[13:16]
    outs = refs[16 : 16 + count + 1]
    rows_s, d_s, flat_s, small_s, *loaded, sems, d_sems, late_sems = refs[17 + count :]
    d_lin_ref, wq_ref, wk_ref, wv_ref, att_ref = loaded
    lin_copies = fetch(tuple(zip(late_refs[:1], loaded[:1])), late_sems)
    small_s[...] = jnp.zeros_like(small_s)
    small_s[:1, :] = gain_ffn_ref[...]
    small_s[2 : 2 + router_ref.shape[0], :] = router_ref[...]
    copies = load_blocks(place_ref[0], rows_refs, rows_s, sems)
    weight_copies = fetch(tuple(zip(late_refs[1:4], loaded[1:4])), late_sems.at[pl.ds(1, 3)])
    d_copies = load_blocks(place_ref[0], d_refs, d_s, d_sems)
    d_copies += fetch(tuple(zip(late_refs[4:], loaded[4:])), late_sems.at[pl.ds(4, 1)])
    wait_all(lin_copies)
    wait_all(copies)
    q_width, kv_width = wq_ref.shape[1], wk_ref.shape[1]
    lin_width = d_lin_ref.shape[1]
    width = rows_s.shape[1]
    for at in range(0, width, 512):
        here = pl.ds(at, 512)
        grads = dot(rows_s[:, here], d_lin_ref[...], TN)
        for c in range(0, lin_width, LANES):
            row = c // LANES * width + at
            flat_s[row : row + 512, :] = grads[:, c : c + LANES].astype(low)
        if at == 0:
            wait_all(weight_copies)
        inner = jnp.sum(wq_ref[here, :].astype(wide) * grads[:, :q_width], axis=1, keepdims=True)
        inner += jnp.sum(
            wk_ref[here, :].astype(wide) * grads[:, q_width : q_width + kv_width], axis=1, keepdims=True
        )
        inner += jnp.sum(
            wv_ref[here, :].astype(wide) * grads[:, q_width + kv_width :], axis=1, keepdims=True
        )
        inner = jnp.transpose(jnp.broadcast_to(inner, (512, LANES)))[:1]
        small_s[1:2, here] = inner / gain_ref[here].reshape(1, -1)
    wait_all(d_copies)
    base = lin_width // LANES * width
    for at in range(0, width, 512):
        grads = dot(att_ref[...], d_s[:, at : at + 512], TN).astype(low)
        for c in range(0, 512, LANES):
            row = base + (at + c) // LANES * q_width
            flat_s[row : row + q_width, :] = grads[:, c : c + LANES]
    base = base + width // LANES * q_width
    size = small_s.shape[0]
    for c in range(0, width, LANES):
        row = base + c // LANES * size
        flat_s[row : row + size, :] = small_s[:, c : c + LANES].astype(low)
    row = base + width // LANES * size
    flat_s[row:, :] = jnp.zeros((flat_s.shape[0] - row, LANES), low)
    ring_parts_of(count, ids_ref, flat_s, outs)


def head_grads(
    place, ids, rows_blocks, d_blocks, att, d_lin, wq, wk, wv, gain, gain_ffn_part, router_part, after=()
):
    count = lax.axis_size("dp")
    rows, width = rows_blocks[0].shape
    length, lin_width = d_lin.shape
    flat = width * (lin_width + att.shape[1]) // LANES + 64 * count
    outs, token = call(
        functools.partial(head_grads_body, count),
        (place, ids, *rows_blocks, *d_blocks, d_lin, wq, wk, wv, att, gain, gain_ffn_part, router_part),
        [SMEM, SMEM] + [ANY] * 13 + [VMEM] * 3,
        [VMEM] * (count + 1),
        [Shape((size, LANES), low) for size in ring_part_sizes(count, flat)],
        [
            pltpu.VMEM((length, width), low),
            pltpu.VMEM((length, width), low),
            pltpu.VMEM((flat, LANES), low),
            pltpu.VMEM((small_rows(count), width), wide),
            *[pltpu.VMEM(array.shape, low) for array in (d_lin, wq, wk, wv, att)],
            pltpu.SemaphoreType.DMA((4,)),
            pltpu.SemaphoreType.DMA((4,)),
            pltpu.SemaphoreType.DMA((5,)),
        ],
        after=after,
        name="head_grads", vmem=62,
        cost=(8e-6 * 1.1e15, 12e6),
    )
    return ring_part_list(count, outs), token


def ring_sum_body(own_ref, up_ref, down_ref, out_ref):
    out_ref[...] = (
        own_ref[...].astype(wide) + up_ref[...].astype(wide) + down_ref[...].astype(wide)
    ).astype(low)


def ring_total(parts, before, then, last, later):
    half = len(parts) // 2
    up, down = ring_scatter(
        [parts[len(parts) - 1 - i] for i in range(half - 1)],
        [parts[1 + i] for i in range(half - 1)],
        parts[half],
        before,
        then,
    )
    total, _ = call(
        ring_sum_body, (parts[0], up, down), [VMEM] * 3, VMEM, Shape(parts[0].shape, low),
        after=last(), name="ring_sum", cost=(1e8, 1e6),
    )
    below, above, far = ring_gather(total, ties=later())
    return [total] + above + list(far) + below[::-1]


def head_place_body(count, ids_ref, *refs):
    blocks = refs[: count + 1]
    grads, small_ref, flat_s = refs[count + 1 : -2], refs[-2], refs[-1]
    part = flat_s.shape[0] // count
    for o, ref in enumerate(blocks):
        size = ref.shape[0]
        if o < count // 2:
            at = ids_ref[o] * part
        elif o > count // 2 + 1:
            at = ids_ref[o - 1] * part
        else:
            at = ids_ref[count // 2] * part + (o - count // 2) * size
        flat_s[pl.ds(pl.multiple_of(at, size), size), :] = ref[...]
    row = 0
    for ref in grads:
        rows, columns = ref.shape
        for c in range(0, columns, LANES):
            ref[:, c : c + LANES] = flat_s[row : row + rows, :].astype(wide)
            row += rows
    rows, columns = small_ref.shape
    for c in range(0, columns, LANES):
        small_ref[:, c : c + LANES] = flat_s[row : row + rows, :].astype(wide)
        row += rows


def head_place(ids, blocks, shapes, small_shape):
    count = lax.axis_size("dp")
    flat = sum(rows * columns for rows, columns in shapes) // LANES + 64 * count
    return call(
        functools.partial(head_place_body, count),
        (ids, *blocks),
        [SMEM] + [VMEM] * (count + 1),
        [VMEM] * (len(shapes) + 1),
        [Shape(shape, wide) for shape in (*shapes, small_shape)],
        [pltpu.VMEM((flat, LANES), low)],
        name="head_place", vmem=24,
        cost=(1e9, 6e6),
    )[0]


def add_body(first_ref, second_ref, out_ref):
    out_ref[...] = (first_ref[...].astype(wide) + second_ref[...].astype(wide)).astype(low)


def add_rows(first, second, after=()):
    return call(
        add_body, (first, second), [VMEM] * 2, VMEM, Shape(first.shape, low), after=after,
        name="add_rows", cost=(1e8, 3e6),
    )


def place_quarters_body(place_ref, *refs):
    del place_ref
    pieces, out_ref = refs[:4], refs[4]
    step = pl.program_id(0)
    for i, ref in enumerate(pieces):

        @pl.when(step == i)
        def _():
            out_ref[0] = ref[...].astype(wide)


def place_quarters(place, pieces):
    rows, columns = pieces[0].shape
    fixed = pl.BlockSpec((rows, columns), lambda i, place_ref: (0, 0))
    out = pl.BlockSpec(
        (1, rows, columns),
        lambda i, place_ref: (i // 2 ^ place_ref[0] % 2, i % 2 ^ place_ref[0] // 2, 0),
    )
    result, token = pl.pallas_call(
        place_quarters_body,
        grid_spec=pltpu.PrefetchScalarGridSpec(
            num_scalar_prefetch=1, grid=(4,), in_specs=[fixed] * 4, out_specs=[out, VMEM]
        ),
        out_shape=[pltpu.HBM((2, 2 * rows, columns), wide), pltpu.VMEM(TOKEN, wide)],
        compiler_params=pltpu.CompilerParams(vmem_limit_bytes=16 * MEGABYTE),
        cost_estimate=pl.CostEstimate(flops=10**8, bytes_accessed=10**7, transcendentals=0),
        name="place_quarters",
    )(place, *pieces)
    return result, Token(token)


def lin_back_body(place_ref, d_lin_ref, wq_ref, wk_ref, wv_ref, mine_ref, other_ref):
    rows = mine_ref.shape[1]
    core = place_ref[0] % 2
    q_width, kv_width = wq_ref.shape[1], wk_ref.shape[1]
    for x in range(2):
        for ref, c in ((other_ref, 1 - core), (mine_ref, core)):
            at = pl.ds(pl.multiple_of((2 * x + c) * rows, rows), rows)
            total = dot(d_lin_ref[at, :q_width], wq_ref[...], NT)
            total += dot(d_lin_ref[at, q_width : q_width + kv_width], wk_ref[...], NT)
            total += dot(d_lin_ref[at, q_width + kv_width :], wv_ref[...], NT)
            ref[x] = total.astype(low)


def lin_back(place, d_lin, wq, wk, wv, after):
    rows, width = d_lin.shape[0] // 4, wq.shape[0]
    return call(
        lin_back_body,
        (place, d_lin, wq, wk, wv),
        [SMEM] + [VMEM] * 4,
        [VMEM] * 2,
        [Shape((2, rows, width), low)] * 2,
        after=after,
        name="lin_back", vmem=20,
        cost=(4e-6 * 1.1e15, 9e6),
    )


def first_norm_body(tokens_ref, gain_ref, cotangent_ref, routes_ref, normed_ref, ups_ref):
    width = cotangent_ref.shape[1]
    routes = routes_ref[...]
    lane = lax.broadcasted_iota(jnp.int32, (LANES, routes.shape[1]), 0)
    chosen = routes[:1, :] == lane
    for k in range(1, routes.shape[0]):
        chosen = chosen | (routes[k : k + 1, :] == lane)
    ups_ref[:, :width] = cotangent_ref[...]
    ups_ref[:, width:] = jnp.transpose(jnp.where(chosen, 1.0, 0.0)).astype(low)
    inputs = tokens_ref[...].astype(wide)
    inverse = lax.rsqrt(jnp.mean(inputs * inputs, axis=1, keepdims=True) + EPS)
    normed_ref[...] = (inputs * inverse * gain_ref[...].reshape(1, -1)).astype(low)


def second_norm_body(tokens_ref, kept_ref, got_ref, gain_ref, residual_ref, normed_ref):
    residual = tokens_ref[...].astype(wide) + (kept_ref[...].astype(wide) + got_ref[...].astype(wide))
    inverse = lax.rsqrt(jnp.mean(residual * residual, axis=1, keepdims=True) + EPS)
    residual_ref[...] = residual
    normed_ref[...] = (residual * inverse * gain_ref[...].reshape(1, -1)).astype(low)


def middle_body(
    own_ref, up_ref, down_ref, residual_ref, normed_ref, ups_ref, router_ref, gain_ref,
    d_residual_ref, d_low_ref, gain_out, router_out,
):
    width = residual_ref.shape[1]
    total = own_ref[...].astype(wide) + up_ref[...].astype(wide) + down_ref[...].astype(wide)
    d_gates = total[:, width:]
    d_gates = d_gates + pltpu.roll(d_gates, LANES // 2, 1)
    lane = lax.broadcasted_iota(jnp.int32, d_gates.shape, 1)
    chosen = ups_ref[:, width:] > 0.0
    normed = normed_ref[...]
    logits = jnp.where(chosen, dot(normed, router_ref[...], NT), NEG)
    largest = jnp.max(logits, axis=1, keepdims=True)
    shifted = jnp.where(chosen, jnp.exp(logits - largest), 0.0)
    gates = shifted / jnp.sum(shifted, axis=1, keepdims=True)
    inner = jnp.sum(gates * d_gates, axis=1, keepdims=True)
    d_logits = (gates * (d_gates - inner)).astype(low)
    router_part = dot(d_logits, normed, TN)[: router_out.shape[0]]
    d_normed = total[:, :width] + dot(d_logits, router_ref[...], NN)
    residual = residual_ref[...]
    inverse = lax.rsqrt(jnp.mean(residual * residual, axis=1, keepdims=True) + EPS)
    scaled = d_normed * gain_ref[...].reshape(1, -1)
    mean = jnp.mean(scaled * residual, axis=1, keepdims=True)
    upstream = ups_ref[:, :width].astype(wide)
    d_residual = upstream + inverse * scaled - residual * (inverse * inverse * inverse * mean)
    gain_part = jnp.sum(d_normed * residual * inverse, axis=0, keepdims=True)

    @pl.when(pl.program_id(0) == 0)
    def _():
        gain_out[...] = gain_part
        router_out[...] = router_part

    @pl.when(pl.program_id(0) > 0)
    def _():
        gain_out[...] += gain_part
        router_out[...] += router_part

    d_residual_ref[...] = d_residual
    d_low_ref[...] = d_residual.astype(low)


def last_body(tokens_ref, kept_ref, got_ref, d_residual_ref, gain_ref, out_ref):
    inputs = tokens_ref[...].astype(wide)
    inverse = lax.rsqrt(jnp.mean(inputs * inputs, axis=1, keepdims=True) + EPS)
    scaled = (kept_ref[...].astype(wide) + got_ref[...].astype(wide)) * gain_ref[...].reshape(1, -1)
    mean = jnp.mean(scaled * inputs, axis=1, keepdims=True)
    d_inputs = inverse * scaled - inputs * (inverse * inverse * inverse * mean)
    out_ref[...] = (d_inputs + d_residual_ref[...]).astype(low)


def on_device(
    tokens,
    gain_attn,
    query_weight,
    key_weight,
    value_weight,
    w_output,
    gain_ffn,
    w_router,
    w_gate,
    w_up,
    w_down,
    segments,
    routes,
    cotangent,
):
    rows_dev, width = tokens.shape
    data_count = lax.axis_size("dp")
    half_count = data_count // 2
    local_experts, _, ff = w_gate.shape
    expert_count = local_experts * data_count
    q_width, kv_width = query_weight.shape[1], key_weight.shape[1]
    place = lax.axis_index("tensor").astype(jnp.int32).reshape(1)
    ids = ring_places()
    cos, sin = rope_tables(segments.shape[1])
    gain_one, gain_two = gain_attn, gain_ffn
    lanes = jnp.arange(LANES, dtype=jnp.int32)
    own_experts = lax.axis_index("dp") * local_experts + jnp.arange(local_experts, dtype=jnp.int32)
    sel = (own_experts[:, None] == lanes[None, :]).astype(wide)
    router = jnp.pad(w_router.T, ((0, LANES - expert_count), (0, 0)))

    half_rows = rows_dev // 2
    row_spec = pl.BlockSpec((half_rows, width), lambda i: (i, 0))
    wide_spec = pl.BlockSpec((half_rows, width + LANES), lambda i: (i, 0))
    gain_spec = pl.BlockSpec((width,), lambda i: (0,))
    sum_spec = pl.BlockSpec((1, width), lambda i: (0, 0))
    (normed_one, ups), _ = call(
        first_norm_body,
        (tokens, gain_one, cotangent, routes.T),
        [row_spec, gain_spec, row_spec, pl.BlockSpec((routes.shape[1], half_rows), lambda i: (0, i))],
        [row_spec, wide_spec],
        [Shape((rows_dev, width), low), Shape((rows_dev, width + LANES), low)],
        grid=(2,), name="first_norm", cost=(1e9, 2e6), vmem=60,
    )
    d_acts = [d_act_block((ups,), w_down)]

    def early_acts(below, above):
        for pair in list(zip(below, above))[: half_count - 2]:
            d_acts.append(d_act_block(pair, w_down))
        return [token for _, token in d_acts]

    ups_below, ups_above, ups_far = ring_gather(ups, early_acts)
    rows_blocks = tensor_blocks(normed_one)
    ups_groups = [(ups,)] + list(zip(ups_below, ups_above)) + [ups_far]
    d_acts += [d_act_block(group, w_down) for group in ups_groups[-2:]]
    (att, q, k, v, lse), _ = attend(
        place, rows_blocks, query_weight, key_weight, value_weight, cos, sin, segments,
        after=(ups_below[0], ups_above[0]),
    )
    other = branch_half(place, att, w_output, True, after=(ups_below[1], ups_above[1]))
    mine = branch_half(place, att, w_output, False)
    kept, got, _ = tensor_scatter(place, mine, other, after=())
    (residual, normed_two), _ = call(
        second_norm_body, (tokens, kept, got, gain_two), [row_spec] * 3 + [gain_spec], [row_spec] * 2,
        [pltpu.HBM((rows_dev, width), wide), pltpu.HBM((rows_dev, width), low)],
        after=(ups_below[-1], ups_above[-1]), grid=(2,), name="second_norm", cost=(1e9, 4e6),
    )
    rows_below, rows_above, rows_far = ring_gather(normed_two, lambda below, above: ())
    rows_groups = [(normed_two,)] + list(zip(rows_below, rows_above)) + [rows_far]
    done = []
    for index, (rows, up) in enumerate(zip(rows_groups, ups_groups)):
        after = () if not done else (done[-1][3],)
        if len(done) in (1, 2):
            after += (d_acts[len(done) - 3][1],)
        done.append(
            expert_block(
                rows, up, d_acts[index][0], sel, router, w_gate, w_up, w_down,
                True, after,
            )
        )
    rows_all = [piece for rows in rows_groups for piece in rows]
    ups_all = [piece for up in ups_groups for piece in up]
    hidden_all, d_gate_all, d_up_all = ([outs[2][i] for outs in done] for i in range(3))
    inner = local_experts * ff
    split_rows = {"down": ff // 2, "gate": width // 2, "up": width // 2}
    grads = {
        "down": outer_products(place, hidden_all, ups_all, inner, width, 1)[0],
        "gate": outer_products(place, rows_all, d_gate_all, width, inner, 2)[0],
        "up": outer_products(place, rows_all, d_up_all, width, inner, 2)[0],
    }
    mixed_parts = [outs[1] for outs in done]
    mixed_steps = ring_steps(
        [parts[0] for parts in mixed_parts[1:-1]], [parts[1] for parts in mixed_parts[1:-1]], mixed_parts[-1]
    )
    next(mixed_steps)
    first_mixed, _, _ = ring_step(mixed_steps)
    names = ("down", "gate", "up")
    halves, half_tokens, quarters, nears, gots = {}, {}, {}, {}, {}

    def quarter(name, after=()):
        got = gots.get(name)
        got = swap(halves[name][1], "tensor", 2) if got is None else got
        quarters[name], token = add_rows(halves[name][0], got, after)
        if name != "up":
            nears[name] = swap(quarters[name], "tensor", 1)
        return token

    def before(index):
        if index > 2:
            return (), ()
        after = (half_tokens[names[index - 1]],) if index else (first_mixed,)
        if index == 2:
            after += (quarter("down"),)
        return after, (grads[names[index]][1],)

    def then(index, _, held):
        if index > 2:
            return
        name = names[index]
        mine, other = (array.reshape(2, split_rows[name], -1) for array in (grads[name][0], held[0]))
        halves[name], half_tokens[name] = split_add(place, mine, swap(other, "tensor", 1))

    d_rows_up, d_rows_down = ring_scatter(
        [outs[0][0] for outs in done[1:-1]], [outs[0][1] for outs in done[1:-1]], done[-1][0], before, then
    )
    gots["gate"] = swap(halves["gate"][1], "tensor", 2)
    (d_residual, d_low, gain_ffn_part, router_part), _ = call(
        middle_body,
        (done[0][0][0], d_rows_up, d_rows_down, residual, normed_two, ups, router, gain_two),
        [wide_spec] * 3
        + [row_spec] * 2
        + [wide_spec, pl.BlockSpec((LANES, width), lambda i: (0, 0)), gain_spec],
        [row_spec] * 2 + [sum_spec, pl.BlockSpec((expert_count, width), lambda i: (0, 0))],
        [
            pltpu.HBM((rows_dev, width), wide),
            pltpu.HBM((rows_dev, width), low),
            Shape((1, width), wide),
            Shape((expert_count, width), wide),
        ],
        grid=(2,),
        after=(gots["gate"], ids),
        name="middle", vmem=62, cost=(4e-6 * 1.1e15, 4e6),
    )
    d_near, d_far = swap(d_low, "tensor", 1), swap(d_low, "tensor", 2)
    quarter("gate")
    pieces = {}

    def gather_pieces(name):
        second = swap(quarters[name], "tensor", 2)
        pieces[name] = (
            quarters[name],
            second,
            nears[name] if name in nears else swap(quarters[name], "tensor", 1),
            swap(second, "tensor", 1),
        )

    mark, (halves["up"][1],), _ = ring_step(mixed_steps, (), (halves["up"][1],))
    for _ in range(half_count - 4):
        mark, _, _ = ring_step(mixed_steps)
    (d_far,) = hold((d_far,), (mark,))
    d_blocks = (d_low, d_near, d_far, swap(d_far, "tensor", 1))
    d_lin, d_lin_token = attend_back(
        place, d_blocks, w_output, att, q, k, v, lse, cos, sin, segments,
        after=(mark, nears["down"], nears["gate"]),
    )
    mark, (quarters["down"],), (mixed_up, mixed_down) = ring_step(
        mixed_steps, (d_lin_token,), (quarters["down"],), 62
    )
    gather_pieces("down")
    parts, parts_token = head_grads(
        place, ids, rows_blocks, d_blocks, att, d_lin, query_weight, key_weight, value_weight, gain_one,
        gain_ffn_part, router_part, after=(mark,),
    )
    up_token = quarter("up", (parts_token,))
    (mine, other), lin_token = lin_back(
        place, d_lin, query_weight, key_weight, value_weight, after=(parts_token,)
    )
    sums, totals = {}, {}

    def before_total(index):
        if index == 0:
            return (mixed_up, mixed_down, pieces["down"][1], up_token), (other, quarters["gate"])
        if index == 1:
            return (totals["down"][1], sums["token"]), (quarters["up"],)
        if index == 2:
            return (pieces["gate"][1],), ()
        return (), ()

    def then_total(index, token, held):
        if index == 0:
            quarters["gate"] = held[1]
            gather_pieces("gate")
            totals["down"] = place_quarters(place, pieces["down"])
            sums["kept"], sums["got"], sums["token"] = tensor_scatter(place, mine, held[0], ())
        if index == 1:
            (quarters["up"],) = held
            gather_pieces("up")
        if index == 2:
            totals["gate"] = place_quarters(place, pieces["gate"])

    blocks = ring_total(parts, before_total, then_total, lambda: (totals["gate"][1],), lambda: (sums["got"],))
    totals["up"] = place_quarters(place, pieces["up"])
    kept, got = sums["kept"], sums["got"]
    mixed = (
        residual + mixed_parts[0][0].astype(wide) + mixed_up.astype(wide) + mixed_down.astype(wide)
    ).astype(low)
    grad_tokens, _ = call(
        last_body, (tokens, kept, got, d_residual, gain_one), [row_spec] * 4 + [gain_spec], row_spec,
        Shape((rows_dev, width), low), grid=(2,), name="last", cost=(1e9, 4e6),
    )
    grad_q, grad_k, grad_v, grad_o, small = head_place(
        ids, blocks, [(width, q_width), (width, kv_width), (width, kv_width), (q_width, width)],
        (small_rows(data_count), width),
    )
    small = small + swap(small, "tensor", 1)
    small = small + swap(small, "tensor", 2)
    return (
        mixed,
        grad_tokens,
        small[1],
        grad_q,
        grad_k,
        grad_v,
        grad_o,
        small[0],
        small[2 : 2 + expert_count].T,
        totals["gate"][0],
        totals["up"][0],
        totals["down"][0],
    )


def solution(mesh):
    in_specs = (
        P(("dp", "tensor"), None),
        P(),
        P(None, "tensor"),
        P(None, "tensor"),
        P(None, "tensor"),
        P("tensor", None),
        P(),
        P(),
        P("dp", None, None),
        P("dp", None, None),
        P("dp", None, None),
        P("dp", None),
        P(("dp", "tensor"), None),
        P(("dp", "tensor"), None),
    )
    out_specs = (
        P(("dp", "tensor"), None),
        P(("dp", "tensor"), None),
        P(),
        P(None, "tensor"),
        P(None, "tensor"),
        P(None, "tensor"),
        P("tensor", None),
        P(),
        P(),
        P("dp", None, None),
        P("dp", None, None),
        P("dp", None, None),
    )
    return jax.shard_map(
        on_device, mesh=mesh, in_specs=in_specs, out_specs=out_specs, check_vma=False
    )
```

```python
import functools
import math

import jax
import jax.numpy as jnp
import numpy as np
from jax import lax
from jax.experimental import pallas as pl
from jax.experimental.pallas import tpu as pltpu
from jax.sharding import PartitionSpec as P

HEAD_WIDTH = 64
EPS = 1e-06
ROPE_BASE = 10000.0
NEG = -1e30
LANES = 128
BLOCK = 256
REACH = 512
MEGABYTE = 1024 * 1024
low = jnp.bfloat16
wide = jnp.float32
NN = (((1,), (0,)), ((), ()))
NT = (((1,), (1,)), ((), ()))
TN = (((0,), (0,)), ((), ()))
dot = functools.partial(lax.dot_general, preferred_element_type=jnp.float32)
Shape = jax.ShapeDtypeStruct
ANY = pl.BlockSpec(memory_space=pl.ANY)
VMEM = pl.BlockSpec(memory_space=pltpu.VMEM)
SMEM = pl.BlockSpec(memory_space=pltpu.SMEM)


def rope_tables(length):
    half = HEAD_WIDTH // 2
    freq = np.exp(-(np.arange(half, dtype=np.float32) * (2.0 / HEAD_WIDTH)) * math.log(ROPE_BASE))
    angle = np.arange(length, dtype=np.float32)[:, None] * freq.astype(np.float32)[None, :]
    cos, sin = np.cos(angle), np.sin(angle)
    cos = np.concatenate([cos] * 4, axis=1).astype(np.float32)
    sin = np.concatenate([-sin, sin, -sin, sin], axis=1).astype(np.float32)
    return jnp.asarray(cos), jnp.asarray(sin)


def ring_order(count):
    return list(range(0, count, 2)) + list(range(count - 1, 0, -2))


def ring_send(array, step):
    count = lax.axis_size("dp")
    order = ring_order(count)
    return lax.ppermute(
        array, "dp", [(order[i], order[(i + step) % count]) for i in range(count)]
    )


def ring_places():
    count = lax.axis_size("dp")
    order = ring_order(count)
    table = [[(order.index(i) + o) % count for o in range(count)] for i in range(count)]
    table = jnp.asarray(np.asarray(table, np.int32))
    return lax.dynamic_index_in_dim(table, lax.axis_index("dp"), 0, keepdims=False)


def ring_gather(array, last=None, ties=()):
    count = lax.axis_size("dp")
    below, above = [], []
    up, down = array, array
    for step in range(1, count // 2):
        if ties and step == count // 2 - 1:
            up, down = hold((up, down), ties)
        up = ring_send(up, 1)
        down = ring_send(down, -1)
        below.append(up)
        above.append(down)
    if last is None:
        half = array.shape[0] // 2
        up, down = up[:half], down[half:]
    else:
        up, down = halves_of(up, down, last(below, above))
    return below, above, (ring_send(up, 1), ring_send(down, -1))


def swap(array, axis, mask):
    return lax.ppermute(array, axis, [(i, i ^ mask) for i in range(lax.axis_size(axis))])


def tensor_blocks(array):
    far = swap(array, "tensor", 2)
    return array, swap(array, "tensor", 1), far, swap(far, "tensor", 1)


class Token:
    def __init__(self, array):
        self.array = array


TOKEN = (8, LANES)


def call(body, operands, in_specs, out_specs, out_shape, scratch=(), grid=None, after=(), name=None, cost=None, alias=None, vmem=10):
    count = len(after)
    position = len(operands)
    single = not isinstance(out_shape, (list, tuple))
    shapes = [out_shape] if single else list(out_shape)
    specs = [out_specs] if single else list(out_specs)

    def kernel(*refs):
        outs = position + count + len(shapes)
        body(*refs[:position], *refs[position + count : outs], *refs[outs + 1 :])

    extra = {} if grid is None else {"grid": grid}
    if cost is not None:
        extra["cost_estimate"] = pl.CostEstimate(
            flops=int(cost[0]), bytes_accessed=int(cost[1]), transcendentals=0
        )
    if alias is not None:
        extra["input_output_aliases"] = alias
    waits = [entry.array if isinstance(entry, Token) else entry for entry in after]
    results = pl.pallas_call(
        kernel,
        in_specs=list(in_specs) + [ANY] * count,
        out_specs=specs + [VMEM],
        out_shape=shapes + [pltpu.VMEM(TOKEN, wide)],
        scratch_shapes=list(scratch),
        compiler_params=pltpu.CompilerParams(vmem_limit_bytes=vmem * MEGABYTE),
        name=name,
        **extra,
    )(*operands, *waits)
    token = Token(results[-1])
    return (results[0] if single else list(results[:-1])), token


def ring_add_body(first, held, up_ref, part_up_ref, down_ref, part_down_ref, *refs):
    up_out, down_out = refs[held : held + 2]

    def add(got_ref, part_ref, out_ref):
        out_ref[...] = (got_ref[...].astype(wide) + part_ref[...].astype(wide)).astype(low)

    def keep(part_ref, out_ref):
        out_ref[...] = part_ref[...]

    if not first:
        add(up_ref, part_up_ref, up_out)
        add(down_ref, part_down_ref, down_out)
        return

    @pl.when(pl.program_id(0) == 0)
    def _():
        add(up_ref, part_up_ref, up_out)
        keep(part_down_ref, down_out)

    @pl.when(pl.program_id(0) == 1)
    def _():
        keep(part_up_ref, up_out)
        add(down_ref, part_down_ref, down_out)


def ring_add(first, up, part_up, down, part_down, after, held, vmem=10):
    rows, width = part_up.shape
    part = pl.BlockSpec((rows // 2, width), lambda i: (i, 0))
    got = pl.BlockSpec((rows // 2, width), lambda i: (0, 0)) if first else part
    return call(
        functools.partial(ring_add_body, first, len(held)),
        (up, part_up, down, part_down, *held),
        [got, part, got, part] + [ANY] * len(held),
        [part, part] + [ANY] * len(held),
        [Shape((rows, width), low)] * 2 + [Shape(array.shape, array.dtype) for array in held],
        grid=(2,),
        after=after,
        name="ring_add", vmem=vmem,
        cost=(1e8, 4e6),
        alias={4 + i: 2 + i for i in range(len(held))},
    )


def halves_body(up_ref, down_ref, top_ref, bottom_ref):
    top_ref[...] = up_ref[...]
    bottom_ref[...] = down_ref[...]


def halves_of(up, down, after):
    half, width = up.shape[0] // 2, up.shape[1]
    rows = half // 2
    out = pl.BlockSpec((rows, width), lambda i: (i, 0))
    return call(
        halves_body, (up, down), [out, pl.BlockSpec((rows, width), lambda i: (i + 2, 0))], [out] * 2,
        [pltpu.HBM((half, width), low)] * 2, grid=(2,), after=after, name="halves", cost=(1e6, 1e5),
    )[0]


def hold_body(*refs):
    del refs


def hold(arrays, after):
    return call(
        hold_body, arrays, [ANY] * len(arrays), [ANY] * len(arrays),
        [Shape(array.shape, array.dtype) for array in arrays], after=after, name="hold", cost=(1e6, 1e5),
        alias={i: i for i in range(len(arrays))},
    )[0]


def ring_steps(below, above, opposite):
    up = ring_send(opposite[0], 1)
    down = ring_send(opposite[1], -1)
    for k in range(len(above), 0, -1):
        after, held, vmem = yield up, down
        (up, down, *held), token = ring_add(
            k == len(above), up, above[k - 1], down, below[k - 1], after, held, vmem
        )
        up, down = yield token, held, (up, down)
        up = ring_send(up, 1)
        down = ring_send(down, -1)
    yield up, down


def ring_step(steps, after=(), held=(), vmem=10):
    token, held, sums = steps.send((after, held, vmem))
    return token, held, steps.send(sums)


def ring_scatter(below, above, opposite, before=None, then=None):
    steps = ring_steps(below, above, opposite)
    next(steps)
    for index in range(len(above)):
        after, held = before(index) if before else ((), ())
        token, held, arrived = ring_step(steps, after, held)
        if then:
            then(index, token, held)
    return arrived


def swap(array, axis, mask):
    return lax.ppermute(array, axis, [(i, i ^ mask) for i in range(lax.axis_size(axis))])


def tensor_blocks(array):
    far = swap(array, "tensor", 2)
    return array, swap(array, "tensor", 1), far, swap(far, "tensor", 1)


class Token:
    def __init__(self, array):
        self.array = array


TOKEN = (8, LANES)


def call(body, operands, in_specs, out_specs, out_shape, scratch=(), grid=None, after=(), name=None, cost=None, alias=None, vmem=10):
    count = len(after)
    position = len(operands)
    single = not isinstance(out_shape, (list, tuple))
    shapes = [out_shape] if single else list(out_shape)
    specs = [out_specs] if single else list(out_specs)

    def kernel(*refs):
        outs = position + count + len(shapes)
        body(*refs[:position], *refs[position + count : outs], *refs[outs + 1 :])

    extra = {} if grid is None else {"grid": grid}
    if cost is not None:
        extra["cost_estimate"] = pl.CostEstimate(
            flops=int(cost[0]), bytes_accessed=int(cost[1]), transcendentals=0
        )
    if alias is not None:
        extra["input_output_aliases"] = alias
    waits = [entry.array if isinstance(entry, Token) else entry for entry in after]
    results = pl.pallas_call(
        kernel,
        in_specs=list(in_specs) + [ANY] * count,
        out_specs=specs + [VMEM],
        out_shape=shapes + [pltpu.VMEM(TOKEN, wide)],
        scratch_shapes=list(scratch),
        compiler_params=pltpu.CompilerParams(vmem_limit_bytes=vmem * MEGABYTE),
        name=name,
        **extra,
    )(*operands, *waits)
    token = Token(results[-1])
    return (results[0] if single else list(results[:-1])), token


def ring_add_body(first, held, up_ref, part_up_ref, down_ref, part_down_ref, *refs):
    up_out, down_out = refs[held : held + 2]

    def add(got_ref, part_ref, out_ref):
        out_ref[...] = (got_ref[...].astype(wide) + part_ref[...].astype(wide)).astype(low)

    def keep(part_ref, out_ref):
        out_ref[...] = part_ref[...]

    if not first:
        add(up_ref, part_up_ref, up_out)
        add(down_ref, part_down_ref, down_out)
        return

    @pl.when(pl.program_id(0) == 0)
    def _():
        add(up_ref, part_up_ref, up_out)
        keep(part_down_ref, down_out)

    @pl.when(pl.program_id(0) == 1)
    def _():
        keep(part_up_ref, up_out)
        add(down_ref, part_down_ref, down_out)


def ring_add(first, up, part_up, down, part_down, after, held, vmem=10):
    rows, width = part_up.shape
    part = pl.BlockSpec((rows // 2, width), lambda i: (i, 0))
    got = pl.BlockSpec((rows // 2, width), lambda i: (0, 0)) if first else part
    return call(
        functools.partial(ring_add_body, first, len(held)),
        (up, part_up, down, part_down, *held),
        [got, part, got, part] + [ANY] * len(held),
        [part, part] + [ANY] * len(held),
        [Shape((rows, width), low)] * 2 + [Shape(array.shape, array.dtype) for array in held],
        grid=(2,),
        after=after,
        name="ring_add", vmem=vmem,
        cost=(1e8, 4e6),
        alias={4 + i: 2 + i for i in range(len(held))},
    )


def halves_body(up_ref, down_ref, top_ref, bottom_ref):
    top_ref[...] = up_ref[...]
    bottom_ref[...] = down_ref[...]


def halves_of(up, down, after):
    half, width = up.shape[0] // 2, up.shape[1]
    rows = half // 2
    out = pl.BlockSpec((rows, width), lambda i: (i, 0))
    return call(
        halves_body, (up, down), [out, pl.BlockSpec((rows, width), lambda i: (i + 2, 0))], [out] * 2,
        [pltpu.HBM((half, width), low)] * 2, grid=(2,), after=after, name="halves", cost=(1e6, 1e5),
    )[0]


def hold_body(*refs):
    del refs


def hold(arrays, after):
    return call(
        hold_body, arrays, [ANY] * len(arrays), [ANY] * len(arrays),
        [Shape(array.shape, array.dtype) for array in arrays], after=after, name="hold", cost=(1e6, 1e5),
        alias={i: i for i in range(len(arrays))},
    )[0]


def ring_scatter(below, above, opposite, before=None, then=None, vmem=()):
    up = ring_send(opposite[0], 1)
    down = ring_send(opposite[1], -1)
    for index, k in enumerate(range(len(above), 0, -1)):
        after, held = before(index) if before else ((), ())
        (up, down, *held), token = ring_add(
            index == 0, up, above[k - 1], down, below[k - 1], after, held, vmem[index] if index < len(vmem) else 10
        )
        if then:
            then(index, token, held)
        up = ring_send(up, 1)
        down = ring_send(down, -1)
    return up, down


def half_turn(array):
    width = array.shape[-1]
    half = HEAD_WIDTH // 2
    lane = lax.broadcasted_iota(jnp.int32, array.shape, 1)
    return jnp.where(
        lane % HEAD_WIDTH < half, pltpu.roll(array, width - half, 1), pltpu.roll(array, half, 1)
    )


def spread_heads(array):
    lane = lax.broadcasted_iota(jnp.int32, array.shape, 1)
    first = lane < HEAD_WIDTH
    other = pltpu.roll(array, HEAD_WIDTH, 1)
    zero = jnp.zeros_like(array)
    return [
        [jnp.where(first, array, zero), jnp.where(first, zero, other)],
        [jnp.where(first, other, zero), jnp.where(first, zero, array)],
    ]


def load_blocks(place, blocks, target, sems):
    rows = blocks[0].shape[0]
    copies = []
    for mask, block in enumerate(blocks):
        start = pl.multiple_of((place ^ mask) * rows, rows)
        copies.append(pltpu.make_async_copy(block, target.at[pl.ds(start, rows), :], sems.at[mask]))
    for copy in copies:
        copy.start()
    return copies


def fetch(pairs, sems):
    copies = [pltpu.make_async_copy(source, target, sems.at[i]) for i, (source, target) in enumerate(pairs)]
    for copy in copies:
        copy.start()
    return copies


def wait_all(copies):
    for copy in copies:
        copy.wait()


def column_of(row_ref, start, size):
    row = jnp.broadcast_to(row_ref[:, start : start + size].astype(wide), (LANES, size))
    return jnp.transpose(row)[:, :1].astype(jnp.int32)


def attend_body(
    place_ref, own, near, far, both, wq_any, wk_any, wv_any, cos_any, sin_any, row_ref,
    att_ref, q_ref, k_ref, v_ref, lse_ref, rows_s, wq_ref, wk_ref, wv_ref, cos_ref, sin_ref, kz_s, vz_s,
    sems, more_sems,
):
    place = place_ref[0]
    loads = fetch(
        ((wq_any, wq_ref), (cos_any, cos_ref), (sin_any, sin_ref), (wk_any, wk_ref), (wv_any, wv_ref)),
        more_sems,
    )
    copies = load_blocks(place, (own, near, far, both), rows_s, sems)
    length = rows_s.shape[0]
    pairs = wq_ref.shape[1] // LANES
    scale = HEAD_WIDTH**-0.5
    rows_dev = own.shape[0]
    for mask, copy in enumerate(copies):
        at = pl.ds(pl.multiple_of((place ^ mask) * rows_dev, rows_dev), rows_dev)
        copy.wait()
        if mask == 0:
            wait_all(loads)
        rows = rows_s[at, :]
        cos, sin = cos_ref[at, :], sin_ref[at, :]
        query = dot(rows, wq_ref[...], NN)
        for j in range(pairs):
            part = query[:, j * LANES : (j + 1) * LANES]
            turned = (part * cos + half_turn(part) * sin).astype(low)
            q_ref[at, j * LANES : (j + 1) * LANES] = (turned.astype(wide) * scale).astype(low)
        key = dot(rows, wk_ref[...], NN)
        key = (key * cos + half_turn(key) * sin).astype(low)
        k_ref[at, :] = key
        value = dot(rows, wv_ref[...], NN).astype(low)
        v_ref[at, :] = value
        keys, values = spread_heads(key.astype(wide)), spread_heads(value.astype(wide))
        for g in range(2):
            for off in range(2):
                kz_s[2 * g + off, at, :] = keys[g][off].astype(low)
                vz_s[2 * g + off, at, :] = values[g][off].astype(low)
    lane = lax.broadcasted_iota(jnp.int32, (BLOCK, LANES), 1)
    for start in range(0, length, BLOCK):
        at = pl.ds(start, BLOCK)
        first = max(0, start - REACH)
        span = start + BLOCK - first
        keys_at = pl.ds(first, span)
        row_id = lax.broadcasted_iota(jnp.int32, (BLOCK, span), 0) + start
        col_id = lax.broadcasted_iota(jnp.int32, (BLOCK, span), 1) + first
        allowed = (column_of(row_ref, start, BLOCK) == row_ref[:, keys_at]) & (row_id >= col_id)
        bias = jnp.where(allowed, 0.0, NEG)
        stats = jnp.zeros((BLOCK, LANES), wide)
        for j in range(pairs):
            query = q_ref[at, j * LANES : (j + 1) * LANES]
            total = None
            for off in range(2):
                h = 2 * j + off
                slot = 2 * (h // pairs) + off
                scores = dot(query, kz_s[slot, keys_at, :], NT) + bias
                largest = jnp.max(scores, axis=1, keepdims=True)
                shifted = jnp.exp(scores - largest)
                summed = jnp.sum(shifted, axis=1, keepdims=True)
                probs = (shifted * (1.0 / summed)).astype(low)
                part = dot(probs, vz_s[slot, keys_at, :], NN)
                total = part if total is None else total + part
                stats = jnp.where(lane == h, largest + jnp.log(summed), stats)
            att_ref[at, j * LANES : (j + 1) * LANES] = total.astype(low)
        lse_ref[at, :] = stats


def attend(place, blocks, wq, wk, wv, cos, sin, segs, after):
    rows, width = blocks[0].shape
    length = 4 * rows
    return call(
        attend_body,
        (place, *blocks, wq, wk, wv, cos, sin, segs.reshape(1, length)),
        [SMEM] + [ANY] * 9 + [VMEM],
        [VMEM] * 5,
        [
            Shape((length, wq.shape[1]), low),
            Shape((length, wq.shape[1]), low),
            Shape((length, wk.shape[1]), low),
            Shape((length, wk.shape[1]), low),
            Shape((length, LANES), wide),
        ],
        [
            pltpu.VMEM((length, width), low),
            pltpu.VMEM(wq.shape, low),
            pltpu.VMEM(wk.shape, low),
            pltpu.VMEM(wv.shape, low),
            pltpu.VMEM(cos.shape, wide),
            pltpu.VMEM(sin.shape, wide),
            pltpu.VMEM((4, length, LANES), low),
            pltpu.VMEM((4, length, LANES), low),
            pltpu.SemaphoreType.DMA((4,)),
            pltpu.SemaphoreType.DMA((5,)),
        ],
        after=after,
        name="attend", vmem=62,
        cost=(15e-6 * 1.1e15, 12e6),
    )


def branch_body(flip, place_ref, att_ref, wo_ref, out_ref):
    rows = out_ref.shape[1]
    core = place_ref[0] % 2
    core = 1 - core if flip else core
    for x in range(2):
        at = pl.ds(pl.multiple_of((2 * x + core) * rows, rows), rows)
        out_ref[x] = dot(att_ref[at, :], wo_ref[...], NN).astype(low)


def branch_half(place, att, wo, flip, after=()):
    rows, width = att.shape[0] // 4, wo.shape[1]
    return call(
        functools.partial(branch_body, flip),
        (place, att, wo),
        [SMEM] + [VMEM] * 2,
        VMEM,
        Shape((2, rows, width), low),
        after=after,
        name="branch", vmem=14,
        cost=(2e9, 4e6),
    )[0]


def attend_back_body(
    place_ref, own, near, far, both, wo_any, att_any, q_any, k_any, v_any, lse_any, cos_any, sin_any, row_ref,
    d_lin_ref, rows_s, wo_ref, att_ref, q_ref, k_ref, v_ref, lse_ref, cos_ref, sin_ref,
    kz_s, kt_s, vz_s, d_att_s, d_key_s, d_value_s, d_query_s, sems, more_sems,
):
    place = place_ref[0]
    copies = load_blocks(place, (own, near, far, both), rows_s, sems)
    copies += fetch(
        ((wo_any, wo_ref), (att_any, att_ref), (lse_any, lse_ref), (k_any, k_ref), (v_any, v_ref)), more_sems
    )
    later = fetch(((q_any, q_ref), (cos_any, cos_ref), (sin_any, sin_ref)), more_sems.at[pl.ds(5, 3)])
    wait_all(copies)
    length, q_width = att_ref.shape
    heads = q_width // HEAD_WIDTH
    pairs = heads // 2
    scale = HEAD_WIDTH**-0.5
    lane = lax.broadcasted_iota(jnp.int32, (BLOCK, LANES), 1)
    stats_t = []
    for start in range(0, length, BLOCK):
        at = pl.ds(start, BLOCK)
        d_att = dot(rows_s[at, :], wo_ref[...], NT).astype(low)
        d_att_s[at, :] = d_att
        product = d_att.astype(wide) * att_ref[at, :].astype(wide)
        stats = lse_ref[at, :]
        for h in range(heads):
            part = product[:, (h // 2) * LANES : (h // 2 + 1) * LANES]
            mine = lane // HEAD_WIDTH == h % 2
            inner = jnp.sum(jnp.where(mine, part, 0.0), axis=1, keepdims=True)
            stats = jnp.where(lane == heads + h, inner, stats)
        stats_t.append(jnp.transpose(stats))
        keys, values = spread_heads(k_ref[at, :].astype(wide)), spread_heads(v_ref[at, :].astype(wide))
        for g in range(2):
            for off in range(2):
                kz_s[2 * g + off, at, :] = keys[g][off].astype(low)
                vz_s[2 * g + off, at, :] = values[g][off].astype(low)
                kt_s[2 * g + off, :, at] = jnp.transpose(keys[g][off]).astype(low)
    d_key_s[...] = jnp.zeros_like(d_key_s)
    d_value_s[...] = jnp.zeros_like(d_value_s)
    wait_all(later)
    for i, start in enumerate(range(0, length, BLOCK)):
        at = pl.ds(start, BLOCK)
        first = max(0, start - REACH)
        span = start + BLOCK - first
        keys_at = pl.ds(first, span)
        key_id = lax.broadcasted_iota(jnp.int32, (span, BLOCK), 0) + first
        query_id = lax.broadcasted_iota(jnp.int32, (span, BLOCK), 1) + start
        allowed = (column_of(row_ref, first, span) == row_ref[:, at]) & (query_id >= key_id)
        bias = jnp.where(allowed, 0.0, NEG)
        for j in range(pairs):
            query = q_ref[at, j * LANES : (j + 1) * LANES]
            d_att = d_att_s[at, j * LANES : (j + 1) * LANES]
            total = None
            for off in range(2):
                h = 2 * j + off
                slot = 2 * (h // pairs) + off
                scores = dot(kz_s[slot, keys_at, :], query, NT) + bias
                probs = jnp.exp(scores - stats_t[i][h : h + 1, :])
                d_probs = dot(vz_s[slot, keys_at, :], d_att, NT)
                d_scores = probs * (d_probs - stats_t[i][heads + h : heads + h + 1, :])
                d_scores = d_scores.astype(low)
                d_value_s[slot, keys_at, :] += dot(probs.astype(low), d_att, NN)
                d_key_s[slot, keys_at, :] += dot(d_scores, query, NN)
                part = dot(kt_s[slot, :, keys_at], d_scores, NN)
                total = part if total is None else total + part
            d_query_s[j * LANES : (j + 1) * LANES, at] = total
    for start in range(0, length, BLOCK):
        at = pl.ds(start, BLOCK)
        cos, sin = cos_ref[at, :], sin_ref[at, :]
        for j in range(pairs):
            part = jnp.transpose(d_query_s[j * LANES : (j + 1) * LANES, at]) * scale
            turned = part * cos - half_turn(part) * sin
            d_lin_ref[at, j * LANES : (j + 1) * LANES] = turned.astype(low)
        both_of = []
        for ref in (d_key_s, d_value_s):
            first_head = ref[0, at, :] + pltpu.roll(ref[1, at, :], HEAD_WIDTH, 1)
            second_head = ref[3, at, :] + pltpu.roll(ref[2, at, :], HEAD_WIDTH, 1)
            both_of.append(jnp.where(lane < HEAD_WIDTH, first_head, second_head))
        d_key, d_value = both_of
        d_lin_ref[at, q_width : q_width + LANES] = (d_key * cos - half_turn(d_key) * sin).astype(low)
        d_lin_ref[at, q_width + LANES :] = d_value.astype(low)


def attend_back(place, blocks, wo, att, q, k, v, lse, cos, sin, segs, after):
    rows, width = blocks[0].shape
    length, q_width = att.shape
    return call(
        attend_back_body,
        (place, *blocks, wo, att, q, k, v, lse, cos, sin, segs.reshape(1, length)),
        [SMEM] + [ANY] * 12 + [VMEM],
        VMEM,
        Shape((length, q_width + 2 * LANES), low),
        [
            pltpu.VMEM((length, width), low),
            pltpu.VMEM(wo.shape, low),
            pltpu.VMEM(att.shape, low),
            pltpu.VMEM(q.shape, low),
            pltpu.VMEM(k.shape, low),
            pltpu.VMEM(v.shape, low),
            pltpu.VMEM(lse.shape, wide),
            pltpu.VMEM(cos.shape, wide),
            pltpu.VMEM(sin.shape, wide),
            pltpu.VMEM((4, length, LANES), low),
            pltpu.VMEM((4, LANES, length), low),
            pltpu.VMEM((4, length, LANES), low),
            pltpu.VMEM((length, q_width), low),
            pltpu.VMEM((4, length, LANES), wide),
            pltpu.VMEM((4, length, LANES), wide),
            pltpu.VMEM((q_width, length), wide),
            pltpu.SemaphoreType.DMA((4,)),
            pltpu.SemaphoreType.DMA((8,)),
        ],
        after=after,
        name="attend_back", vmem=62,
        cost=(15e-6 * 1.1e15, 12e6),
    )


def split_add_body(place_ref, mine_ref, got_ref, kept_ref, sent_ref):
    far = place_ref[0] // 2
    kept_ref[...] = (mine_ref[far].astype(wide) + got_ref[far].astype(wide)).astype(low)
    sent_ref[...] = (mine_ref[1 - far].astype(wide) + got_ref[1 - far].astype(wide)).astype(low)


def tensor_scatter(place, mine, other, after):
    (kept, sent), token = split_add(place, mine, swap(other, "tensor", 1), after)
    return kept, swap(sent, "tensor", 2), token


def split_add(place, mine, got, after=()):
    rows, width = mine.shape[1:]
    return call(
        split_add_body,
        (place, mine, got),
        [SMEM] + [pl.BlockSpec((2, rows // 2, width), lambda i: (0, i, 0))] * 2,
        [pl.BlockSpec((rows // 2, width), lambda i: (i, 0))] * 2,
        [pltpu.HBM((rows, width), low)] * 2,
        grid=(2,),
        after=after,
        name="split_add", vmem=12,
        cost=(1e9, 6e6),
    )


def expert_body(pieces, cuts, local, with_mixed, *refs):
    rows_refs = refs[:pieces]
    up_refs = refs[pieces : 2 * pieces]
    d_act_ref, sel_ref, router_ref, gate_ref, up_w_ref = refs[2 * pieces : 2 * pieces + 5]
    outs = refs[2 * pieces + 5 :]
    if with_mixed:
        down_ref, outs = outs[0], outs[1:]
        mixed_refs, outs = outs[:pieces], outs[pieces:]
        mixed_s, outs = outs[-1], outs[:-1]
    d_rows_refs, outs = outs[:pieces], outs[pieces:]
    hidden_ref, d_gate_ref, d_up_ref, rows_s, mask_s, d_rows_s, gates_s, d_gates_s, sems = outs
    step = pl.program_id(0)
    width = rows_s.shape[1]

    @pl.when(step == 0)
    def _():
        copies, start = [], 0
        for i in range(pieces):
            at = pl.ds(start, rows_refs[i].shape[0])
            start += rows_refs[i].shape[0]
            copies.append(pltpu.make_async_copy(rows_refs[i], rows_s.at[at, :], sems.at[i]))
            copies.append(
                pltpu.make_async_copy(
                    up_refs[i].at[:, pl.ds(width, LANES)], mask_s.at[at, :], sems.at[pieces + i]
                )
            )
        for copy in copies:
            copy.start()
        wait_all(copies)
        chosen = mask_s[...] > 0.0
        logits = jnp.where(chosen, dot(rows_s[...], router_ref[...], NT), NEG)
        largest = jnp.max(logits, axis=1, keepdims=True)
        shifted = jnp.where(chosen, jnp.exp(logits - largest), 0.0)
        gates_s[...] = shifted / jnp.sum(shifted, axis=1, keepdims=True)
        d_gates_s[...] = jnp.zeros_like(d_gates_s)

    expert = step // cuts
    pick = sel_ref[0:1, :]
    for e in range(1, local):
        pick = jnp.where(expert == e, sel_ref[e : e + 1, :], pick)
    gate = jnp.sum(gates_s[...] * pick, axis=1, keepdims=True)
    rows = rows_s[...]
    gate_w, up_w = gate_ref[0], up_w_ref[0]
    gate_pre = dot(rows, gate_w, NN)
    up_pre = dot(rows, up_w, NN)
    d_act = d_act_ref[...].astype(wide)
    sig = 1.0 / (1.0 + jnp.exp(-gate_pre))
    act = gate_pre * sig
    hidden = act * up_pre
    d_gates_s[...] += jnp.sum(hidden * d_act, axis=1, keepdims=True) * pick
    hidden = (gate * hidden).astype(low)
    d_act = gate * d_act
    d_gate = (d_act * up_pre * sig * (1.0 + gate_pre * (1.0 - sig))).astype(low)
    d_up = (d_act * act).astype(low)
    hidden_ref[...] = hidden
    d_gate_ref[...] = d_gate
    d_up_ref[...] = d_up
    sums = [(d_rows_s, dot(d_gate, gate_w, NT) + dot(d_up, up_w, NT))]
    if with_mixed:
        sums.append((mixed_s, dot(hidden, down_ref[0], NN)))

    @pl.when(step == 0)
    def _():
        for ref, value in sums:
            ref[...] = value

    @pl.when(step > 0)
    def _():
        for ref, value in sums:
            ref[...] += value

    @pl.when(step == pl.num_programs(0) - 1)
    def _():
        lane = lax.broadcasted_iota(jnp.int32, d_gates_s.shape, 1)
        d_gates = d_gates_s[...]
        d_gates = jnp.where(lane < LANES // 2, d_gates, pltpu.roll(d_gates, LANES // 2, 1))
        rounded = d_gates.astype(low).astype(wide)
        d_gates = jnp.where(lane < LANES // 2, rounded, d_gates - rounded).astype(low)
        start = 0
        for i, d_rows_ref in enumerate(d_rows_refs):
            size = d_rows_ref.shape[0]
            d_rows_ref[:, :width] = d_rows_s[start : start + size, :].astype(low)
            d_rows_ref[:, width:] = d_gates[start : start + size, :]
            if with_mixed:
                mixed_refs[i][...] = mixed_s[start : start + size, :].astype(low)
            start += size


def expert_block(rows_list, ups_list, d_act, sel, w_router, w_gate, w_up, w_down, with_mixed, after=()):
    pieces = len(rows_list)
    sizes = [rows.shape[0] for rows in rows_list]
    rows = sum(sizes)
    local, width, ff = w_gate.shape
    cut = min(512, ff)
    cuts = ff // cut
    whole = lambda shape: pl.BlockSpec(shape, lambda j: (0,) * len(shape))
    across = pl.BlockSpec((1, width, cut), lambda j: (j // cuts, 0, j % cuts))
    tall = pl.BlockSpec((1, cut, width), lambda j: (j // cuts, j % cuts, 0))
    part = pl.BlockSpec((rows, cut), lambda j: (0, j))
    mixed_out = with_mixed * pieces
    outs, token = call(
        functools.partial(expert_body, pieces, cuts, local, with_mixed),
        (*rows_list, *ups_list, d_act, sel, w_router, w_gate, w_up) + (w_down,) * with_mixed,
        [ANY] * (2 * pieces)
        + [part, whole((local, LANES)), whole((LANES, width)), across, across]
        + [tall] * with_mixed,
        [whole((size, width)) for size in sizes[:mixed_out]]
        + [whole((size, width + LANES)) for size in sizes]
        + [part, part, part],
        [pltpu.HBM((size, width), low) for size in sizes[:mixed_out]]
        + [pltpu.HBM((size, width + LANES), low) for size in sizes]
        + [pltpu.HBM((rows, local * ff), low)] * 3,
        [
            pltpu.VMEM((rows, width), low),
            pltpu.VMEM((rows, LANES), low),
            pltpu.VMEM((rows, width), wide),
            pltpu.VMEM((rows, LANES), wide),
            pltpu.VMEM((rows, LANES), wide),
            pltpu.SemaphoreType.DMA((2 * pieces,)),
        ]
        + [pltpu.VMEM((rows, width), wide)] * with_mixed,
        grid=(local * cuts,),
        after=after,
        name="experts", vmem=40,
        cost=(14 * rows * width * local * ff, 6 * local * width * ff + 8 * rows * width),
    )
    return (
        outs[mixed_out : mixed_out + pieces], outs[:mixed_out], outs[mixed_out + pieces :], token
    )


def d_act_body(pieces, *refs):
    up_refs = refs[:pieces]
    down_ref, out_ref, ups_s, sems = refs[pieces:]

    @pl.when(pl.program_id(0) == 0)
    def _():
        copies, start = [], 0
        for i, ref in enumerate(up_refs):
            size = ref.shape[0]
            copies.append(
                pltpu.make_async_copy(
                    ref.at[:, pl.ds(0, ups_s.shape[1])], ups_s.at[pl.ds(start, size), :], sems.at[i]
                )
            )
            start += size
        for copy in copies:
            copy.start()
        wait_all(copies)

    out_ref[...] = dot(ups_s[...], down_ref[0], NT).astype(low)


def d_act_block(ups_list, w_down, after=()):
    local, ff, width = w_down.shape
    rows = sum(ups.shape[0] for ups in ups_list)
    return call(
        functools.partial(d_act_body, len(ups_list)),
        (*ups_list, w_down),
        [ANY] * len(ups_list) + [pl.BlockSpec((1, ff, width), lambda e: (e, 0, 0))],
        pl.BlockSpec((rows, ff), lambda e: (0, e)),
        Shape((rows, local * ff), low),
        [pltpu.VMEM((rows, width), low), pltpu.SemaphoreType.DMA((len(ups_list),))],
        grid=(local,),
        after=after,
        name="d_act", vmem=20,
        cost=(5e8, 1e6),
    )


def outer_body(pieces, seconds, split, place_ref, *refs):
    first_refs = refs[:pieces]
    second_refs = refs[pieces : pieces + seconds]
    mine_ref, other_ref, first_s, second_s, first_sems, second_sems = refs[pieces + seconds :]
    core = place_ref[0] % 2
    step = pl.program_id(0)
    cut = first_s.shape[2]
    width = second_s.shape[1]

    def load(at, slot):
        copies, start = [], 0
        for i, ref in enumerate(first_refs):
            size = ref.shape[0]
            copies.append(
                pltpu.make_async_copy(
                    ref.at[:, pl.ds(pl.multiple_of(at * cut, cut), cut)],
                    first_s.at[slot, pl.ds(start, size), :],
                    first_sems.at[slot, i],
                )
            )
            start += size
        return copies

    slot = step % 2

    @pl.when(step == 0)
    def _():
        for copy in load(0, 0):
            copy.start()
        copies, start = [], 0
        for i, ref in enumerate(second_refs):
            size = ref.shape[0]
            copies.append(
                pltpu.make_async_copy(
                    ref.at[:, pl.ds(0, width)], second_s.at[pl.ds(start, size), :], second_sems.at[i]
                )
            )
            start += size
        for copy in copies:
            copy.start()
        wait_all(copies)

    @pl.when(step + 1 < pl.num_programs(0))
    def _():
        for copy in load(step + 1, 1 - slot):
            copy.start()

    wait_all(load(step, slot))
    product = dot(first_s[slot], second_s[...], TN).astype(low)
    if split == 1:

        @pl.when(step == core)
        def _():
            mine_ref[...] = product

        @pl.when(step != core)
        def _():
            other_ref[...] = product
    else:
        first, last = product[:, : width // 2], product[:, width // 2 :]
        mine_ref[...] = jnp.where(core == 0, first, last)
        other_ref[...] = jnp.where(core == 0, last, first)


def outer_products(place, first, second, first_width, second_width, split, after=()):
    cut = 512
    steps = first_width // cut
    rows = sum(piece.shape[0] for piece in first)
    if split == 1:
        out_shape = Shape((cut, second_width), low)
        out_spec = pl.BlockSpec((cut, second_width), lambda i: (0, 0))
    else:
        out_shape = Shape((first_width, second_width // 2), low)
        out_spec = pl.BlockSpec((cut, second_width // 2), lambda i: (i, 0))
    return call(
        functools.partial(outer_body, len(first), len(second), split),
        (place, *first, *second),
        [SMEM] + [ANY] * (len(first) + len(second)),
        [out_spec] * 2,
        [out_shape] * 2,
        [
            pltpu.VMEM((2, rows, cut), low),
            pltpu.VMEM((rows, second_width), low),
            pltpu.SemaphoreType.DMA((2, len(first))),
            pltpu.SemaphoreType.DMA((len(second),)),
        ],
        grid=(steps,),
        after=after,
        name="outer_products", vmem=24 if rows <= 4096 else 58,
        cost=(3.5 * rows * first_width * second_width, 12e6),
    )


def ring_parts_of(count, ids_ref, flat_s, outs):
    part = flat_s.shape[0] // count
    for o, ref in enumerate(outs):
        size = ref.shape[0]
        if o < count // 2:
            at = ids_ref[o] * part
        elif o > count // 2 + 1:
            at = ids_ref[o - 1] * part
        else:
            at = ids_ref[count // 2] * part + (o - count // 2) * size
        ref[...] = flat_s[pl.ds(pl.multiple_of(at, size), size), :]


def ring_part_sizes(count, flat):
    part = flat // count
    return [part] * (count // 2) + [part // 2] * 2 + [part] * (count // 2 - 1)


def small_rows(count):
    return 4 * count


def ring_part_list(count, outs):
    half = count // 2
    return list(outs[:half]) + [tuple(outs[half : half + 2])] + list(outs[half + 2 :])


def head_grads_body(count, place_ref, ids_ref, *refs):
    rows_refs, d_refs, late_refs = refs[:4], refs[4:8], refs[8:13]
    gain_ref, gain_ffn_ref, router_ref = refs[13:16]
    outs = refs[16 : 16 + count + 1]
    rows_s, d_s, flat_s, small_s, *loaded, sems, d_sems, late_sems = refs[17 + count :]
    d_lin_ref, wq_ref, wk_ref, wv_ref, att_ref = loaded
    lin_copies = fetch(tuple(zip(late_refs[:1], loaded[:1])), late_sems)
    small_s[...] = jnp.zeros_like(small_s)
    small_s[:1, :] = gain_ffn_ref[...]
    small_s[2 : 2 + router_ref.shape[0], :] = router_ref[...]
    copies = load_blocks(place_ref[0], rows_refs, rows_s, sems)
    weight_copies = fetch(tuple(zip(late_refs[1:4], loaded[1:4])), late_sems.at[pl.ds(1, 3)])
    d_copies = load_blocks(place_ref[0], d_refs, d_s, d_sems)
    d_copies += fetch(tuple(zip(late_refs[4:], loaded[4:])), late_sems.at[pl.ds(4, 1)])
    wait_all(lin_copies)
    wait_all(copies)
    q_width, kv_width = wq_ref.shape[1], wk_ref.shape[1]
    lin_width = d_lin_ref.shape[1]
    width = rows_s.shape[1]
    for at in range(0, width, 512):
        here = pl.ds(at, 512)
        grads = dot(rows_s[:, here], d_lin_ref[...], TN)
        for c in range(0, lin_width, LANES):
            row = c // LANES * width + at
            flat_s[row : row + 512, :] = grads[:, c : c + LANES].astype(low)
        if at == 0:
            wait_all(weight_copies)
        inner = jnp.sum(wq_ref[here, :].astype(wide) * grads[:, :q_width], axis=1, keepdims=True)
        inner += jnp.sum(
            wk_ref[here, :].astype(wide) * grads[:, q_width : q_width + kv_width], axis=1, keepdims=True
        )
        inner += jnp.sum(
            wv_ref[here, :].astype(wide) * grads[:, q_width + kv_width :], axis=1, keepdims=True
        )
        inner = jnp.transpose(jnp.broadcast_to(inner, (512, LANES)))[:1]
        small_s[1:2, here] = inner / gain_ref[here].reshape(1, -1)
    wait_all(d_copies)
    base = lin_width // LANES * width
    for at in range(0, width, 512):
        grads = dot(att_ref[...], d_s[:, at : at + 512], TN).astype(low)
        for c in range(0, 512, LANES):
            row = base + (at + c) // LANES * q_width
            flat_s[row : row + q_width, :] = grads[:, c : c + LANES]
    base = base + width // LANES * q_width
    size = small_s.shape[0]
    for c in range(0, width, LANES):
        row = base + c // LANES * size
        flat_s[row : row + size, :] = small_s[:, c : c + LANES].astype(low)
    row = base + width // LANES * size
    flat_s[row:, :] = jnp.zeros((flat_s.shape[0] - row, LANES), low)
    ring_parts_of(count, ids_ref, flat_s, outs)


def head_grads(
    place, ids, rows_blocks, d_blocks, att, d_lin, wq, wk, wv, gain, gain_ffn_part, router_part, after=()
):
    count = lax.axis_size("dp")
    rows, width = rows_blocks[0].shape
    length, lin_width = d_lin.shape
    flat = width * (lin_width + att.shape[1]) // LANES + 64 * count
    outs, token = call(
        functools.partial(head_grads_body, count),
        (place, ids, *rows_blocks, *d_blocks, d_lin, wq, wk, wv, att, gain, gain_ffn_part, router_part),
        [SMEM, SMEM] + [ANY] * 13 + [VMEM] * 3,
        [VMEM] * (count + 1),
        [Shape((size, LANES), low) for size in ring_part_sizes(count, flat)],
        [
            pltpu.VMEM((length, width), low),
            pltpu.VMEM((length, width), low),
            pltpu.VMEM((flat, LANES), low),
            pltpu.VMEM((small_rows(count), width), wide),
            *[pltpu.VMEM(array.shape, low) for array in (d_lin, wq, wk, wv, att)],
            pltpu.SemaphoreType.DMA((4,)),
            pltpu.SemaphoreType.DMA((4,)),
            pltpu.SemaphoreType.DMA((5,)),
        ],
        after=after,
        name="head_grads", vmem=62,
        cost=(8e-6 * 1.1e15, 12e6),
    )
    return ring_part_list(count, outs), token


def ring_sum_body(own_ref, up_ref, down_ref, out_ref):
    out_ref[...] = (
        own_ref[...].astype(wide) + up_ref[...].astype(wide) + down_ref[...].astype(wide)
    ).astype(low)


def ring_total(parts, before, then, last, later):
    half = len(parts) // 2
    up, down = ring_scatter(
        [parts[len(parts) - 1 - i] for i in range(half - 1)],
        [parts[1 + i] for i in range(half - 1)],
        parts[half],
        before,
        then,
    )
    total, _ = call(
        ring_sum_body, (parts[0], up, down), [VMEM] * 3, VMEM, Shape(parts[0].shape, low),
        after=last(), name="ring_sum", cost=(1e8, 1e6),
    )
    below, above, far = ring_gather(total, ties=later())
    return [total] + above + list(far) + below[::-1]


def head_place_body(count, ids_ref, *refs):
    blocks = refs[: count + 1]
    grads, small_ref, flat_s = refs[count + 1 : -2], refs[-2], refs[-1]
    part = flat_s.shape[0] // count
    for o, ref in enumerate(blocks):
        size = ref.shape[0]
        if o < count // 2:
            at = ids_ref[o] * part
        elif o > count // 2 + 1:
            at = ids_ref[o - 1] * part
        else:
            at = ids_ref[count // 2] * part + (o - count // 2) * size
        flat_s[pl.ds(pl.multiple_of(at, size), size), :] = ref[...]
    row = 0
    for ref in grads:
        rows, columns = ref.shape
        for c in range(0, columns, LANES):
            ref[:, c : c + LANES] = flat_s[row : row + rows, :].astype(wide)
            row += rows
    rows, columns = small_ref.shape
    for c in range(0, columns, LANES):
        small_ref[:, c : c + LANES] = flat_s[row : row + rows, :].astype(wide)
        row += rows


def head_place(ids, blocks, shapes, small_shape, after):
    count = lax.axis_size("dp")
    flat = sum(rows * columns for rows, columns in shapes) // LANES + 64 * count
    return call(
        functools.partial(head_place_body, count),
        (ids, *blocks),
        [SMEM] + [VMEM] * (count + 1),
        [VMEM] * (len(shapes) + 1),
        [Shape(shape, wide) for shape in (*shapes, small_shape)],
        [pltpu.VMEM((flat, LANES), low)],
        after=after,
        name="head_place", vmem=24,
        cost=(1e9, 6e6),
    )[0]


def add_body(first_ref, second_ref, out_ref):
    out_ref[...] = (first_ref[...].astype(wide) + second_ref[...].astype(wide)).astype(low)


def add_rows(first, second, after=()):
    return call(
        add_body, (first, second), [VMEM] * 2, VMEM, Shape(first.shape, low), after=after,
        name="add_rows", cost=(1e8, 3e6),
    )


def place_quarters_body(place_ref, *refs):
    del place_ref
    pieces, out_ref = refs[:4], refs[4]
    step = pl.program_id(0)
    for i, ref in enumerate(pieces):

        @pl.when(step == i)
        def _():
            out_ref[0] = ref[...].astype(wide)


def place_quarters(place, pieces):
    rows, columns = pieces[0].shape
    fixed = pl.BlockSpec((rows, columns), lambda i, place_ref: (0, 0))
    out = pl.BlockSpec(
        (1, rows, columns),
        lambda i, place_ref: (i // 2 ^ place_ref[0] % 2, i % 2 ^ place_ref[0] // 2, 0),
    )
    result, token = pl.pallas_call(
        place_quarters_body,
        grid_spec=pltpu.PrefetchScalarGridSpec(
            num_scalar_prefetch=1, grid=(4,), in_specs=[fixed] * 4, out_specs=[out, VMEM]
        ),
        out_shape=[pltpu.HBM((2, 2 * rows, columns), wide), pltpu.VMEM(TOKEN, wide)],
        compiler_params=pltpu.CompilerParams(vmem_limit_bytes=16 * MEGABYTE),
        cost_estimate=pl.CostEstimate(flops=10**8, bytes_accessed=10**7, transcendentals=0),
        name="place_quarters",
    )(place, *pieces)
    return result, Token(token)


def lin_back_body(place_ref, d_lin_ref, wq_ref, wk_ref, wv_ref, mine_ref, other_ref):
    rows = mine_ref.shape[1]
    core = place_ref[0] % 2
    q_width, kv_width = wq_ref.shape[1], wk_ref.shape[1]
    for x in range(2):
        for ref, c in ((other_ref, 1 - core), (mine_ref, core)):
            at = pl.ds(pl.multiple_of((2 * x + c) * rows, rows), rows)
            total = dot(d_lin_ref[at, :q_width], wq_ref[...], NT)
            total += dot(d_lin_ref[at, q_width : q_width + kv_width], wk_ref[...], NT)
            total += dot(d_lin_ref[at, q_width + kv_width :], wv_ref[...], NT)
            ref[x] = total.astype(low)


def lin_back(place, d_lin, wq, wk, wv, after):
    rows, width = d_lin.shape[0] // 4, wq.shape[0]
    return call(
        lin_back_body,
        (place, d_lin, wq, wk, wv),
        [SMEM] + [VMEM] * 4,
        [VMEM] * 2,
        [Shape((2, rows, width), low)] * 2,
        after=after,
        name="lin_back", vmem=20,
        cost=(4e-6 * 1.1e15, 9e6),
    )


def first_norm_body(tokens_ref, gain_ref, cotangent_ref, routes_ref, normed_ref, ups_ref):
    width = cotangent_ref.shape[1]
    routes = routes_ref[...]
    lane = lax.broadcasted_iota(jnp.int32, (LANES, routes.shape[1]), 0)
    chosen = routes[:1, :] == lane
    for k in range(1, routes.shape[0]):
        chosen = chosen | (routes[k : k + 1, :] == lane)
    ups_ref[:, :width] = cotangent_ref[...]
    ups_ref[:, width:] = jnp.transpose(jnp.where(chosen, 1.0, 0.0)).astype(low)
    inputs = tokens_ref[...].astype(wide)
    inverse = lax.rsqrt(jnp.mean(inputs * inputs, axis=1, keepdims=True) + EPS)
    normed_ref[...] = (inputs * inverse * gain_ref[...].reshape(1, -1)).astype(low)


def second_norm_body(tokens_ref, kept_ref, got_ref, gain_ref, residual_ref, normed_ref):
    residual = tokens_ref[...].astype(wide) + (kept_ref[...].astype(wide) + got_ref[...].astype(wide))
    inverse = lax.rsqrt(jnp.mean(residual * residual, axis=1, keepdims=True) + EPS)
    residual_ref[...] = residual
    normed_ref[...] = (residual * inverse * gain_ref[...].reshape(1, -1)).astype(low)


def middle_body(
    own_ref, up_ref, down_ref, residual_ref, normed_ref, ups_ref, router_ref, gain_ref,
    d_residual_ref, d_low_ref, gain_out, router_out,
):
    width = residual_ref.shape[1]
    total = own_ref[...].astype(wide) + up_ref[...].astype(wide) + down_ref[...].astype(wide)
    d_gates = total[:, width:]
    d_gates = d_gates + pltpu.roll(d_gates, LANES // 2, 1)
    lane = lax.broadcasted_iota(jnp.int32, d_gates.shape, 1)
    chosen = ups_ref[:, width:] > 0.0
    normed = normed_ref[...]
    logits = jnp.where(chosen, dot(normed, router_ref[...], NT), NEG)
    largest = jnp.max(logits, axis=1, keepdims=True)
    shifted = jnp.where(chosen, jnp.exp(logits - largest), 0.0)
    gates = shifted / jnp.sum(shifted, axis=1, keepdims=True)
    inner = jnp.sum(gates * d_gates, axis=1, keepdims=True)
    d_logits = (gates * (d_gates - inner)).astype(low)
    router_part = dot(d_logits, normed, TN)[: router_out.shape[0]]
    d_normed = total[:, :width] + dot(d_logits, router_ref[...], NN)
    residual = residual_ref[...]
    inverse = lax.rsqrt(jnp.mean(residual * residual, axis=1, keepdims=True) + EPS)
    scaled = d_normed * gain_ref[...].reshape(1, -1)
    mean = jnp.mean(scaled * residual, axis=1, keepdims=True)
    upstream = ups_ref[:, :width].astype(wide)
    d_residual = upstream + inverse * scaled - residual * (inverse * inverse * inverse * mean)
    gain_part = jnp.sum(d_normed * residual * inverse, axis=0, keepdims=True)

    @pl.when(pl.program_id(0) == 0)
    def _():
        gain_out[...] = gain_part
        router_out[...] = router_part

    @pl.when(pl.program_id(0) > 0)
    def _():
        gain_out[...] += gain_part
        router_out[...] += router_part

    d_residual_ref[...] = d_residual
    d_low_ref[...] = d_residual.astype(low)


def last_body(tokens_ref, kept_ref, got_ref, d_residual_ref, gain_ref, out_ref):
    inputs = tokens_ref[...].astype(wide)
    inverse = lax.rsqrt(jnp.mean(inputs * inputs, axis=1, keepdims=True) + EPS)
    scaled = (kept_ref[...].astype(wide) + got_ref[...].astype(wide)) * gain_ref[...].reshape(1, -1)
    mean = jnp.mean(scaled * inputs, axis=1, keepdims=True)
    d_inputs = inverse * scaled - inputs * (inverse * inverse * inverse * mean)
    out_ref[...] = (d_inputs + d_residual_ref[...]).astype(low)


def on_device(
    tokens,
    gain_attn,
    query_weight,
    key_weight,
    value_weight,
    w_output,
    gain_ffn,
    w_router,
    w_gate,
    w_up,
    w_down,
    segments,
    routes,
    cotangent,
):
    rows_dev, width = tokens.shape
    data_count = lax.axis_size("dp")
    half_count = data_count // 2
    local_experts, _, ff = w_gate.shape
    expert_count = local_experts * data_count
    q_width, kv_width = query_weight.shape[1], key_weight.shape[1]
    place = lax.axis_index("tensor").astype(jnp.int32).reshape(1)
    ids = ring_places()
    cos, sin = rope_tables(segments.shape[1])
    gain_one, gain_two = gain_attn, gain_ffn
    lanes = jnp.arange(LANES, dtype=jnp.int32)
    own_experts = lax.axis_index("dp") * local_experts + jnp.arange(local_experts, dtype=jnp.int32)
    sel = (own_experts[:, None] == lanes[None, :]).astype(wide)
    router = jnp.pad(w_router.T, ((0, LANES - expert_count), (0, 0)))

    half_rows = rows_dev // 2
    row_spec = pl.BlockSpec((half_rows, width), lambda i: (i, 0))
    wide_spec = pl.BlockSpec((half_rows, width + LANES), lambda i: (i, 0))
    gain_spec = pl.BlockSpec((width,), lambda i: (0,))
    sum_spec = pl.BlockSpec((1, width), lambda i: (0, 0))
    (normed_one, ups), _ = call(
        first_norm_body,
        (tokens, gain_one, cotangent, routes.T),
        [row_spec, gain_spec, row_spec, pl.BlockSpec((routes.shape[1], half_rows), lambda i: (0, i))],
        [row_spec, wide_spec],
        [Shape((rows_dev, width), low), Shape((rows_dev, width + LANES), low)],
        grid=(2,), name="first_norm", cost=(1e9, 2e6), vmem=60,
    )
    d_acts = [d_act_block((ups,), w_down)]

    def early_acts(below, above):
        for pair in list(zip(below, above))[: half_count - 2]:
            d_acts.append(d_act_block(pair, w_down))
        return [token for _, token in d_acts]

    ups_below, ups_above, ups_far = ring_gather(ups, early_acts)
    rows_blocks = tensor_blocks(normed_one)
    ups_groups = [(ups,)] + list(zip(ups_below, ups_above)) + [ups_far]
    d_acts += [d_act_block(group, w_down) for group in ups_groups[-2:]]
    (att, q, k, v, lse), _ = attend(
        place, rows_blocks, query_weight, key_weight, value_weight, cos, sin, segments,
        after=(ups_below[0], ups_above[0]),
    )
    other = branch_half(place, att, w_output, True, after=(ups_below[1], ups_above[1]))
    mine = branch_half(place, att, w_output, False)
    kept, got, _ = tensor_scatter(place, mine, other, after=())
    (residual, normed_two), _ = call(
        second_norm_body, (tokens, kept, got, gain_two), [row_spec] * 3 + [gain_spec], [row_spec] * 2,
        [pltpu.HBM((rows_dev, width), wide), pltpu.HBM((rows_dev, width), low)],
        after=(ups_below[-1], ups_above[-1]), grid=(2,), name="second_norm", cost=(1e9, 4e6),
    )
    rows_below, rows_above, rows_far = ring_gather(normed_two, lambda below, above: ())
    rows_groups = [(normed_two,)] + list(zip(rows_below, rows_above)) + [rows_far]
    done = []
    for index, (rows, up) in enumerate(zip(rows_groups, ups_groups)):
        after = () if not done else (done[-1][3],)
        if len(done) in (1, 2):
            after += (d_acts[len(done) - 3][1],)
        done.append(
            expert_block(
                rows, up, d_acts[index][0], sel, router, w_gate, w_up, w_down,
                True, after,
            )
        )
    rows_all = [piece for rows in rows_groups for piece in rows]
    ups_all = [piece for up in ups_groups for piece in up]
    hidden_all, d_gate_all, d_up_all = ([outs[2][i] for outs in done] for i in range(3))
    inner = local_experts * ff
    split_rows = {"down": ff // 2, "gate": width // 2, "up": width // 2}
    grads = {
        "down": outer_products(place, hidden_all, ups_all, inner, width, 1)[0],
        "gate": outer_products(place, rows_all, d_gate_all, width, inner, 2)[0],
        "up": outer_products(place, rows_all, d_up_all, width, inner, 2)[0],
    }
    mixed_parts = [outs[1] for outs in done]
    mixed_steps = ring_steps(
        [parts[0] for parts in mixed_parts[1:-1]], [parts[1] for parts in mixed_parts[1:-1]], mixed_parts[-1]
    )
    next(mixed_steps)
    first_mixed, _, _ = ring_step(mixed_steps)
    names = ("down", "gate", "up")
    halves, half_tokens, quarters, nears, gots = {}, {}, {}, {}, {}

    def quarter(name, after=()):
        got = gots.get(name)
        got = swap(halves[name][1], "tensor", 2) if got is None else got
        quarters[name], token = add_rows(halves[name][0], got, after)
        if name != "up":
            nears[name] = swap(quarters[name], "tensor", 1)
        return token

    def before(index):
        if index > 2:
            return (), ()
        after = (half_tokens[names[index - 1]],) if index else (first_mixed,)
        if index == 2:
            after += (quarter("down"),)
        return after, (grads[names[index]][1],)

    def then(index, _, held):
        if index > 2:
            return
        name = names[index]
        mine, other = (array.reshape(2, split_rows[name], -1) for array in (grads[name][0], held[0]))
        halves[name], half_tokens[name] = split_add(place, mine, swap(other, "tensor", 1))

    d_rows_up, d_rows_down = ring_scatter(
        [outs[0][0] for outs in done[1:-1]], [outs[0][1] for outs in done[1:-1]], done[-1][0], before, then
    )
    gots["gate"] = swap(halves["gate"][1], "tensor", 2)
    (d_residual, d_low, gain_ffn_part, router_part), _ = call(
        middle_body,
        (done[0][0][0], d_rows_up, d_rows_down, residual, normed_two, ups, router, gain_two),
        [wide_spec] * 3
        + [row_spec] * 2
        + [wide_spec, pl.BlockSpec((LANES, width), lambda i: (0, 0)), gain_spec],
        [row_spec] * 2 + [sum_spec, pl.BlockSpec((expert_count, width), lambda i: (0, 0))],
        [
            pltpu.HBM((rows_dev, width), wide),
            pltpu.HBM((rows_dev, width), low),
            Shape((1, width), wide),
            Shape((expert_count, width), wide),
        ],
        grid=(2,),
        after=(gots["gate"], ids),
        name="middle", vmem=62, cost=(4e-6 * 1.1e15, 4e6),
    )
    d_near, d_far = swap(d_low, "tensor", 1), swap(d_low, "tensor", 2)
    quarter("gate")
    pieces = {}

    def gather_pieces(name):
        second = swap(quarters[name], "tensor", 2)
        pieces[name] = (
            quarters[name],
            second,
            nears[name] if name in nears else swap(quarters[name], "tensor", 1),
            swap(second, "tensor", 1),
        )

    mark, (halves["up"][1],), _ = ring_step(mixed_steps, (), (halves["up"][1],))
    for _ in range(half_count - 4):
        mark, _, _ = ring_step(mixed_steps)
    (d_far,) = hold((d_far,), (mark,))
    d_blocks = (d_low, d_near, d_far, swap(d_far, "tensor", 1))
    d_lin, d_lin_token = attend_back(
        place, d_blocks, w_output, att, q, k, v, lse, cos, sin, segments,
        after=(mark, nears["down"], nears["gate"]),
    )
    mark, (quarters["down"],), (mixed_up, mixed_down) = ring_step(
        mixed_steps, (d_lin_token,), (quarters["down"],), 62
    )
    gather_pieces("down")
    parts, parts_token = head_grads(
        place, ids, rows_blocks, d_blocks, att, d_lin, query_weight, key_weight, value_weight, gain_one,
        gain_ffn_part, router_part, after=(mark,),
    )
    up_token = quarter("up", (parts_token,))
    (mine, other), lin_token = lin_back(
        place, d_lin, query_weight, key_weight, value_weight, after=(parts_token,)
    )
    sums, totals = {}, {}

    def before_total(index):
        if index == 0:
            return (mixed_up, mixed_down, pieces["down"][1], up_token), (other, quarters["gate"])
        if index == 1:
            return (totals["down"][1], sums["token"]), (quarters["up"],)
        if index == 2:
            return (pieces["gate"][1],), ()
        return (), ()

    def then_total(index, token, held):
        if index == 0:
            quarters["gate"] = held[1]
            gather_pieces("gate")
            totals["down"] = place_quarters(place, pieces["down"])
            sums["kept"], sums["got"], sums["token"] = tensor_scatter(place, mine, held[0], ())
        if index == 1:
            (quarters["up"],) = held
            gather_pieces("up")
        if index == 2:
            totals["gate"] = place_quarters(place, pieces["gate"])

    blocks = ring_total(parts, before_total, then_total, lambda: (totals["gate"][1],), lambda: (sums["got"],))
    totals["up"] = place_quarters(place, pieces["up"])
    kept, got = sums["kept"], sums["got"]
    mixed = (
        residual + mixed_parts[0][0].astype(wide) + mixed_up.astype(wide) + mixed_down.astype(wide)
    ).astype(low)
    grad_tokens, last_token = call(
        last_body, (tokens, kept, got, d_residual, gain_one), [row_spec] * 4 + [gain_spec], row_spec,
        Shape((rows_dev, width), low), grid=(2,), name="last", cost=(1e9, 4e6),
    )
    grad_q, grad_k, grad_v, grad_o, small = head_place(
        ids, blocks, [(width, q_width), (width, kv_width), (width, kv_width), (q_width, width)],
        (small_rows(data_count), width),
        (last_token,),
    )
    small = small + swap(small, "tensor", 1)
    small = small + swap(small, "tensor", 2)
    return (
        mixed,
        grad_tokens,
        small[1],
        grad_q,
        grad_k,
        grad_v,
        grad_o,
        small[0],
        small[2 : 2 + expert_count].T,
        totals["gate"][0],
        totals["up"][0],
        totals["down"][0],
    )


def solution(mesh):
    in_specs = (
        P(("dp", "tensor"), None),
        P(),
        P(None, "tensor"),
        P(None, "tensor"),
        P(None, "tensor"),
        P("tensor", None),
        P(),
        P(),
        P("dp", None, None),
        P("dp", None, None),
        P("dp", None, None),
        P("dp", None),
        P(("dp", "tensor"), None),
        P(("dp", "tensor"), None),
    )
    out_specs = (
        P(("dp", "tensor"), None),
        P(("dp", "tensor"), None),
        P(),
        P(None, "tensor"),
        P(None, "tensor"),
        P(None, "tensor"),
        P("tensor", None),
        P(),
        P(),
        P("dp", None, None),
        P("dp", None, None),
        P("dp", None, None),
    )
    return jax.shard_map(
        on_device, mesh=mesh, in_specs=in_specs, out_specs=out_specs, check_vma=False
    )
```
